32 devices in a mesh: seq: 8 (over z, x), wshard: 4 (over y, core).
Axes of the slice: x: 2, y: 2, z: 4, core: 2. Of those that a mesh axis runs over, the one named last changes fastest.
Arguments:
- inputs: bfloat16 [8, 4096, 512], P('wshard', 'seq'), may hold values from -6 to 6
- teacher: bfloat16 [8, 4096, 512], P('wshard', 'seq'), may hold values from -6 to 6
- segment_ids: int32 [8, 4096], P('wshard', 'seq'), may hold values from 0 to 31, never falling along the last dimension, each value on 1 to 1024 neighbouring positions
- valid_mask: int32 [8, 4096], P('wshard', 'seq'), may hold values from 0 to 1
- ln_gain: bfloat16 [512], P('wshard'), may hold values from 0.5 to 1.5
- ln_bias: bfloat16 [512], P('wshard'), may hold values from -3 to 3
- b_weight: bfloat16 [512, 768], P('wshard'), may hold values from -0.5 to 0.5
- c_weight: bfloat16 [768, 512], P('wshard'), may hold values from -0.21875 to 0.21875
- skip_weight: bfloat16 [512], P('wshard'), may hold values from -4 to 4
- glu_weight: bfloat16 [512, 512], P('wshard'), may hold values from -0.25 to 0.25
- glu_bias: bfloat16 [512], P('wshard'), may hold values from -3 to 3
- lambda_real: float32 [384], P('seq'), may hold values from -1 to 0, as said below
- lambda_imag: float32 [384], P('seq'), may hold values from -3.140625 to 3.140625
- log_step: float32 [384], P('seq'), may hold values from -4.159 to -2.773
Outputs:
- output: bfloat16 [8, 4096, 512], P('wshard', 'seq')
- distill_loss: float32 [], replicated
- input_grad: float32 [8, 4096, 512], P('wshard', 'seq')
- grad_ln_gain: float32 [512], P('wshard')
- grad_ln_bias: float32 [512], P('wshard')
- grad_b_weight: float32 [512, 768], P('wshard')
- grad_c_weight: float32 [768, 512], P('wshard')
- grad_skip_weight: float32 [512], P('wshard')
- grad_glu_weight: float32 [512, 512], P('wshard')
- grad_glu_bias: float32 [512], P('wshard')
- grad_lambda_real: float32 [384], P('seq')
- grad_lambda_imag: float32 [384], P('seq')
- grad_log_step: float32 [384], P('seq')
The draws below stay inside these ranges and needn't reach their ends.
Inputs may be any that keep to these rules, and one draw needn't show every extreme that they name: `segment_ids`: within each sequence the numbers never fall; a document holds 1 to 1024 tokens and some document holds exactly 1024. `lambda_real`: negative.
All inputs are finite; a program needn't handle non-finite values.
Results may differ from the reference program's by a relative error of at most 0.0074.
Values may be sent and summed in bfloat16 or wider, within the bound.
No kernel may reach another device: no remote copies, remote signals or barrier semaphores. Data moves between devices by JAX's collectives and lax.ppermute only.
A program may use at most 192 MiB of HBM per device.

```python
import math
import jax
import jax.numpy as jnp
import numpy as np
from jax import lax

H = 512
P_SIZE = 384
SEQUENCES = 8
LENGTH = 4096
DOCS = 32
DOC_MOST = 1024


def draw_valid_mask(key, part):
    places = jnp.arange(LENGTH, dtype=jnp.int32)
    limit = 300 + 650 * places // LENGTH
    rolled = jax.random.randint(key, (SEQUENCES, LENGTH), 0, 1000, dtype=jnp.int32)
    return (rolled < limit[None, :]).astype(jnp.int32)


def draw_lambda_real(key, part):
    lower = 0.1 / LENGTH
    upper = 0.8
    spread = jax.random.uniform(key, (P_SIZE,), jnp.float32)
    return -jnp.exp(jnp.log(lower) + spread * (jnp.log(upper) - jnp.log(lower)))


def shard_levels(rng, dims, shards, low, largest):
    factor_of, own = 1.0, jax.random.fold_in(rng, 6)
    for position, parts in shards:
        heights = jnp.exp(jax.random.uniform(jax.random.fold_in(own, position), (parts,), jnp.float32, low / len(shards), largest / len(shards)))
        factor_of = factor_of * jnp.repeat(heights, dims[position] // parts).reshape([-1 if axis == position else 1 for axis in range(len(dims))])
    return factor_of


def split_up(count, total, most, slope):
    weights = [(1 << 20) // math.isqrt(standing ** slope) + 1 for standing in range(2, count + 1)]
    rest, counts = total - most - (count - 1), [1] * (count - 1)
    while rest > 0:
        candidates = [i for i in range(count - 1) if counts[i] < most]
        pool, left = sum([weights[i] for i in candidates]), rest
        for i in candidates:
            more = min(most - counts[i], max(1, left * weights[i] // pool), rest)
            counts[i] = counts[i] + more
            rest = rest - more
    return np.array([most] + counts)


def ragged_sizes(key, number_of, total, bound, lean):
    if number_of == 2:
        one = jax.random.randint(key, (), max(1, total - bound), min(bound, total - 1) + 1)
        return jnp.stack([one, total - one])
    sizes = jnp.asarray(split_up(number_of, total, bound, lean), jnp.int32)
    pairs = (number_of - 1) // 2
    giver, taker = sizes[1:1 + 2 * pairs:2], sizes[2:2 + 2 * pairs:2]
    slack = jnp.minimum(giver - 1, bound - taker)
    shifted = jax.random.randint(jax.random.fold_in(key, 1), (pairs,), 0, 1 << 20) % (slack + 1)
    sizes = sizes.at[1:1 + 2 * pairs:2].set(giver - shifted).at[2:2 + 2 * pairs:2].set(taker + shifted)
    return sizes[jax.random.permutation(jax.random.fold_in(key, 2), number_of)]


def noise(own_key, extent, scale, most, pieces=(), kind=jnp.bfloat16):
    level = shard_levels(own_key, extent, pieces, -0.22, 0.18) if pieces else 1.0
    array = jax.random.normal(own_key, extent, jnp.float32) * scale * level
    return jnp.minimum(jnp.maximum(array, -most), most).astype(kind)


def setup_inputs(seed: int = 0) -> dict:
    keys = jax.random.split(jax.random.key(seed), 15)
    inputs = noise(keys[0], (SEQUENCES, LENGTH, H), 1.0, 6.0, ((0, 4), (1, 8)))
    teacher = noise(keys[1], (SEQUENCES, LENGTH, H), 1.0, 6.0, ((0, 4), (1, 8)))
    segment_ids = jax.vmap(lambda own: jnp.searchsorted(jnp.cumsum(ragged_sizes(own, DOCS, LENGTH, DOC_MOST, 2)), jnp.arange(LENGTH), side="right"))(jax.random.split(keys[2], SEQUENCES)).reshape((SEQUENCES, LENGTH)).astype(jnp.int32)
    valid_mask = draw_valid_mask(jax.random.fold_in(keys[14], 71), 0)
    ln_gain = jnp.clip(1.0 + 0.1 * jax.random.normal(keys[4], (H,), jnp.float32), 0.5, 1.5).astype(jnp.bfloat16)
    ln_bias = noise(keys[5], (H,), 0.5, 3.0, ((0, 4),))
    b_weight = noise(keys[6], (H, 2 * P_SIZE), (H // 4) ** -0.5, 0.5, ((0, 4),))
    c_weight = noise(keys[7], (2 * P_SIZE, H), (2 * P_SIZE) ** -0.5, 0.21875, ((0, 4),))
    skip_weight = noise(keys[8], (H,), 1.0, 4.0, ((0, 4),))
    glu_weight = noise(keys[9], (H, H), H ** -0.5, 0.25, ((0, 4),))
    glu_bias = noise(keys[10], (H,), 0.5, 3.0, ((0, 4),))
    lambda_real = draw_lambda_real(jax.random.fold_in(keys[14], 71), 0)
    lambda_imag = jnp.clip(jax.random.uniform(keys[12], (P_SIZE,), jnp.float32, -3.140625, 3.140625), -3.140625, 3.140625)
    log_step = jnp.clip(-4.159 + 1.3859999 * jax.random.uniform(keys[13], (P_SIZE,), jnp.float32) ** shard_levels(keys[13], (P_SIZE,), ((0, 8),), -0.2, 0.2), -4.159, -2.773)
    return dict(inputs=inputs, teacher=teacher, segment_ids=segment_ids, valid_mask=valid_mask, ln_gain=ln_gain, ln_bias=ln_bias, b_weight=b_weight, c_weight=c_weight, skip_weight=skip_weight, glu_weight=glu_weight, glu_bias=glu_bias, lambda_real=lambda_real, lambda_imag=lambda_imag, log_step=log_step)


@jax.custom_vjp
def low(v):
    return lax.optimization_barrier(v.astype(jnp.bfloat16)).astype(jnp.float32)

@jax.custom_vjp
def low_back(v):
    return v

def low_keep(v):
    return (low(v), None)

def low_pass(kept, grad):
    return (grad,)

def back_keep(v):
    return (v, None)

def back_low(kept, grad):
    return (low(grad),)
low.defvjp(low_keep, low_pass)
low_back.defvjp(back_keep, back_low)

def layer_norm(values, scales, shifts):
    average = lax.optimization_barrier(jnp.mean(values, -1, keepdims=True))
    centered = values - average
    variance = lax.optimization_barrier(jnp.mean(centered * centered, -1, keepdims=True))
    return centered * lax.rsqrt(variance + 1e-05) * scales + shifts

def rates_map(real_rate, imag_rate, log_rate):
    time_step = jnp.exp(log_rate)
    grow_re = real_rate * time_step
    turn_im = imag_rate * time_step
    growth = jnp.exp(grow_re)
    abar_re = growth * jnp.cos(turn_im)
    abar_im = growth * jnp.sin(turn_im)
    half_sine = jnp.sin(0.5 * turn_im)
    numer_re = jnp.expm1(grow_re) * jnp.cos(turn_im) - 2.0 * half_sine * half_sine
    numer_im = abar_im
    divisor = real_rate * real_rate + imag_rate * imag_rate
    scale_re = (numer_re * real_rate + numer_im * imag_rate) / divisor
    scale_im = (numer_im * real_rate - numer_re * imag_rate) / divisor
    return (abar_re, abar_im, scale_re, scale_im)

def combine(earlier, later):
    mult_re = later[0] * earlier[0] - later[1] * earlier[1]
    mult_im = later[0] * earlier[1] + later[1] * earlier[0]
    add_re = later[0] * earlier[2] - later[1] * earlier[3] + later[2]
    add_im = later[0] * earlier[3] + later[1] * earlier[2] + later[3]
    return (mult_re, mult_im, add_re, add_im)

def reference(inputs, teacher, segment_ids, valid_mask, ln_gain, ln_bias, b_weight, c_weight, skip_weight, glu_weight, glu_bias, lambda_real, lambda_imag, log_step):
    highest = lax.Precision.HIGHEST
    states = lambda_real.shape[0]
    model_width = inputs.shape[2]
    token_total = inputs.shape[0] * inputs.shape[1]
    linked = jnp.concatenate([jnp.zeros((segment_ids.shape[0], 1), jnp.float32), (segment_ids[:, 1:] == segment_ids[:, :-1]).astype(jnp.float32)], 1)
    mask_f = valid_mask.astype(jnp.float32)
    valid_count = jnp.sum(mask_f)
    target = teacher.astype(jnp.float32)

    def forward(source, norm_gain, norm_bias, w_in, w_out, skip_vec, w_glu, gate_bias, real_rate, imag_rate, log_rate):
        normed = layer_norm(source, norm_gain, norm_bias)
        low_in = low(normed)
        projected = jnp.einsum('sth,hc->stc', low_in, w_in, precision=highest)
        projected = low_back(low(projected))
        abar_re, abar_im, scale_re, scale_im = rates_map(real_rate, imag_rate, log_rate)
        proj_re = projected[..., :states]
        proj_im = projected[..., states:]
        inject_re = scale_re * proj_re - scale_im * proj_im
        inject_im = scale_re * proj_im + scale_im * proj_re
        step_re = linked[..., None] * abar_re
        step_im = linked[..., None] * abar_im
        scanned = lax.associative_scan(combine, (step_re, step_im, inject_re, inject_im), axis=1)
        state = low_back(low(jnp.concatenate([scanned[2], scanned[3]], -1)))
        mixed_out = low_back(jnp.einsum('stc,ch->sth', state, w_out, precision=highest))
        ssm_out = mixed_out + skip_vec * low_in
        activation = low(jax.nn.gelu(ssm_out, approximate=False))
        gate_lin = low_back(jnp.einsum('sti,ij->stj', activation, w_glu, precision=highest))
        gate_pre = gate_lin + gate_bias
        result = source + activation * jax.nn.sigmoid(gate_pre)
        errors = result - target
        loss_value = jnp.sum(mask_f * lax.optimization_barrier(jnp.sum(errors * errors, -1))) / (valid_count * model_width)
        return (0.5 * token_total * model_width * loss_value, (result, loss_value))
    primals = (inputs.astype(jnp.float32), ln_gain.astype(jnp.float32), ln_bias.astype(jnp.float32), b_weight.astype(jnp.float32), c_weight.astype(jnp.float32), skip_weight.astype(jnp.float32), glu_weight.astype(jnp.float32), glu_bias.astype(jnp.float32), lambda_real, lambda_imag, log_step)
    objective, pullback, aux_out = jax.vjp(forward, *primals, has_aux=True)
    result, loss_value = aux_out
    grads = pullback(jnp.ones_like(objective))
    return (result.astype(jnp.bfloat16), loss_value, grads[0], grads[1], grads[2], grads[3], grads[4], grads[5], grads[6], grads[7], grads[8], grads[9], grads[10])
```

```python
import functools

import jax
import jax.numpy as jnp
from jax import lax
from jax.experimental import pallas as pl
from jax.experimental.pallas import tpu as pltpu
from jax.sharding import PartitionSpec as P

CHUNKS = 8
LANES = 128
TILE = 256
MIB = 1024 * 1024
F32 = jnp.float32
BF16 = jnp.bfloat16


def rates_map(real_rate, imag_rate, log_rate):
    time_step = jnp.exp(log_rate)
    grow_re = real_rate * time_step
    turn_im = imag_rate * time_step
    growth = jnp.exp(grow_re)
    abar_re = growth * jnp.cos(turn_im)
    abar_im = growth * jnp.sin(turn_im)
    half_sine = jnp.sin(0.5 * turn_im)
    numer_re = jnp.expm1(grow_re) * jnp.cos(turn_im) - 2.0 * half_sine * half_sine
    divisor = real_rate * real_rate + imag_rate * imag_rate
    scale_re = (numer_re * real_rate + abar_im * imag_rate) / divisor
    scale_im = (abar_im * real_rate - numer_re * imag_rate) / divisor
    return (abar_re, abar_im, scale_re, scale_im)


def cmul(xr, xi, yr, yi):
    return xr * yr - xi * yi, xr * yi + xi * yr


def power2(xr, xi, times):
    for _ in range(times):
        xr, xi = xr * xr - xi * xi, 2.0 * xr * xi
    return xr, xi


def log2(n):
    return n.bit_length() - 1


def wide(v, groups):
    return jnp.concatenate([v] * groups, axis=1)


def fold_rows(v):
    return jnp.sum(v.reshape(-1, 8, v.shape[-1]), axis=0)


def take(ref, at, first, count):
    return jnp.concatenate([ref[first + g, at, :] for g in range(count)], axis=1)


def put(ref, at, first, v):
    for g in range(v.shape[1] // LANES):
        ref[first + g, at, :] = v[:, g * LANES : (g + 1) * LANES]


def one_row(v):
    return jnp.sum(v, axis=0, keepdims=True)


def nt_dot(a, b):
    return lax.dot_general(a, b, (((1,), (1,)), ((), ())), preferred_element_type=F32)


def tn_dot(a, b):
    return lax.dot_general(a, b, (((0,), (0,)), ((), ())), preferred_element_type=F32)


def chunk_scan(ar, ai, br, bi, reverse):
    rows = lax.broadcasted_iota(jnp.int32, ar.shape, 0)
    d = 1
    while d < CHUNKS:
        shift = (CHUNKS - d) if reverse else d
        keep = (rows < CHUNKS - d) if reverse else (rows >= d)
        pr, pi = pltpu.roll(ar, shift, 0), pltpu.roll(ai, shift, 0)
        qr, qi = pltpu.roll(br, shift, 0), pltpu.roll(bi, shift, 0)
        mr, mi = cmul(ar, ai, qr, qi)
        br, bi = jnp.where(keep, br + mr, br), jnp.where(keep, bi + mi, bi)
        mr, mi = cmul(ar, ai, pr, pi)
        ar, ai = jnp.where(keep, mr, ar), jnp.where(keep, mi, ai)
        d *= 2
    return ar, ai, br, bi


def carry_in(recvs, ids, s, own_row, ar, ai, block_len, conj):
    states = ar.shape[1]
    pr, pi = power2(ar, -ai if conj else ai, log2(block_len))
    cr = jnp.zeros((1, states), F32)
    ci = jnp.zeros((1, states), F32)
    own = wide(ids[own_row : own_row + 1, :], states // LANES)
    for ref in reversed(recvs):
        msg = ref[s : s + 1, :]
        same = wide(msg[:, 2 * states :], states // LANES) == own
        cr, ci = cmul(pr, pi, cr, ci)
        cr = cr + jnp.where(same, msg[:, :states], 0.0)
        ci = ci + jnp.where(same, msg[:, states : 2 * states], 0.0)
    return cr, ci


def k1_body(w_ref, x_ref, b0, b1, b2, b3, rates_ref, marks_ref, ids_ref,
            low_ref, proj_ref, s1_ref, msg_ref, vec_ref, w_scr, *, seqs):
    rows, width = x_ref.shape
    states = rates_ref.shape[1]
    shard = b0.shape[0] - 16
    groups = states // LANES
    steps = rows // seqs // CHUNKS
    block_len = rows // seqs
    w = w_ref[0]
    for k, piece in enumerate((b0, b1, b2, b3)):
        at = pl.multiple_of((w ^ k) * shard, shard)
        w_scr[pl.ds(at, shard), :] = piece[:shard, :]
        extra = piece[shard:, :].astype(F32)
        for v in range(4):
            vec_ref[v : v + 1, pl.ds(at, shard)] = extra[0:1, v * shard : (v + 1) * shard]
    vec_ref[4:8, :] = jnp.zeros((4, width), F32)
    gain = vec_ref[0:1, :]
    bias = vec_ref[1:2, :]
    for i in range(rows // TILE):
        at = slice(i * TILE, (i + 1) * TILE)
        x = x_ref[at, :].astype(F32)
        c = x - jnp.mean(x, -1, keepdims=True)
        r = lax.rsqrt(jnp.mean(c * c, -1, keepdims=True) + 1e-05)
        low = (c * r * gain + bias).astype(BF16)
        low_ref[at, :] = low
        p = jnp.dot(low, w_scr[...], preferred_element_type=F32)
        put(proj_ref, at, 0, p.astype(BF16).astype(F32))
    a1r, a1i = rates_ref[0:1, :], rates_ref[1:2, :]
    ar = jnp.broadcast_to(a1r, (CHUNKS, states))
    ai = jnp.broadcast_to(a1i, (CHUNKS, states))

    def step(j, carry):
        out = []
        for s in range(seqs):
            ur, ui, q = carry[s]
            at = pl.ds(s * block_len + j, CHUNKS, stride=steps)
            lk = marks_ref[0, at, :]
            lw = wide(lk, groups)
            nr, ni = cmul(ar, ai, ur, ui)
            out.append((lw * nr + take(proj_ref, at, 0, groups), lw * ni + take(proj_ref, at, groups, groups), q * lk))
        return tuple(out)

    zero = jnp.zeros((CHUNKS, states), F32)
    init = tuple((zero, zero, jnp.ones((CHUNKS, LANES), F32)) for _ in range(seqs))
    ends = lax.fori_loop(0, steps, step, init, unroll=8)
    pr, pi = power2(ar, ai, log2(steps))
    for s in range(seqs):
        ur, ui, q = ends[s]
        qw = wide(q, groups)
        sc = chunk_scan(pr * qw, pi * qw, ur, ui, False)
        for v in range(4):
            s1_ref[s * CHUNKS : (s + 1) * CHUNKS, v * states : (v + 1) * states] = sc[v]
        msg_ref[s : s + 1, :states] = sc[2][CHUNKS - 1 :, :]
        msg_ref[s : s + 1, states : 2 * states] = sc[3][CHUNKS - 1 :, :]
        msg_ref[s : s + 1, 2 * states :] = ids_ref[seqs + s : seqs + s + 1, :]


def k2_body(*refs, seqs, hops):
    (w_ref, scale_ref, x_ref, t_ref, marks_ref, ids_ref, low_ref, proj_ref, s1_ref, rates_ref, vec_ref,
     c0, c1, c2, c3) = refs[:15]
    recvs = refs[15 : 15 + hops]
    (out_ref, state_ref, first_ref, gs_ref, gres_ref, gssm_ref, s2_ref, msg_ref, send_ref, keep_ref, sums_ref,
     wc_scr, wg_scr, act_scr, gate_scr, ssl_scr, sl_scr, gc_scr, gg_scr) = refs[15 + hops :]
    rows, width = x_ref.shape
    states = rates_ref.shape[1]
    groups = states // LANES
    block_len = rows // seqs
    steps = block_len // CHUNKS
    g_shard = width // 4
    c_shard = 2 * states // 4
    w = w_ref[0]
    for k, piece in enumerate((c0, c1, c2, c3)):
        wc_scr[pl.ds(pl.multiple_of((w ^ k) * c_shard, c_shard), c_shard), :] = piece[:c_shard, :]
        wg_scr[pl.ds(pl.multiple_of((w ^ k) * g_shard, g_shard), g_shard), :] = piece[c_shard:, :]
    a1r, a1i = rates_ref[0:1, :], rates_ref[1:2, :]
    ar = jnp.broadcast_to(a1r, (CHUNKS, states))
    ai = jnp.broadcast_to(a1i, (CHUNKS, states))
    zr = jnp.broadcast_to(rates_ref[2:3, :], (CHUNKS, states))
    zi = jnp.broadcast_to(rates_ref[3:4, :], (CHUNKS, states))
    top = lax.broadcasted_iota(jnp.int32, (CHUNKS, states), 0)
    ids = ids_ref[...]
    init = []
    for s in range(seqs):
        cr, ci = carry_in(recvs, ids, s, s, a1r, a1i, block_len, False)
        sc = [s1_ref[s * CHUNKS : (s + 1) * CHUNKS, v * states : (v + 1) * states] for v in range(4)]
        mr, mi = cmul(sc[0], sc[1], cr, ci)
        br = jnp.where(top == 0, cr, pltpu.roll(sc[2] + mr, 1, 0))
        bi = jnp.where(top == 0, ci, pltpu.roll(sc[3] + mi, 1, 0))
        init.append((br, bi))
        fr, fi = cmul(zr, zi, br, bi)
        first_ref[s * CHUNKS : (s + 1) * CHUNKS, :states] = fr
        first_ref[s * CHUNKS : (s + 1) * CHUNKS, states:] = fi

    def step(j, carry):
        out = []
        for s in range(seqs):
            ur, ui = carry[s]
            at = pl.ds(s * block_len + j, CHUNKS, stride=steps)
            lw = wide(marks_ref[0, at, :], groups)
            nr, ni = cmul(ar, ai, ur, ui)
            ur, ui = lw * nr + take(proj_ref, at, 0, groups), lw * ni + take(proj_ref, at, groups, groups)
            sr, si = cmul(zr, zi, ur, ui)
            put(state_ref, at, 0, sr)
            put(state_ref, at, groups, si)
            out.append((ur, ui))
        return tuple(out)

    lax.fori_loop(0, steps, step, tuple(init), unroll=8)

    grad_scale = scale_ref[0, 0]
    skip = vec_ref[2:3, :]
    gbias = vec_ref[3:4, :]
    loss_acc = jnp.zeros((8, width), F32)
    gbias_acc = jnp.zeros((8, width), F32)
    skip_acc = jnp.zeros((8, width), F32)
    for i in range(rows // TILE):
        at = slice(i * TILE, (i + 1) * TILE)
        sl = take(state_ref, at, 0, 2 * groups).astype(BF16)
        sl_scr[at, :] = sl
        low_f = low_ref[at, :].astype(F32)
        so = jnp.dot(sl, wc_scr[...], preferred_element_type=F32) + skip * low_f
        z = jnp.abs(so) * 0.7071067811865476
        e = jnp.exp(-z * z)
        t = 1.0 / (1.0 + 0.3275911 * z)
        poly = t * (0.254829592 + t * (-0.284496736 + t * (1.421413741 + t * (-1.453152027 + t * 1.061405429))))
        tail = 0.5 * poly * e
        phi = jnp.where(so >= 0.0, 1.0 - tail, tail)
        act = (so * phi).astype(BF16)
        act_scr[at, :] = act
        dgelu = phi + so * e * 0.3989422804014327
        act_f = act.astype(F32)
        g = 0.5 * jnp.tanh(0.5 * (jnp.dot(act, wg_scr[...], preferred_element_type=F32) + gbias)) + 0.5
        res = x_ref[at, :].astype(F32) + act_f * g
        out_ref[at, :] = res.astype(BF16)
        err = res - t_ref[at, :].astype(F32)
        em = err * wide(marks_ref[1, at, :], width // LANES)
        loss_acc = loss_acc + fold_rows(em * err)
        gr = grad_scale * em
        gres_ref[at, :] = gr
        gg = gr * act_f * g * (1.0 - g)
        gbias_acc = gbias_acc + fold_rows(gg)
        gl = gg.astype(BF16)
        gate_scr[at, :] = gl
        gssm = dgelu * (gr * g + nt_dot(gl, wg_scr[...]))
        gssm_ref[at, :] = gssm
        skip_acc = skip_acc + fold_rows(gssm * low_f)
        ssl = gssm.astype(BF16)
        ssl_scr[at, :] = ssl
        put(gs_ref, at, 0, nt_dot(ssl, wc_scr[...]).astype(BF16).astype(F32))
    sums_ref[0:1, :] = one_row(gbias_acc)
    sums_ref[1:2, :] = one_row(skip_acc)
    sums_ref[2:3, :] = one_row(loss_acc)
    sums_ref[3:8, :] = jnp.zeros((5, width), F32)

    def back(i, carry):
        j = steps - 1 - i
        out = []
        for s in range(seqs):
            yr, yi, q = carry[s]
            at = pl.ds(s * block_len + j, CHUNKS, stride=steps)
            lk = marks_ref[0, at, :]
            lw = wide(lk, groups)
            nr, ni = cmul(ar, -ai, yr, yi)
            out.append((lw * (nr + take(gs_ref, at, 0, groups)), lw * (ni + take(gs_ref, at, groups, groups)), q * lk))
        return tuple(out)

    zero = jnp.zeros((CHUNKS, states), F32)
    init = tuple((zero, zero, jnp.ones((CHUNKS, LANES), F32)) for _ in range(seqs))
    ends = lax.fori_loop(0, steps, back, init, unroll=8)
    pr, pi = power2(ar, -ai, log2(steps))
    for s in range(seqs):
        yr, yi, q = ends[s]
        qw = wide(q, groups)
        sc = chunk_scan(pr * qw, pi * qw, yr, yi, True)
        for v in range(4):
            s2_ref[s * CHUNKS : (s + 1) * CHUNKS, v * states : (v + 1) * states] = sc[v]
        msg_ref[s : s + 1, :states] = sc[2][:1, :]
        msg_ref[s : s + 1, states : 2 * states] = sc[3][:1, :]
        msg_ref[s : s + 1, 2 * states :] = ids_ref[s : s + 1, :]

    gg_scr[...] = tn_dot(act_scr[...], gate_scr[...])
    gc_scr[...] = tn_dot(sl_scr[...], ssl_scr[...])
    for k, (dst, slot) in enumerate(((keep_ref, 0), (send_ref, 0), (keep_ref, 1), (send_ref, 1))):
        q = w ^ k
        dst[slot, :c_shard, :] = gc_scr[pl.ds(pl.multiple_of(q * c_shard, c_shard), c_shard), :].astype(BF16)
        dst[slot, c_shard:, :] = gg_scr[pl.ds(pl.multiple_of(q * g_shard, g_shard), g_shard), :].astype(BF16)


def split16(v):
    high = v.astype(BF16)
    return high, (v - high.astype(F32)).astype(BF16)


def k3_body(*refs, seqs, hops):
    (w_ref, x_ref, marks_ref, ids_ref, low_ref, proj_ref, state_ref, first_ref, gs_ref, gres_ref, gssm_ref,
     s2_ref, sums_ref, rates_ref, vec_ref, b0, b1, b2, b3) = refs[:19]
    recvs = refs[19 : 19 + hops]
    (ingrad_ref, send_ref, keep_ref, gp_scr, gpl_scr, w_scr, gb_scr, vec_scr) = refs[19 + hops :]
    rows, width = x_ref.shape
    states = rates_ref.shape[1]
    groups = states // LANES
    block_len = rows // seqs
    steps = block_len // CHUNKS
    shard = b0.shape[0] - 16
    w = w_ref[0]
    for k, piece in enumerate((b0, b1, b2, b3)):
        w_scr[pl.ds(pl.multiple_of((w ^ k) * shard, shard), shard), :] = piece[:shard, :]
    a1r, a1i = rates_ref[0:1, :], rates_ref[1:2, :]
    ar = jnp.broadcast_to(a1r, (CHUNKS, states))
    ai = jnp.broadcast_to(a1i, (CHUNKS, states))
    zr = jnp.broadcast_to(rates_ref[2:3, :], (CHUNKS, states))
    zi = jnp.broadcast_to(rates_ref[3:4, :], (CHUNKS, states))
    rowid = lax.broadcasted_iota(jnp.int32, (CHUNKS, states), 0)
    ids = ids_ref[...]
    rate_sums = [jnp.zeros((CHUNKS, states), F32) for _ in range(4)]
    for s in range(seqs):
        cr, ci = carry_in(recvs, ids, s, seqs + s, a1r, a1i, block_len, True)
        sc = [s2_ref[s * CHUNKS : (s + 1) * CHUNKS, v * states : (v + 1) * states] for v in range(4)]
        mr, mi = cmul(sc[0], sc[1], cr, ci)
        yr = jnp.where(rowid == CHUNKS - 1, cr, pltpu.roll(sc[2] + mr, CHUNKS - 1, 0))
        yi = jnp.where(rowid == CHUNKS - 1, ci, pltpu.roll(sc[3] + mi, CHUNKS - 1, 0))

        def one(j, at, prev_r, prev_i, carry):
            yr, yi, gar, gai, gsr, gsi = carry
            lw = wide(marks_ref[0, at, :], groups)
            nr, ni = cmul(ar, -ai, yr, yi)
            dr, di = nr + take(gs_ref, at, 0, groups), ni + take(gs_ref, at, groups, groups)
            yr, yi = lw * dr, lw * di
            pr, pi = take(proj_ref, at, 0, groups), take(proj_ref, at, groups, groups)
            put(gp_scr, at, 0, zr * dr + zi * di)
            put(gp_scr, at, groups, zr * di - zi * dr)
            return (
                yr, yi,
                gar + (prev_r * yr + prev_i * yi), gai + (prev_r * yi - prev_i * yr),
                gsr + (pr * dr + pi * di), gsi + (pr * di - pi * dr),
            )

        def step(i, carry):
            j = steps - 1 - i
            at = pl.ds(s * block_len + j, CHUNKS, stride=steps)
            before = pl.ds(s * block_len + j - 1, CHUNKS, stride=steps)
            return one(j, at, take(state_ref, before, 0, groups), take(state_ref, before, groups, groups), carry)

        carry = lax.fori_loop(0, steps - 1, step, (yr, yi, *rate_sums), unroll=7)
        mine = slice(s * CHUNKS, (s + 1) * CHUNKS)
        at = pl.ds(s * block_len, CHUNKS, stride=steps)
        carry = one(0, at, first_ref[mine, :states], first_ref[mine, states:], carry)
        rate_sums = list(carry[2:])

    skip = vec_ref[2:3, :]
    gain = vec_ref[0:1, :]
    gain_acc = jnp.zeros((8, width), F32)
    bias_acc = jnp.zeros((8, width), F32)
    for i in range(rows // TILE):
        at = slice(i * TILE, (i + 1) * TILE)
        gpl = take(gp_scr, at, 0, 2 * groups).astype(BF16)
        gpl_scr[at, :] = gpl
        gn = nt_dot(gpl, w_scr[...]) + skip * gssm_ref[at, :]
        x = x_ref[at, :].astype(F32)
        c = x - jnp.mean(x, -1, keepdims=True)
        r = lax.rsqrt(jnp.mean(c * c, -1, keepdims=True) + 1e-05)
        n = c * r
        q = gn * gain
        gain_acc = gain_acc + fold_rows(gn * n)
        bias_acc = bias_acc + fold_rows(gn)
        ingrad_ref[at, :] = gres_ref[at, :] + (
            q - jnp.mean(q, -1, keepdims=True) - n * jnp.mean(q * n, -1, keepdims=True)
        ) * r
    gb_scr[...] = tn_dot(low_ref[...], gpl_scr[...])
    sums4 = [one_row(v) for v in rate_sums]
    rate_grads = []
    for k in range(3):
        rate_grads.append(sum(rates_ref[8 + 3 * c + k : 9 + 3 * c + k, :] * sums4[c] for c in range(4)))
    vec_scr[0:1, :] = one_row(gain_acc)
    vec_scr[1:2, :] = one_row(bias_acc)
    vec_scr[2:3, :] = sums_ref[1:2, :]
    vec_scr[3:4, :] = sums_ref[0:1, :]
    loss = jnp.sum(sums_ref[2:3, :], axis=1, keepdims=True)
    extra = 3 * shard // 2
    half = shard // 2
    for k, (dst, slot) in enumerate(((keep_ref, 0), (send_ref, 0), (keep_ref, 1), (send_ref, 1))):
        q = pl.multiple_of((w ^ k) * shard, shard)
        dst[slot, :shard, :] = gb_scr[pl.ds(q, shard), :width].astype(BF16)
        dst[slot, shard:extra, : width // 2] = gb_scr[pl.ds(q, half), width:].astype(BF16)
        dst[slot, shard:extra, width // 2 :] = gb_scr[pl.ds(q + half, half), width:].astype(BF16)
        vec = jnp.concatenate([vec_scr[v : v + 1, pl.ds(q, shard)] for v in range(4)], axis=1)
        lines = [vec] + [jnp.concatenate([g, jnp.zeros((1, width - states), F32)], axis=1) for g in rate_grads]
        lines += [jnp.broadcast_to(loss, (1, width)), jnp.zeros((3, width), F32)]
        high, rest = split16(jnp.concatenate(lines, axis=0))
        dst[slot, extra:, :] = jnp.concatenate([high.astype(F32), rest.astype(F32)], axis=0).astype(BF16)


def whole(n, smem=()):
    return [pl.BlockSpec(memory_space=pltpu.SMEM if i in smem else pltpu.VMEM) for i in range(n)]


def call(body, outs, scratch, smem, *args, flops=1_000_000_000, limit=60):
    return pl.pallas_call(
        body,
        out_shape=[jax.ShapeDtypeStruct(*o) for o in outs],
        in_specs=whole(len(args), smem),
        out_specs=whole(len(outs)),
        scratch_shapes=[pltpu.VMEM(*s) for s in scratch],
        compiler_params=pltpu.CompilerParams(vmem_limit_bytes=limit * MIB),
        cost_estimate=pl.CostEstimate(flops=flops, bytes_accessed=8 * MIB, transcendentals=0),
    )(*args)


def per_device(inputs, teacher, segment_ids, valid_mask, ln_gain, ln_bias, b_weight, c_weight, skip_weight,
               glu_weight, glu_bias, lambda_real, lambda_imag, log_step):
    S, W = lax.axis_size("seq"), lax.axis_size("wshard")
    s_at, w_at = lax.axis_index("seq"), lax.axis_index("wshard")
    seqs, block_len, width = inputs.shape
    rows = seqs * block_len
    length = S * block_len
    own = lambda_real.shape[0]
    states = own * S
    doc_most = {4096: 1024, 32768: 8192}.get(length, length)
    hops = min((doc_most - 2) // block_len + 1, S - 1)

    def swap(v, axis, n, bit):
        return lax.ppermute(v, axis, [(i, i ^ bit) for i in range(n)])

    def gather4(v):
        far = swap(v, "wshard", W, 2)
        near = swap(v, "wshard", W, 1)
        both = swap(far, "wshard", W, 1)
        return (v, near, far, both)

    shard = b_weight.shape[0]
    line = jnp.concatenate([ln_gain, ln_bias, skip_weight, glu_bias, jnp.zeros((b_weight.shape[1] - 4 * shard,), BF16)])
    b_msg = jnp.concatenate([b_weight, jnp.pad(line[None], ((0, 15), (0, 0)))], 0)
    bs = gather4(b_msg)

    rate_parts, rate_back = jax.vjp(rates_map, lambda_real, lambda_imag, log_step)
    one, zero = jnp.ones_like(lambda_real), jnp.zeros_like(lambda_real)
    jac = []
    for c in range(4):
        jac += list(rate_back(tuple(one if i == c else zero for i in range(4))))
    count = jnp.sum(valid_mask).astype(F32)
    count_line = jnp.where(lax.iota(jnp.int32, own) == 0, count, 0.0)
    mine = jnp.stack(list(rate_parts) + [count_line] + [zero] * 3 + jac + [zero] * 4)
    table = lax.dynamic_update_slice(jnp.zeros((mine.shape[0], states), F32), mine, (0, s_at * own))
    bit = 1
    while bit < S:
        table = table + swap(table, "seq", S, bit)
        bit *= 2
    total = jnp.sum(table[4]).reshape(1, 1)
    for bit in (1, 2):
        total = total + swap(total, "wshard", W, bit)
    grad_scale = (length * seqs * W) / total

    cs = gather4(jnp.concatenate([c_weight, glu_weight], 0))

    same = (segment_ids[:, 1:] == segment_ids[:, :-1]).astype(F32)
    link = jnp.concatenate([jnp.ones((seqs, 1), F32), same], 1).reshape(rows, 1)
    mask = valid_mask.astype(F32).reshape(rows, 1)
    marks = jnp.broadcast_to(jnp.stack([link, mask]), (2, rows, LANES))
    ends = jnp.concatenate([segment_ids[:, 0], segment_ids[:, -1]]).astype(F32)
    ids = jnp.broadcast_to(ends[:, None], (2 * seqs, LANES))

    wid = w_at.astype(jnp.int32).reshape(1)
    x = inputs.reshape(rows, width)
    teach = teacher.reshape(rows, width)
    R = seqs * CHUNKS
    slab = (2 * states // LANES, rows, LANES)
    msg_shape = ((seqs, 2 * states + LANES), F32)
    low, proj, s1, fwd, vec = call(
        functools.partial(k1_body, seqs=seqs),
        [((rows, width), BF16), (slab, F32), ((R, 4 * states), F32), msg_shape, ((8, width), F32)],
        [((width, 2 * states), BF16)],
        (0,),
        wid, x, *bs, table, marks, ids,
    )
    fwds = [lax.ppermute(fwd, "seq", [(i, i + k) for i in range(S - k)]) for k in range(1, hops + 1)]
    shard2 = c_weight.shape[0] + glu_weight.shape[0]
    out, state, first, gs, gres, gssm, s2, bwd, send_c, keep_c, sums = call(
        functools.partial(k2_body, seqs=seqs, hops=hops),
        [((rows, width), BF16), (slab, F32), ((R, 2 * states), F32), (slab, F32),
         ((rows, width), F32), ((rows, width), F32), ((R, 4 * states), F32), msg_shape,
         ((2, shard2, width), BF16), ((2, shard2, width), BF16), ((8, width), F32)],
        [((2 * states, width), BF16), ((width, width), BF16), ((rows, width), BF16), ((rows, width), BF16),
         ((rows, width), BF16), ((rows, 2 * states), BF16), ((2 * states, width), F32), ((width, width), F32)],
        (0, 1),
        wid, grad_scale, x, teach, marks, ids, low, proj, s1, table, vec, *cs, *fwds,
    )
    bwds = [lax.ppermute(bwd, "seq", [(i + k, i) for i in range(S - k)]) for k in range(1, hops + 1)]
    extra = 3 * shard // 2
    ingrad, send_b, keep_b = call(
        functools.partial(k3_body, seqs=seqs, hops=hops),
        [((rows, width), F32), ((2, extra + 16, width), BF16), ((2, extra + 16, width), BF16)],
        [(slab, F32), ((rows, 2 * states), BF16), ((width, 2 * states), BF16),
         ((width, 2 * states), F32), ((8, width), F32)],
        (0,),
        wid, x, marks, ids, low, proj, state, first, gs, gres, gssm, s2, sums, table, vec, *bs, *bwds,
    )

    def add16(a, b):
        return (a.astype(F32) + b.astype(F32)).astype(BF16)

    def add_split(a, b):
        v = a[..., :8, :].astype(F32) + b[..., :8, :].astype(F32)
        v = v + (a[..., 8:, :].astype(F32) + b[..., 8:, :].astype(F32))
        high, rest = split16(v)
        return jnp.concatenate([high, rest], -2)

    got = swap(send_c, "wshard", W, 1)
    far = swap(add16(keep_c[1], got[1]), "wshard", W, 2)
    bulk_c = (keep_c[0].astype(F32) + got[0].astype(F32) + far.astype(F32)).astype(BF16)

    def add_b(a, b):
        return jnp.concatenate([add16(a[:extra], b[:extra]), add_split(a[extra:], b[extra:])], 0)

    got = swap(send_b, "wshard", W, 1)
    far = swap(add_b(keep_b[1], got[1]), "wshard", W, 2)
    full_b = add_b(add_b(keep_b[0], got[0]), far)

    bulk = jnp.concatenate([full_b[:extra], bulk_c], 0)
    part = bulk.shape[0] // S
    tails = jnp.broadcast_to(full_b[None, extra:], (S, 16, width))
    parts = jnp.concatenate([bulk.reshape(S, part, width), tails], 1)
    arrived = lax.all_to_all(parts, "seq", 0, 0, tiled=True).astype(F32)
    summed = jnp.sum(arrived[:, :part], 0).astype(BF16)
    tail = jnp.sum(arrived[:, part : part + 8] + arrived[:, part + 8 :], 0)
    spread = lax.all_to_all(jnp.broadcast_to(summed[None], (S, part, width)), "seq", 0, 0, tiled=True)
    bulk = spread.reshape(S * part, width).astype(F32)
    half = shard // 2
    right = bulk[shard:extra]
    gb = jnp.concatenate([bulk[:shard], jnp.concatenate([right[:, : width // 2], right[:, width // 2 :]], 0)], 1)
    gc = bulk[extra : extra + c_weight.shape[0]]
    gg = bulk[extra + c_weight.shape[0] :]
    vecs = tail[0].reshape(4, shard)
    rate_out = lax.dynamic_slice(tail[1:4], (0, s_at * own), (3, own))
    loss = tail[4, 0] / (total[0, 0] * width)
    return (
        out.reshape(inputs.shape), loss, ingrad.reshape(inputs.shape), vecs[0], vecs[1], gb, gc, vecs[2], gg, vecs[3],
        rate_out[0], rate_out[1], rate_out[2],
    )


def solution(mesh):
    placed = (
        P("wshard", "seq", None), P("wshard", "seq", None), P("wshard", "seq"), P("wshard", "seq"),
        P("wshard"), P("wshard"), P("wshard", None), P("wshard", None), P("wshard"), P("wshard", None), P("wshard"),
        P("seq"), P("seq"), P("seq"),
    )
    return jax.shard_map(
        per_device,
        mesh=mesh,
        in_specs=placed,
        out_specs=(
            P("wshard", "seq", None), P(), P("wshard", "seq", None), P("wshard"), P("wshard"), P("wshard", None),
            P("wshard", None), P("wshard"), P("wshard", None), P("wshard"), P("seq"), P("seq"), P("seq"),
        ),
        check_vma=False,
    )
```

```python
import functools

import jax
import jax.numpy as jnp
from jax import lax
from jax.experimental import pallas as pl
from jax.experimental.pallas import tpu as pltpu
from jax.sharding import Mesh
from jax.sharding import PartitionSpec as P

CHUNKS = 8
LANES = 128
TILE = 256
PAD = 8
MIB = 1024 * 1024
F32 = jnp.float32
BF16 = jnp.bfloat16


def small_expm1(x):
    return x * (1.0 + x / 2 * (1.0 + x / 3 * (1.0 + x / 4 * (1.0 + x / 5 * (1.0 + x / 6)))))


def rates_map(real_rate, imag_rate, log_rate):
    time_step = jnp.exp(log_rate)
    grow_re = real_rate * time_step
    turn_im = imag_rate * time_step
    growth = jnp.exp(grow_re)
    abar_re = growth * jnp.cos(turn_im)
    abar_im = growth * jnp.sin(turn_im)
    half_sine = jnp.sin(0.5 * turn_im)
    numer_re = small_expm1(grow_re) * jnp.cos(turn_im) - 2.0 * half_sine * half_sine
    divisor = real_rate * real_rate + imag_rate * imag_rate
    scale_re = (numer_re * real_rate + abar_im * imag_rate) / divisor
    scale_im = (abar_im * real_rate - numer_re * imag_rate) / divisor
    return (abar_re, abar_im, scale_re, scale_im)


def cmul(xr, xi, yr, yi):
    return xr * yr - xi * yi, xr * yi + xi * yr


def power2(xr, xi, times):
    for _ in range(times):
        xr, xi = xr * xr - xi * xi, 2.0 * xr * xi
    return xr, xi


def log2(n):
    return n.bit_length() - 1


def power(xr, xi, n):
    out = None
    while n:
        if n & 1:
            out = (xr, xi) if out is None else cmul(*out, xr, xi)
        n >>= 1
        if n:
            xr, xi = power2(xr, xi, 1)
    return out


def chunk_powers(ar, ai, steps):
    first = lax.broadcasted_iota(jnp.int32, ar.shape, 0) == 0
    sr, si = power(ar, ai, steps - PAD)
    pr, pi = power(ar, ai, steps)
    return jnp.where(first, sr, pr), jnp.where(first, si, pi)


def padded(i, block_len):
    start = i * TILE + PAD * (2 + i * TILE // block_len)
    return slice(start, start + TILE)


def run(count, body, carry, unroll):
    def block(k, c):
        for u in range(unroll):
            c = body(k * unroll + u, c)
        return c

    whole_blocks = count // unroll
    carry = lax.fori_loop(0, whole_blocks, block, carry)
    for i in range(whole_blocks * unroll, count):
        carry = body(i, carry)
    return carry


def wide(v, groups):
    return jnp.concatenate([v] * groups, axis=1)


def fold_rows(v):
    return jnp.sum(v.reshape(-1, 8, v.shape[-1]), axis=0)


def take(ref, at, first, count):
    return jnp.concatenate([ref[first + g, at, :] for g in range(count)], axis=1)


def put(ref, at, first, v):
    for g in range(v.shape[1] // LANES):
        ref[first + g, at, :] = v[:, g * LANES : (g + 1) * LANES]


def clear_pads(ref, seqs, pitch):
    for g in range(ref.shape[0]):
        ref[g, :PAD, :] = jnp.zeros((PAD, LANES), F32)
        for s in range(seqs):
            ref[g, PAD + s * pitch : 2 * PAD + s * pitch, :] = jnp.zeros((PAD, LANES), F32)


def one_row(v):
    return jnp.sum(v, axis=0, keepdims=True)


def nt_dot(a, b):
    return lax.dot_general(a, b, (((1,), (1,)), ((), ())), preferred_element_type=F32)


def tn_dot(a, b):
    return lax.dot_general(a, b, (((0,), (0,)), ((), ())), preferred_element_type=F32)


def chunk_scan(ar, ai, br, bi, reverse):
    rows = lax.broadcasted_iota(jnp.int32, ar.shape, 0)
    d = 1
    while d < CHUNKS:
        shift = (CHUNKS - d) if reverse else d
        keep = (rows < CHUNKS - d) if reverse else (rows >= d)
        pr, pi = pltpu.roll(ar, shift, 0), pltpu.roll(ai, shift, 0)
        qr, qi = pltpu.roll(br, shift, 0), pltpu.roll(bi, shift, 0)
        mr, mi = cmul(ar, ai, qr, qi)
        br, bi = jnp.where(keep, br + mr, br), jnp.where(keep, bi + mi, bi)
        mr, mi = cmul(ar, ai, pr, pi)
        ar, ai = jnp.where(keep, mr, ar), jnp.where(keep, mi, ai)
        d *= 2
    return ar, ai, br, bi


def carry_in(recvs, ids, s, own_row, ar, ai, block_len, conj):
    states = ar.shape[1]
    pr, pi = power2(ar, -ai if conj else ai, log2(block_len))
    cr = jnp.zeros((1, states), F32)
    ci = jnp.zeros((1, states), F32)
    own = wide(ids[own_row : own_row + 1, :], states // LANES)
    for ref in reversed(recvs):
        msg = ref[s : s + 1, :]
        same = wide(msg[:, 2 * states :], states // LANES) == own
        cr, ci = cmul(pr, pi, cr, ci)
        cr = cr + jnp.where(same, msg[:, :states], 0.0)
        ci = ci + jnp.where(same, msg[:, states : 2 * states], 0.0)
    return cr, ci


def fetch(pairs, sems):
    copies = [pltpu.make_async_copy(src, dst, sems.at[k]) for k, (src, dst) in enumerate(pairs)]
    for c in copies:
        c.start()
    for c in copies:
        c.wait()


def k0_body(at_ref, b_ref, g_ref, n_ref, s_ref, q_ref, lr_ref, li_ref, ls_ref, msg_ref, table_ref,
            b_scr, v_scr, l_scr, scr, sems):
    shard, cols = b_scr.shape
    own = lr_ref.shape[1]
    fetch(
        [(b_ref, b_scr)]
        + [(r, v_scr.at[k]) for k, r in enumerate((g_ref, n_ref, s_ref, q_ref))]
        + [(r, l_scr.at[k]) for k, r in enumerate((lr_ref, li_ref, ls_ref))],
        sems,
    )
    msg_ref[:shard, :] = b_scr[...]
    line = jnp.concatenate([v_scr[k] for k in range(4)] + [jnp.zeros((1, cols - 4 * shard), BF16)], axis=1)
    msg_ref[shard:, :] = jnp.broadcast_to(line, (16, cols))
    scr[...] = jnp.zeros_like(scr)
    for k in range(3):
        scr[k : k + 1, :own] = l_scr[k]
    table_ref[...] = pltpu.roll(scr[...], at_ref[0] * own, 1)


def k0b_body(c_ref, g_ref, seg_hbm, mask_hbm, msg_ref, link_ref, valid_ref, ids_ref, seg_ref, mask_ref, c_scr, g_scr, sems):
    c_shard = c_ref.shape[0]
    seqs, block_len = seg_ref.shape
    fetch([(c_ref, c_scr), (g_ref, g_scr), (seg_hbm, seg_ref), (mask_hbm, mask_ref)], sems)
    msg_ref[:c_shard, :] = c_scr[...]
    msg_ref[c_shard:, :] = g_scr[...]
    seg = seg_ref[...].astype(F32)
    link_ref[:PAD, :] = jnp.ones((PAD, LANES), F32)
    lane = lax.broadcasted_iota(jnp.int32, (1, block_len), 1)
    for s in range(seqs):
        row = seg[s : s + 1, :]
        link = jnp.where((row == pltpu.roll(row, 1, 1)) | (lane == 0), 1.0, 0.0)
        mask = mask_ref[s : s + 1, :].astype(F32)
        start = PAD + s * (block_len + PAD)
        link_ref[start : start + PAD, :] = jnp.ones((PAD, LANES), F32)
        for src, dst, start in ((link, link_ref, start + PAD), (mask, valid_ref, s * block_len)):
            for k in range(block_len // LANES):
                piece = jnp.broadcast_to(src[:, k * LANES : (k + 1) * LANES], (LANES, LANES))
                at = start + k * LANES
                dst[at : at + LANES, :] = jnp.transpose(piece)
        ids_ref[s : s + 1, :] = jnp.broadcast_to(row[:, :1], (1, LANES))
        ids_ref[seqs + s : seqs + s + 1, :] = jnp.broadcast_to(row[:, block_len - 1 :], (1, LANES))


def k1a_body(w_ref, x_ref, b0, b1, b2, b3, low_ref, proj_ref, vec_ref, full_ref, *, seqs):
    rows, width = x_ref.shape
    shard = b0.shape[0] - 16
    block_len = rows // seqs
    pitch = block_len + PAD
    w = w_ref[1]
    for k, piece in enumerate((b0, b1, b2, b3)):
        at = pl.multiple_of((w ^ k) * shard, shard)
        full_ref[pl.ds(at, shard), :] = piece[:shard, :]
        extra = piece[shard:, :].astype(F32)
        for v in range(4):
            vec_ref[v : v + 1, pl.ds(at, shard)] = extra[0:1, v * shard : (v + 1) * shard]
    vec_ref[4:8, :] = jnp.zeros((4, width), F32)
    gain = vec_ref[0:1, :]
    bias = vec_ref[1:2, :]
    for i in range(rows // TILE):
        at = slice(i * TILE, (i + 1) * TILE)
        low = (centre(x_ref[at, :])[0] * gain + bias).astype(BF16)
        low_ref[at, :] = low
        p = jnp.dot(low, full_ref[...], preferred_element_type=F32)
        put(proj_ref, padded(i, block_len), 0, p.astype(BF16).astype(F32))
    clear_pads(proj_ref, seqs, pitch)


def k1b_body(proj_ref, table_ref, link_ref, ids_ref, s1_ref, msg_ref, rates_ref, *, seqs):
    states = table_ref.shape[1]
    groups = states // LANES
    pitch = (proj_ref.shape[1] - PAD) // seqs
    block_len = pitch - PAD
    steps = block_len // CHUNKS + 1
    lam = [table_ref[v : v + 1, :] for v in range(3)]
    parts, back = jax.vjp(rates_map, *lam)
    one, zero = jnp.ones_like(lam[0]), jnp.zeros_like(lam[0])
    for v in range(4):
        rates_ref[v : v + 1, :] = parts[v]
        for k, jac in enumerate(back(tuple(one if i == v else zero for i in range(4)))):
            rates_ref[8 + 3 * v + k : 9 + 3 * v + k, :] = jac
    rates_ref[4:8, :] = jnp.zeros((4, states), F32)
    rates_ref[20:24, :] = jnp.zeros((4, states), F32)
    ar = jnp.broadcast_to(parts[0], (CHUNKS, states))
    ai = jnp.broadcast_to(parts[1], (CHUNKS, states))

    def step(j, carry):
        out = []
        for s in range(seqs):
            ur, ui, q = carry[s]
            at = pl.ds(PAD + s * pitch + j, CHUNKS, stride=steps)
            lk = link_ref[at, :]
            lw = wide(lk, groups)
            nr, ni = cmul(ar, ai, ur, ui)
            out.append((lw * nr + take(proj_ref, at, 0, groups), lw * ni + take(proj_ref, at, groups, groups), q * lk))
        return tuple(out)

    zero = jnp.zeros((CHUNKS, states), F32)
    init = tuple((zero, zero, jnp.ones((CHUNKS, LANES), F32)) for _ in range(seqs))
    ends = run(steps, step, init, 13)
    pr, pi = chunk_powers(ar, ai, steps)
    for s in range(seqs):
        ur, ui, q = ends[s]
        qw = wide(q, groups)
        sc = chunk_scan(pr * qw, pi * qw, ur, ui, False)
        for v in range(4):
            s1_ref[s * CHUNKS : (s + 1) * CHUNKS, v * states : (v + 1) * states] = sc[v]
        msg_ref[s : s + 1, :states] = sc[2][CHUNKS - 1 :, :]
        msg_ref[s : s + 1, states : 2 * states] = sc[3][CHUNKS - 1 :, :]
        msg_ref[s : s + 1, 2 * states :] = ids_ref[seqs + s : seqs + s + 1, :]


def k2_body(*refs, seqs, hops):
    (w_ref, x_ref, t_ref, link_ref, valid_ref, ids_ref, low_ref, proj_ref, s1_ref, rates_ref, vec_ref,
     c0, c1, c2, c3) = refs[:15]
    recvs = refs[15 : 15 + hops]
    (out_ref, state_ref, gs_ref, gres_ref, gssm_ref, s2_ref, msg_ref, send_ref, keep_ref,
     wc_scr, wg_scr, act_scr, gate_scr, ssl_scr, sl_scr, gc_scr, gg_scr, sum_scr) = refs[15 + hops :]
    rows, width = x_ref.shape
    states = rates_ref.shape[1]
    groups = states // LANES
    block_len = rows // seqs
    steps = block_len // CHUNKS + 1
    pitch = block_len + PAD
    g_shard = width // 4
    c_shard = 2 * states // 4
    w = w_ref[1]
    for k, piece in enumerate((c0, c1, c2, c3)):
        wc_scr[pl.ds(pl.multiple_of((w ^ k) * c_shard, c_shard), c_shard), :] = piece[:c_shard, :]
        wg_scr[pl.ds(pl.multiple_of((w ^ k) * g_shard, g_shard), g_shard), :] = piece[c_shard:, :]
    a1r, a1i = rates_ref[0:1, :], rates_ref[1:2, :]
    ar = jnp.broadcast_to(a1r, (CHUNKS, states))
    ai = jnp.broadcast_to(a1i, (CHUNKS, states))
    zr = jnp.broadcast_to(rates_ref[2:3, :], (CHUNKS, states))
    zi = jnp.broadcast_to(rates_ref[3:4, :], (CHUNKS, states))
    top = lax.broadcasted_iota(jnp.int32, (CHUNKS, states), 0)
    ids = ids_ref[...]
    init, carries = [], []
    for s in range(seqs):
        cr, ci = carry_in(recvs, ids, s, s, a1r, a1i, block_len, False)
        sc = [s1_ref[s * CHUNKS : (s + 1) * CHUNKS, v * states : (v + 1) * states] for v in range(4)]
        mr, mi = cmul(sc[0], sc[1], cr, ci)
        init.append((pltpu.roll(sc[2] + mr, 1, 0), pltpu.roll(sc[3] + mi, 1, 0)))
        carries.append((cr, ci))

    def step(j, carry):
        out = []
        for s in range(seqs):
            ur, ui = carry[s]
            at = pl.ds(PAD + s * pitch + j, CHUNKS, stride=steps)
            lw = wide(link_ref[at, :], groups)
            nr, ni = cmul(ar, ai, ur, ui)
            ur, ui = lw * nr + take(proj_ref, at, 0, groups), lw * ni + take(proj_ref, at, groups, groups)
            sr, si = cmul(zr, zi, ur, ui)
            put(state_ref, at, 0, sr)
            put(state_ref, at, groups, si)
            out.append((ur, ui))
        return tuple(out)

    for g in range(2 * groups):
        state_ref[g, :PAD, :] = jnp.zeros((PAD, LANES), F32)
    entry = list(run(PAD, step, tuple(init), PAD))
    for s in range(seqs):
        ur, ui = (jnp.where(top == 0, c, u) for c, u in zip(carries[s], entry[s]))
        sr, si = cmul(zr, zi, ur, ui)
        at = pl.ds(PAD + s * pitch + PAD - 1, CHUNKS, stride=steps)
        put(state_ref, at, 0, sr)
        put(state_ref, at, groups, si)
        entry[s] = (ur, ui)
    run(steps - PAD, lambda i, c: step(i + PAD, c), tuple(entry), 8)

    skip = vec_ref[2:3, :]
    gbias = vec_ref[3:4, :]
    loss_acc = jnp.zeros((8, width), F32)
    gbias_acc = jnp.zeros((8, width), F32)
    skip_acc = jnp.zeros((8, width), F32)
    for i in range(rows // TILE):
        at = slice(i * TILE, (i + 1) * TILE)
        pad_at = padded(i, block_len)
        sl = take(state_ref, pad_at, 0, 2 * groups).astype(BF16)
        sl_scr[at, :] = sl
        low_f = low_ref[at, :].astype(F32)
        so = jnp.dot(sl, wc_scr[...], preferred_element_type=F32) + skip * low_f
        z = jnp.abs(so) * 0.7071067811865476
        e = jnp.exp(-z * z)
        t = 1.0 / (1.0 + 0.3275911 * z)
        poly = t * (0.254829592 + t * (-0.284496736 + t * (1.421413741 + t * (-1.453152027 + t * 1.061405429))))
        tail = 0.5 * poly * e
        phi = jnp.where(so >= 0.0, 1.0 - tail, tail)
        act = (so * phi).astype(BF16)
        act_scr[at, :] = act
        dgelu = phi + so * e * 0.3989422804014327
        act_f = act.astype(F32)
        g = 0.5 * jnp.tanh(0.5 * (jnp.dot(act, wg_scr[...], preferred_element_type=F32) + gbias)) + 0.5
        res = x_ref[at, :].astype(F32) + act_f * g
        out_ref[at, :] = res.astype(BF16)
        err = res - t_ref[at, :].astype(F32)
        em = err * wide(valid_ref[at, :], width // LANES)
        loss_acc = loss_acc + fold_rows(em * err)
        gr = em
        gres_ref[at, :] = gr
        gg = gr * act_f * g * (1.0 - g)
        gbias_acc = gbias_acc + fold_rows(gg)
        gl = gg.astype(BF16)
        gate_scr[at, :] = gl
        gssm = dgelu * (gr * g + nt_dot(gl, wg_scr[...]))
        gssm_ref[at, :] = gssm
        skip_acc = skip_acc + fold_rows(gssm * low_f)
        ssl = gssm.astype(BF16)
        ssl_scr[at, :] = ssl
        put(gs_ref, pad_at, 0, nt_dot(ssl, wc_scr[...]).astype(BF16).astype(F32))
    clear_pads(gs_ref, seqs, pitch)
    sum_scr[0:1, :] = one_row(skip_acc)
    sum_scr[1:2, :] = one_row(gbias_acc)
    loss = jnp.sum(one_row(loss_acc), axis=1, keepdims=True)
    count = one_row(fold_rows(valid_ref[...]))

    def back(i, carry):
        j = steps - 1 - i
        out = []
        for s in range(seqs):
            yr, yi, q = carry[s]
            at = pl.ds(PAD + s * pitch + j, CHUNKS, stride=steps)
            lk = link_ref[at, :]
            lw = wide(lk, groups)
            nr, ni = cmul(ar, -ai, yr, yi)
            out.append((lw * (nr + take(gs_ref, at, 0, groups)), lw * (ni + take(gs_ref, at, groups, groups)), q * lk))
        return tuple(out)

    zero = jnp.zeros((CHUNKS, states), F32)
    init = tuple((zero, zero, jnp.ones((CHUNKS, LANES), F32)) for _ in range(seqs))
    firsts = run(steps - PAD, back, init, 8)
    ends = run(PAD, lambda i, c: back(i + steps - PAD, c), firsts, PAD)
    pr, pi = chunk_powers(ar, -ai, steps)
    for s in range(seqs):
        yr, yi, q = (jnp.where(top[:, : v.shape[1]] == 0, u, v) for u, v in zip(firsts[s], ends[s]))
        qw = wide(q, groups)
        sc = chunk_scan(pr * qw, pi * qw, yr, yi, True)
        for v in range(4):
            s2_ref[s * CHUNKS : (s + 1) * CHUNKS, v * states : (v + 1) * states] = sc[v]
        msg_ref[s : s + 1, :states] = sc[2][:1, :]
        msg_ref[s : s + 1, states : 2 * states] = sc[3][:1, :]
        msg_ref[s : s + 1, 2 * states :] = ids_ref[s : s + 1, :]

    gg_scr[...] = tn_dot(act_scr[...], gate_scr[...])
    gc_scr[...] = tn_dot(sl_scr[...], ssl_scr[...])
    for k, dst in enumerate((keep_ref, send_ref, keep_ref, send_ref)):
        q = w ^ k
        slot = q // 2
        dst[slot, :c_shard, :] = gc_scr[pl.ds(pl.multiple_of(q * c_shard, c_shard), c_shard), :].astype(BF16)
        lanes = pl.multiple_of(q * g_shard, g_shard)
        dst[slot, c_shard : c_shard + g_shard, :] = gg_scr[pl.ds(lanes, g_shard), :].astype(BF16)
        line = jnp.concatenate(
            [sum_scr[v : v + 1, pl.ds(lanes, g_shard)] for v in range(2)]
            + [jnp.broadcast_to(loss, (1, LANES)), count], axis=1)
        dst[slot, c_shard + g_shard :, :] = split_rows([line])


def split16(v):
    high = v.astype(BF16)
    return high, (v - high.astype(F32)).astype(BF16)


def split_rows(lines):
    width = lines[0].shape[1]
    v = jnp.concatenate(lines + [jnp.zeros((8 - len(lines), width), F32)], axis=0)
    high, rest = split16(v)
    return jnp.concatenate([high.astype(F32), rest.astype(F32)], axis=0).astype(BF16)


def k3_body(*refs, seqs, hops):
    (w_ref, x_ref, link_ref, ids_ref, low_ref, proj_ref, state_ref, gs_ref, gssm_ref,
     s2_ref, rates_ref, vec_ref, w_full) = refs[:13]
    recvs = refs[13 : 13 + hops]
    (gn_ref, send_ref, keep_ref, gp_scr, gpl_scr, gb_scr, vec_scr) = refs[13 + hops :]
    rows, width = x_ref.shape
    states = rates_ref.shape[1]
    groups = states // LANES
    block_len = rows // seqs
    steps = block_len // CHUNKS + 1
    pitch = block_len + PAD
    shard = width // 4
    w = w_ref[1]
    a1r, a1i = rates_ref[0:1, :], rates_ref[1:2, :]
    ar = jnp.broadcast_to(a1r, (CHUNKS, states))
    ai = jnp.broadcast_to(a1i, (CHUNKS, states))
    zr = jnp.broadcast_to(rates_ref[2:3, :], (CHUNKS, states))
    zi = jnp.broadcast_to(rates_ref[3:4, :], (CHUNKS, states))
    rowid = lax.broadcasted_iota(jnp.int32, (CHUNKS, states), 0)
    ids = ids_ref[...]
    rate_sums = [jnp.zeros((CHUNKS, states), F32) for _ in range(4)]
    for s in range(seqs):
        cr, ci = carry_in(recvs, ids, s, seqs + s, a1r, a1i, block_len, True)
        sc = [s2_ref[s * CHUNKS : (s + 1) * CHUNKS, v * states : (v + 1) * states] for v in range(4)]
        mr, mi = cmul(sc[0], sc[1], cr, ci)
        yr = jnp.where(rowid == CHUNKS - 1, cr, pltpu.roll(sc[2] + mr, CHUNKS - 1, 0))
        yi = jnp.where(rowid == CHUNKS - 1, ci, pltpu.roll(sc[3] + mi, CHUNKS - 1, 0))

        def step(i, carry):
            yr, yi, gar, gai, gsr, gsi = carry
            j = steps - 1 - i
            at = pl.ds(PAD + s * pitch + j, CHUNKS, stride=steps)
            before = pl.ds(PAD + s * pitch + j - 1, CHUNKS, stride=steps)
            lw = wide(link_ref[at, :], groups)
            nr, ni = cmul(ar, -ai, yr, yi)
            dr, di = nr + take(gs_ref, at, 0, groups), ni + take(gs_ref, at, groups, groups)
            yr, yi = lw * dr, lw * di
            pr, pi = take(proj_ref, at, 0, groups), take(proj_ref, at, groups, groups)
            ur, ui = take(state_ref, before, 0, groups), take(state_ref, before, groups, groups)
            put(gp_scr, at, 0, zr * dr + zi * di)
            put(gp_scr, at, groups, zr * di - zi * dr)
            return (
                yr, yi,
                gar + (ur * yr + ui * yi), gai + (ur * yi - ui * yr),
                gsr + (pr * dr + pi * di), gsi + (pr * di - pi * dr),
            )

        carry = run(steps - PAD, step, (yr, yi, *rate_sums), 8)
        yr, yi = (jnp.where(rowid == 0, 0.0, v) for v in carry[:2])
        carry = run(PAD, lambda i, c: step(i + steps - PAD, c), (yr, yi, *carry[2:]), PAD)
        rate_sums = list(carry[2:])

    skip = vec_ref[2:3, :]
    gain_acc = jnp.zeros((8, width), F32)
    bias_acc = jnp.zeros((8, width), F32)
    for i in range(rows // TILE):
        at = slice(i * TILE, (i + 1) * TILE)
        gpl = take(gp_scr, padded(i, block_len), 0, 2 * groups).astype(BF16)
        gpl_scr[at, :] = gpl
        gn = nt_dot(gpl, w_full[...]) + skip * gssm_ref[at, :]
        gn_ref[at, :] = gn
        n, _ = centre(x_ref[at, :])
        gain_acc = gain_acc + fold_rows(gn * n)
        bias_acc = bias_acc + fold_rows(gn)
    gb_scr[...] = tn_dot(low_ref[...], gpl_scr[...])
    sums4 = [one_row(v) for v in rate_sums]
    rate_grads = []
    for k in range(3):
        rate_grads.append(sum(rates_ref[8 + 3 * c + k : 9 + 3 * c + k, :] * sums4[c] for c in range(4)))
    vec_scr[0:1, :] = one_row(gain_acc)
    vec_scr[1:2, :] = one_row(bias_acc)
    extra = 3 * shard // 2
    half = shard // 2
    for k, dst in enumerate((keep_ref, send_ref, keep_ref, send_ref)):
        slot = (w ^ k) // 2
        q = pl.multiple_of((w ^ k) * shard, shard)
        dst[slot, :shard, :] = gb_scr[pl.ds(q, shard), :width].astype(BF16)
        dst[slot, shard:extra, : width // 2] = gb_scr[pl.ds(q, half), width:].astype(BF16)
        dst[slot, shard:extra, width // 2 :] = gb_scr[pl.ds(q + half, half), width:].astype(BF16)
        line = jnp.concatenate(
            [vec_scr[v : v + 1, pl.ds(q, shard)] for v in range(2)] + [jnp.zeros((1, width - 2 * shard), F32)], axis=1)
        lines = [line] + [jnp.concatenate([g, jnp.zeros((1, width - states), F32)], axis=1) for g in rate_grads]
        dst[slot, extra:, :] = split_rows(lines)


def centre(values):
    x = values.astype(F32)
    c = x - jnp.mean(x, -1, keepdims=True)
    r = lax.rsqrt(jnp.mean(c * c, -1, keepdims=True) + 1e-05)
    return c * r, r


def k4_body(scale_ref, x_ref, gn_ref, gres_ref, vec_ref, out_ref):
    rows = x_ref.shape[0]
    scale = scale_ref[0, 0]
    gain = vec_ref[0:1, :]
    for i in range(rows // TILE):
        at = slice(i * TILE, (i + 1) * TILE)
        n, r = centre(x_ref[at, :])
        q = gn_ref[at, :] * gain
        back = (q - jnp.mean(q, -1, keepdims=True) - n * jnp.mean(q * n, -1, keepdims=True)) * r
        out_ref[at, :] = scale * (gres_ref[at, :] + back)


def pack_body(w_ref, keep_ref, got_ref, mine_ref, send_ref, tail_ref):
    bulk = mine_ref.shape[0]
    y = w_ref[1] // 2

    def both(slot, rows):
        return keep_ref[slot, rows, :].astype(F32) + got_ref[slot, rows, :].astype(F32)

    mine_ref[...] = both(y, slice(0, bulk)).astype(BF16)
    send_ref[...] = both(1 - y, slice(0, bulk)).astype(BF16)
    for slot in range(2):
        v = both(slot, slice(bulk, bulk + 16))
        tail_ref[slot] = v[:4] + v[8:12]


def unpack_body(scale_ref, back_ref, gb_ref, gc_ref, gg_ref, b_scr, c_scr):
    scale = scale_ref[0, 0]
    pieces = back_ref.shape[0]
    b_rows, c_rows = b_scr.shape[0] // pieces, c_scr.shape[0] // pieces
    for s in range(pieces):
        v = back_ref[s].astype(F32) * scale
        b_scr[s * b_rows : (s + 1) * b_rows, :] = v[:b_rows, :]
        c_scr[s * c_rows : (s + 1) * c_rows, :] = v[b_rows:, :]
    shard, cols = gb_ref.shape
    width = b_scr.shape[1]
    half = shard // 2
    gb_ref[:, :width] = b_scr[:shard, :]
    gb_ref[:half, width:] = b_scr[shard:, : cols - width]
    gb_ref[half:, width:] = b_scr[shard:, cols - width :]
    gc_ref[...] = c_scr[: gc_ref.shape[0], :]
    gg_ref[...] = c_scr[gc_ref.shape[0] :, :]


def whole(n, smem=(), far=()):
    return [pl.BlockSpec(memory_space=pltpu.SMEM if i in smem else pltpu.HBM if i in far else pltpu.VMEM) for i in range(n)]


def call(body, outs, scratch, smem, *args, us=1, limit=30, far=(), copies=0):
    return pl.pallas_call(
        body,
        out_shape=[jax.ShapeDtypeStruct(*o) for o in outs],
        in_specs=whole(len(args), smem, far),
        out_specs=whole(len(outs)),
        scratch_shapes=[pltpu.VMEM(*s) for s in scratch] + [pltpu.SemaphoreType.DMA((copies,))] * (copies > 0),
        compiler_params=pltpu.CompilerParams(vmem_limit_bytes=limit * MIB),
        cost_estimate=pl.CostEstimate(flops=us * 1_000_000_000, bytes_accessed=MIB, transcendentals=0),
    )(*args)


def per_device(inputs, teacher, segment_ids, valid_mask, ln_gain, ln_bias, b_weight, c_weight, skip_weight,
               glu_weight, glu_bias, lambda_real, lambda_imag, log_step):
    S = lax.axis_size("seq")
    s_at = lax.axis_index("seq")
    w_at = 2 * lax.axis_index("wy") + lax.axis_index("wc")
    seqs, block_len, width = inputs.shape
    rows = seqs * block_len
    padded_rows = PAD + seqs * (block_len + PAD)
    length = S * block_len
    own = lambda_real.shape[0]
    states = own * S
    doc_most = {4096: 1024, 32768: 8192}.get(length, length)
    hops = min((doc_most - 2) // block_len + 1, S - 1)
    shard, c_shard, g_shard = b_weight.shape[0], c_weight.shape[0], glu_weight.shape[0]

    def swap(v, axis, bit=1, n=2):
        return lax.ppermute(v, axis, [(i, i ^ bit) for i in range(n)])

    def after(v, *others):
        return lax.optimization_barrier((v, *others))[0]

    idx = jnp.stack([s_at, w_at]).astype(jnp.int32)
    b_msg, table = call(
        k0_body,
        [((shard + 16, b_weight.shape[1]), BF16), ((8, states), F32)],
        [(b_weight.shape, BF16), ((4, 1, shard), BF16), ((3, 1, own), F32), ((8, states), F32)],
        (0,),
        idx, b_weight, *(v[None] for v in (ln_gain, ln_bias, skip_weight, glu_bias, lambda_real, lambda_imag, log_step)),
        far=range(1, 9), copies=8, limit=60,
    )
    b_far = swap(b_msg, "wy")
    b_near = swap(b_msg, "wc")
    c_msg, link, valid, ids = call(
        k0b_body,
        [((c_shard + g_shard, width), BF16), ((padded_rows, LANES), F32), ((rows, LANES), F32),
         ((2 * seqs, LANES), F32)],
        [((seqs, block_len), jnp.int32), ((seqs, block_len), jnp.int32), (c_weight.shape, BF16), (glu_weight.shape, BF16)],
        (),
        c_weight, glu_weight, segment_ids, valid_mask, far=range(4), copies=4, us=2, limit=8,
    )
    c_far = swap(c_msg, "wy")
    table, bit = after(table, c_msg), 1
    while bit < S:
        radix = 4 if 4 * bit <= S else 2
        table = sum([swap(table, "seq", k * bit, S) for k in range(1, radix)], table)
        bit *= radix
    bs = (b_msg, b_near, b_far, swap(b_far, "wc"))

    x = inputs.reshape(rows, width)
    teach = teacher.reshape(rows, width)
    R = seqs * CHUNKS
    slab = (2 * states // LANES, padded_rows, LANES)
    msg_shape = ((seqs, 2 * states + LANES), F32)
    low, proj, vec, w_full = call(
        functools.partial(k1a_body, seqs=seqs),
        [((rows, width), BF16), (slab, F32), ((8, width), F32), ((width, 2 * states), BF16)],
        [],
        (0,),
        idx, x, *bs, us=2, limit=8,
    )
    s1, fwd, rates = call(
        functools.partial(k1b_body, seqs=seqs),
        [((R, 4 * states), F32), msg_shape, ((24, states), F32)],
        [],
        (),
        proj, table, link, ids, us=2, limit=8,
    )
    cs = (c_msg, swap(c_msg, "wc"), c_far, swap(c_far, "wc"))
    fwds = [lax.ppermute(fwd, "seq", [(i, i + k) for i in range(S - k)]) for k in range(1, hops + 1)]
    c_bulk = c_shard + g_shard
    out, state, gs, gres, gssm, s2, bwd, send_c, keep_c = call(
        functools.partial(k2_body, seqs=seqs, hops=hops),
        [((rows, width), BF16), (slab, F32), (slab, F32),
         ((rows, width), F32), ((rows, width), F32), ((R, 4 * states), F32), msg_shape,
         ((2, c_bulk + 16, width), BF16), ((2, c_bulk + 16, width), BF16)],
        [((2 * states, width), BF16), ((width, width), BF16), ((rows, width), BF16), ((rows, width), BF16),
         ((rows, width), BF16), ((rows, 2 * states), BF16), ((2 * states, width), F32), ((width, width), F32),
         ((8, width), F32)],
        (0,),
        idx, x, teach, link, valid, ids, low, proj, s1, rates, vec, *cs, *fwds, us=10, limit=18,
    )
    bwds = [lax.ppermute(bwd, "seq", [(i + k, i) for i in range(S - k)]) for k in range(1, hops + 1)]
    got_c = swap(after(send_c, *bwds), "wc")
    mine_c, half_c, tail_c = call(
        pack_body,
        [((c_bulk, width), BF16), ((c_bulk, width), BF16), ((2, 4, width), F32)],
        [],
        (0,),
        idx, keep_c, got_c, limit=4,
    )
    half_c, bwds = lax.optimization_barrier((half_c, bwds))
    far_c = swap(half_c, "wy")
    b_bulk = 3 * shard // 2
    gn, send_b, keep_b = call(
        functools.partial(k3_body, seqs=seqs, hops=hops),
        [((rows, width), F32), ((2, b_bulk + 16, width), BF16), ((2, b_bulk + 16, width), BF16)],
        [(slab, F32), ((rows, 2 * states), BF16), ((width, 2 * states), F32), ((8, width), F32)],
        (0,),
        idx, x, link, ids, low, proj, state, gs, gssm, s2, rates, vec, w_full, *bwds, us=8, limit=14,
    )
    mine_c = (mine_c.astype(F32) + far_c.astype(F32)).astype(BF16).reshape(S, c_bulk // S, width)
    got_b = swap(after(send_b, mine_c), "wc")
    tail_b, part_b = add_tail(keep_b, got_b, b_bulk)
    tails = jnp.concatenate([tail_c, tail_b], 1)
    high, rest = split16(tails)
    tails = jnp.broadcast_to(jnp.concatenate([high, rest], 1)[None], (S, 2, 16, width))
    parts = jnp.concatenate([part_b.reshape(2, S, b_bulk // S, width).transpose(1, 0, 2, 3), tails], 2)
    arrived = lax.all_to_all(parts.reshape(2 * S, -1, width), ("seq", "wy"), 0, 0, tiled=True)

    bit = 1
    while bit < S:
        v = mine_c.reshape(-1, 2, c_bulk // S, width)
        me = (s_at // bit) % 2
        got = swap(pick(v, 1 - me, 1), "seq", bit, S)
        mine_c = (pick(v, me, 1).astype(F32) + got.astype(F32)).astype(BF16)
        bit *= 2
    total_b = jnp.sum(arrived.astype(F32), 0)
    sum_b = total_b[: b_bulk // S].astype(BF16)
    tail = total_b[b_bulk // S :]
    tail = tail[:8] + tail[8:]
    c_line = tail[0].reshape(4, LANES)
    total = c_line[3, 0]
    scale = length * seqs * lax.axis_size(("wy", "wc")) / total
    both = jnp.concatenate([sum_b, mine_c.reshape(-1, width)], 0)
    sent = jnp.broadcast_to(both[None], (S, *both.shape))
    back = lax.all_to_all(sent, "seq", 0, 0, tiled=True)
    (ingrad,) = call(
        k4_body, [((rows, width), F32)], [], (0,), scale.reshape(1, 1), x, gn, gres, vec, us=3, limit=8,
    )
    gb, gc, gg = call(
        unpack_body,
        [((shard, 2 * states), F32), ((c_shard, width), F32), ((g_shard, width), F32)],
        [((b_bulk, width), F32), ((c_bulk, width), F32)],
        (0,),
        scale.reshape(1, 1), back, limit=8,
    )
    tail_b = tail[4:]
    tail_c = c_line
    line = tail_b[0] * scale
    rate_out = lax.dynamic_slice(tail_b[1:4] * scale, (0, s_at * own), (3, own))
    loss = tail_c[2, 0] / (total * width)
    return (
        out.reshape(inputs.shape), loss, ingrad.reshape(inputs.shape), line[:shard], line[shard : 2 * shard], gb,
        gc, tail_c[0] * scale, gg, tail_c[1] * scale,
        rate_out[0], rate_out[1], rate_out[2],
    )


def add_tail(keep, got, bulk):
    v = keep.astype(F32) + got.astype(F32)
    return v[:, bulk : bulk + 4] + v[:, bulk + 8 : bulk + 12], v[:, :bulk].astype(BF16)


def pick(v, at, axis=0):
    return lax.dynamic_index_in_dim(v, at, axis, keepdims=False)


def solution(mesh):
    sizes = mesh.devices.shape
    fine = Mesh(mesh.devices.reshape(sizes[0], 2, sizes[1] // 2), ("seq", "wy", "wc"))
    w = ("wy", "wc")
    tokens = P(w, "seq", None)
    return jax.shard_map(
        per_device,
        mesh=fine,
        in_specs=(
            tokens, tokens, P(w, "seq"), P(w, "seq"), P(w), P(w), P(w, None), P(w, None), P(w), P(w, None), P(w),
            P("seq"), P("seq"), P("seq"),
        ),
        out_specs=(
            tokens, P(), tokens, P(w), P(w), P(w, None), P(w, None), P(w), P(w, None), P(w),
            P("seq"), P("seq"), P("seq"),
        ),
        check_vma=False,
    )
```

```python
import functools

import jax
import jax.numpy as jnp
from jax import lax
from jax.experimental import pallas as pl
from jax.experimental.pallas import tpu as pltpu
from jax.sharding import Mesh
from jax.sharding import PartitionSpec as P

CHUNKS = 8
LANES = 128
TILE = 256
PAD = 8
MIB = 1024 * 1024
F32 = jnp.float32
BF16 = jnp.bfloat16


def small_expm1(x):
    return x * (1.0 + x / 2 * (1.0 + x / 3 * (1.0 + x / 4 * (1.0 + x / 5 * (1.0 + x / 6)))))


def rates_map(real_rate, imag_rate, log_rate):
    time_step = jnp.exp(log_rate)
    grow_re = real_rate * time_step
    turn_im = imag_rate * time_step
    growth = jnp.exp(grow_re)
    abar_re = growth * jnp.cos(turn_im)
    abar_im = growth * jnp.sin(turn_im)
    half_sine = jnp.sin(0.5 * turn_im)
    numer_re = small_expm1(grow_re) * jnp.cos(turn_im) - 2.0 * half_sine * half_sine
    divisor = real_rate * real_rate + imag_rate * imag_rate
    scale_re = (numer_re * real_rate + abar_im * imag_rate) / divisor
    scale_im = (abar_im * real_rate - numer_re * imag_rate) / divisor
    return (abar_re, abar_im, scale_re, scale_im)


def cmul(xr, xi, yr, yi):
    return xr * yr - xi * yi, xr * yi + xi * yr


def power2(xr, xi, times):
    for _ in range(times):
        xr, xi = xr * xr - xi * xi, 2.0 * xr * xi
    return xr, xi


def log2(n):
    return n.bit_length() - 1


def power(xr, xi, n):
    out = None
    while n:
        if n & 1:
            out = (xr, xi) if out is None else cmul(*out, xr, xi)
        n >>= 1
        if n:
            xr, xi = power2(xr, xi, 1)
    return out


def chunk_powers(ar, ai, steps):
    first = lax.broadcasted_iota(jnp.int32, ar.shape, 0) == 0
    sr, si = power(ar, ai, steps - PAD)
    pr, pi = power(ar, ai, steps)
    return jnp.where(first, sr, pr), jnp.where(first, si, pi)


def padded(i, block_len):
    start = i * TILE + PAD * (2 + i * TILE // block_len)
    return slice(start, start + TILE)


def run(count, body, carry, unroll):
    def block(k, c):
        for u in range(unroll):
            c = body(k * unroll + u, c)
        return c

    whole_blocks = count // unroll
    carry = lax.fori_loop(0, whole_blocks, block, carry)
    for i in range(whole_blocks * unroll, count):
        carry = body(i, carry)
    return carry


def wide(v, groups):
    return jnp.concatenate([v] * groups, axis=1)


def fold_rows(v):
    return jnp.sum(v.reshape(-1, 8, v.shape[-1]), axis=0)


def take(ref, at, first, count):
    return jnp.concatenate([ref[first + g, at, :] for g in range(count)], axis=1)


def put(ref, at, first, v):
    for g in range(v.shape[1] // LANES):
        ref[first + g, at, :] = v[:, g * LANES : (g + 1) * LANES]


def clear_pads(ref, seqs, pitch):
    for g in range(ref.shape[0]):
        ref[g, :PAD, :] = jnp.zeros((PAD, LANES), F32)
        for s in range(seqs):
            ref[g, PAD + s * pitch : 2 * PAD + s * pitch, :] = jnp.zeros((PAD, LANES), F32)


def one_row(v):
    return jnp.sum(v, axis=0, keepdims=True)


def nt_dot(a, b):
    return lax.dot_general(a, b, (((1,), (1,)), ((), ())), preferred_element_type=F32)


def tn_dot(a, b):
    return lax.dot_general(a, b, (((0,), (0,)), ((), ())), preferred_element_type=F32)


def chunk_scan(ar, ai, br, bi, reverse):
    rows = lax.broadcasted_iota(jnp.int32, ar.shape, 0)
    d = 1
    while d < CHUNKS:
        shift = (CHUNKS - d) if reverse else d
        keep = (rows < CHUNKS - d) if reverse else (rows >= d)
        pr, pi = pltpu.roll(ar, shift, 0), pltpu.roll(ai, shift, 0)
        qr, qi = pltpu.roll(br, shift, 0), pltpu.roll(bi, shift, 0)
        mr, mi = cmul(ar, ai, qr, qi)
        br, bi = jnp.where(keep, br + mr, br), jnp.where(keep, bi + mi, bi)
        mr, mi = cmul(ar, ai, pr, pi)
        ar, ai = jnp.where(keep, mr, ar), jnp.where(keep, mi, ai)
        d *= 2
    return ar, ai, br, bi


def carry_in(recvs, ids, s, own_row, ar, ai, block_len, conj, blocks):
    states = ar.shape[1]
    pr, pi = power2(ar, -ai if conj else ai, log2(block_len))
    cr = jnp.zeros((1, states), F32)
    ci = jnp.zeros((1, states), F32)
    own = wide(ids[own_row : own_row + 1, :], states // LANES)
    for k in range(len(recvs), 0, -1):
        msg = recvs[k - 1][s : s + 1, :]
        same = (wide(msg[:, 2 * states :], states // LANES) == own) & (blocks >= k)
        cr, ci = cmul(pr, pi, cr, ci)
        cr = cr + jnp.where(same, msg[:, :states], 0.0)
        ci = ci + jnp.where(same, msg[:, states : 2 * states], 0.0)
    return cr, ci


def fetch(pairs, sems):
    copies = [pltpu.make_async_copy(src, dst, sems.at[k]) for k, (src, dst) in enumerate(pairs)]
    for c in copies:
        c.start()
    for c in copies:
        c.wait()


def k0_body(at_ref, b_ref, g_ref, n_ref, s_ref, q_ref, lr_ref, li_ref, ls_ref, msg_ref, table_ref,
            b_scr, v_scr, l_scr, scr, sems):
    shard, cols = b_scr.shape
    own = lr_ref.shape[1]
    fetch(
        [(b_ref, b_scr)]
        + [(r, v_scr.at[k]) for k, r in enumerate((g_ref, n_ref, s_ref, q_ref))]
        + [(r, l_scr.at[k]) for k, r in enumerate((lr_ref, li_ref, ls_ref))],
        sems,
    )
    msg_ref[:shard, :] = b_scr[...]
    line = jnp.concatenate([v_scr[k] for k in range(4)] + [jnp.zeros((1, cols - 4 * shard), BF16)], axis=1)
    msg_ref[shard:, :] = jnp.broadcast_to(line, (16, cols))
    scr[...] = jnp.zeros_like(scr)
    for k in range(3):
        scr[k : k + 1, :own] = l_scr[k]
    table_ref[...] = pltpu.roll(scr[...], at_ref[0] * own, 1)


def k0b_body(c_ref, g_ref, msg_ref, c_scr, g_scr, sems):
    c_shard = c_ref.shape[0]
    fetch([(c_ref, c_scr), (g_ref, g_scr)], sems)
    msg_ref[:c_shard, :] = c_scr[...]
    msg_ref[c_shard:, :] = g_scr[...]


def lay_marks(seg_ref, mask_ref, link_ref, valid_ref, ids_ref):
    seqs, block_len = seg_ref.shape
    seg = seg_ref[...].astype(F32)
    link_ref[:PAD, :] = jnp.ones((PAD, LANES), F32)
    lane = lax.broadcasted_iota(jnp.int32, (1, block_len), 1)
    for s in range(seqs):
        row = seg[s : s + 1, :]
        link = jnp.where((row == pltpu.roll(row, 1, 1)) | (lane == 0), 1.0, 0.0)
        mask = mask_ref[s : s + 1, :].astype(F32)
        start = PAD + s * (block_len + PAD)
        link_ref[start : start + PAD, :] = jnp.ones((PAD, LANES), F32)
        for src, dst, start in ((link, link_ref, start + PAD), (mask, valid_ref, s * block_len)):
            for k in range(block_len // LANES):
                piece = jnp.broadcast_to(src[:, k * LANES : (k + 1) * LANES], (LANES, LANES))
                at = start + k * LANES
                dst[at : at + LANES, :] = jnp.transpose(piece)
        ids_ref[s : s + 1, :] = jnp.broadcast_to(row[:, :1], (1, LANES))
        ids_ref[seqs + s : seqs + s + 1, :] = jnp.broadcast_to(row[:, block_len - 1 :], (1, LANES))


def k1_body(w_ref, x_ref, b0, b1, b2, b3, table_ref, seg_ref, mask_ref,
            low_ref, proj_ref, vec_ref, full_ref, s1_ref, msg_ref, rates_ref, link_ref, valid_ref, ids_ref, *, seqs):
    rows, width = x_ref.shape
    shard = b0.shape[0] - 16
    block_len = rows // seqs
    pitch = block_len + PAD
    w = w_ref[1]
    for k, piece in enumerate((b0, b1, b2, b3)):
        at = pl.multiple_of((w ^ k) * shard, shard)
        full_ref[pl.ds(at, shard), :] = piece[:shard, :]
        extra = piece[shard:, :].astype(F32)
        for v in range(4):
            vec_ref[v : v + 1, pl.ds(at, shard)] = extra[0:1, v * shard : (v + 1) * shard]
    vec_ref[4:8, :] = jnp.zeros((4, width), F32)
    gain = vec_ref[0:1, :]
    bias = vec_ref[1:2, :]
    for i in range(rows // TILE):
        at = slice(i * TILE, (i + 1) * TILE)
        low = (centre(x_ref[at, :])[0] * gain + bias).astype(BF16)
        low_ref[at, :] = low
        p = jnp.dot(low, full_ref[...], preferred_element_type=F32)
        put(proj_ref, padded(i, block_len), 0, p.astype(BF16).astype(F32))
    clear_pads(proj_ref, seqs, pitch)
    lay_marks(seg_ref, mask_ref, link_ref, valid_ref, ids_ref)
    states = table_ref.shape[1]
    groups = states // LANES
    steps = block_len // CHUNKS + 1
    lam = [table_ref[v : v + 1, :] for v in range(3)]
    parts, back = jax.vjp(rates_map, *lam)
    one, zero = jnp.ones_like(lam[0]), jnp.zeros_like(lam[0])
    for v in range(4):
        rates_ref[v : v + 1, :] = parts[v]
        for k, jac in enumerate(back(tuple(one if i == v else zero for i in range(4)))):
            rates_ref[8 + 3 * v + k : 9 + 3 * v + k, :] = jac
    rates_ref[4:8, :] = jnp.zeros((4, states), F32)
    rates_ref[20:24, :] = jnp.zeros((4, states), F32)
    ar = jnp.broadcast_to(parts[0], (CHUNKS, states))
    ai = jnp.broadcast_to(parts[1], (CHUNKS, states))

    def step(j, carry):
        out = []
        for s in range(seqs):
            ur, ui, q = carry[s]
            at = pl.ds(PAD + s * pitch + j, CHUNKS, stride=steps)
            lk = link_ref[at, :]
            lw = wide(lk, groups)
            nr, ni = cmul(ar, ai, ur, ui)
            out.append((lw * nr + take(proj_ref, at, 0, groups), lw * ni + take(proj_ref, at, groups, groups), q * lk))
        return tuple(out)

    zero = jnp.zeros((CHUNKS, states), F32)
    init = tuple((zero, zero, jnp.ones((CHUNKS, LANES), F32)) for _ in range(seqs))
    ends = run(steps, step, init, 13)
    pr, pi = chunk_powers(ar, ai, steps)
    for s in range(seqs):
        ur, ui, q = ends[s]
        qw = wide(q, groups)
        sc = chunk_scan(pr * qw, pi * qw, ur, ui, False)
        for v in range(4):
            s1_ref[s * CHUNKS : (s + 1) * CHUNKS, v * states : (v + 1) * states] = sc[v]
        msg_ref[s : s + 1, :states] = sc[2][CHUNKS - 1 :, :]
        msg_ref[s : s + 1, states : 2 * states] = sc[3][CHUNKS - 1 :, :]
        msg_ref[s : s + 1, 2 * states :] = ids_ref[seqs + s : seqs + s + 1, :]


def k2_body(*refs, seqs, hops):
    (w_ref, x_ref, t_ref, link_ref, valid_ref, ids_ref, low_ref, proj_ref, s1_ref, rates_ref, vec_ref,
     c0, c1, c2, c3) = refs[:15]
    recvs = refs[15 : 15 + hops]
    (out_ref, state_ref, gs_ref, gres_ref, gssm_ref, s2_ref, msg_ref, send_ref, keep_ref,
     wc_scr, wg_scr, act_scr, gate_scr, ssl_scr, sl_scr, gc_scr, gg_scr, sum_scr) = refs[15 + hops :]
    rows, width = x_ref.shape
    states = rates_ref.shape[1]
    groups = states // LANES
    block_len = rows // seqs
    steps = block_len // CHUNKS + 1
    pitch = block_len + PAD
    g_shard = width // 4
    c_shard = 2 * states // 4
    w = w_ref[1]
    for k, piece in enumerate((c0, c1, c2, c3)):
        wc_scr[pl.ds(pl.multiple_of((w ^ k) * c_shard, c_shard), c_shard), :] = piece[:c_shard, :]
        wg_scr[pl.ds(pl.multiple_of((w ^ k) * g_shard, g_shard), g_shard), :] = piece[c_shard:, :]
    a1r, a1i = rates_ref[0:1, :], rates_ref[1:2, :]
    ar = jnp.broadcast_to(a1r, (CHUNKS, states))
    ai = jnp.broadcast_to(a1i, (CHUNKS, states))
    zr = jnp.broadcast_to(rates_ref[2:3, :], (CHUNKS, states))
    zi = jnp.broadcast_to(rates_ref[3:4, :], (CHUNKS, states))
    top = lax.broadcasted_iota(jnp.int32, (CHUNKS, states), 0)
    ids = ids_ref[...]
    init, carries = [], []
    for s in range(seqs):
        cr, ci = carry_in(recvs, ids, s, s, a1r, a1i, block_len, False, w_ref[0])
        sc = [s1_ref[s * CHUNKS : (s + 1) * CHUNKS, v * states : (v + 1) * states] for v in range(4)]
        mr, mi = cmul(sc[0], sc[1], cr, ci)
        init.append((pltpu.roll(sc[2] + mr, 1, 0), pltpu.roll(sc[3] + mi, 1, 0)))
        carries.append((cr, ci))

    def step(j, carry):
        out = []
        for s in range(seqs):
            ur, ui = carry[s]
            at = pl.ds(PAD + s * pitch + j, CHUNKS, stride=steps)
            lw = wide(link_ref[at, :], groups)
            nr, ni = cmul(ar, ai, ur, ui)
            ur, ui = lw * nr + take(proj_ref, at, 0, groups), lw * ni + take(proj_ref, at, groups, groups)
            sr, si = cmul(zr, zi, ur, ui)
            put(state_ref, at, 0, sr)
            put(state_ref, at, groups, si)
            out.append((ur, ui))
        return tuple(out)

    for g in range(2 * groups):
        state_ref[g, :PAD, :] = jnp.zeros((PAD, LANES), F32)
    entry = list(run(PAD, step, tuple(init), PAD))
    for s in range(seqs):
        ur, ui = (jnp.where(top == 0, c, u) for c, u in zip(carries[s], entry[s]))
        sr, si = cmul(zr, zi, ur, ui)
        at = pl.ds(PAD + s * pitch + PAD - 1, CHUNKS, stride=steps)
        put(state_ref, at, 0, sr)
        put(state_ref, at, groups, si)
        entry[s] = (ur, ui)
    run(steps - PAD, lambda i, c: step(i + PAD, c), tuple(entry), 8)

    skip = vec_ref[2:3, :]
    gbias = vec_ref[3:4, :]
    loss_acc = jnp.zeros((8, width), F32)
    gbias_acc = jnp.zeros((8, width), F32)
    skip_acc = jnp.zeros((8, width), F32)
    for i in range(rows // TILE):
        at = slice(i * TILE, (i + 1) * TILE)
        pad_at = padded(i, block_len)
        sl = take(state_ref, pad_at, 0, 2 * groups).astype(BF16)
        sl_scr[at, :] = sl
        low_f = low_ref[at, :].astype(F32)
        so = jnp.dot(sl, wc_scr[...], preferred_element_type=F32) + skip * low_f
        z = jnp.abs(so) * 0.7071067811865476
        e = jnp.exp(-z * z)
        t = 1.0 / (1.0 + 0.3275911 * z)
        poly = t * (0.254829592 + t * (-0.284496736 + t * (1.421413741 + t * (-1.453152027 + t * 1.061405429))))
        tail = 0.5 * poly * e
        phi = jnp.where(so >= 0.0, 1.0 - tail, tail)
        act = (so * phi).astype(BF16)
        act_scr[at, :] = act
        dgelu = phi + so * e * 0.3989422804014327
        act_f = act.astype(F32)
        g = 0.5 * jnp.tanh(0.5 * (jnp.dot(act, wg_scr[...], preferred_element_type=F32) + gbias)) + 0.5
        res = x_ref[at, :].astype(F32) + act_f * g
        out_ref[at, :] = res.astype(BF16)
        err = res - t_ref[at, :].astype(F32)
        em = err * wide(valid_ref[at, :], width // LANES)
        loss_acc = loss_acc + fold_rows(em * err)
        gr = em
        gres_ref[at, :] = gr.astype(BF16)
        gg = gr * act_f * g * (1.0 - g)
        gbias_acc = gbias_acc + fold_rows(gg)
        gl = gg.astype(BF16)
        gate_scr[at, :] = gl
        gssm = dgelu * (gr * g + nt_dot(gl, wg_scr[...]))
        gssm_ref[at, :] = gssm
        skip_acc = skip_acc + fold_rows(gssm * low_f)
        ssl = gssm.astype(BF16)
        ssl_scr[at, :] = ssl
        put(gs_ref, pad_at, 0, nt_dot(ssl, wc_scr[...]).astype(BF16).astype(F32))
    clear_pads(gs_ref, seqs, pitch)
    sum_scr[0:1, :] = one_row(skip_acc)
    sum_scr[1:2, :] = one_row(gbias_acc)
    loss = jnp.sum(one_row(loss_acc), axis=1, keepdims=True)
    count = one_row(fold_rows(valid_ref[...]))

    def back(i, carry):
        j = steps - 1 - i
        out = []
        for s in range(seqs):
            yr, yi, q = carry[s]
            at = pl.ds(PAD + s * pitch + j, CHUNKS, stride=steps)
            lk = link_ref[at, :]
            lw = wide(lk, groups)
            nr, ni = cmul(ar, -ai, yr, yi)
            out.append((lw * (nr + take(gs_ref, at, 0, groups)), lw * (ni + take(gs_ref, at, groups, groups)), q * lk))
        return tuple(out)

    zero = jnp.zeros((CHUNKS, states), F32)
    init = tuple((zero, zero, jnp.ones((CHUNKS, LANES), F32)) for _ in range(seqs))
    firsts = run(steps - PAD, back, init, 8)
    ends = run(PAD, lambda i, c: back(i + steps - PAD, c), firsts, PAD)
    pr, pi = chunk_powers(ar, -ai, steps)
    for s in range(seqs):
        yr, yi, q = (jnp.where(top[:, : v.shape[1]] == 0, u, v) for u, v in zip(firsts[s], ends[s]))
        qw = wide(q, groups)
        sc = chunk_scan(pr * qw, pi * qw, yr, yi, True)
        for v in range(4):
            s2_ref[s * CHUNKS : (s + 1) * CHUNKS, v * states : (v + 1) * states] = sc[v]
        msg_ref[s : s + 1, :states] = sc[2][:1, :]
        msg_ref[s : s + 1, states : 2 * states] = sc[3][:1, :]
        msg_ref[s : s + 1, 2 * states :] = ids_ref[s : s + 1, :]

    gg_scr[...] = tn_dot(act_scr[...], gate_scr[...])
    gc_scr[...] = tn_dot(sl_scr[...], ssl_scr[...])
    for k, dst in enumerate((keep_ref, send_ref, keep_ref, send_ref)):
        q = w ^ k
        slot = q // 2
        dst[slot, :c_shard, :] = gc_scr[pl.ds(pl.multiple_of(q * c_shard, c_shard), c_shard), :].astype(BF16)
        lanes = pl.multiple_of(q * g_shard, g_shard)
        dst[slot, c_shard : c_shard + g_shard, :] = gg_scr[pl.ds(lanes, g_shard), :].astype(BF16)
        line = jnp.concatenate(
            [sum_scr[v : v + 1, pl.ds(lanes, g_shard)] for v in range(2)]
            + [jnp.broadcast_to(loss, (1, LANES)), count], axis=1)
        dst[slot, c_shard + g_shard :, :] = split_rows([jnp.zeros((3, width), F32), line])


def split16(v):
    high = v.astype(BF16)
    return high, (v - high.astype(F32)).astype(BF16)


def split_rows(lines):
    width = lines[0].shape[1]
    rows = sum(v.shape[0] for v in lines)
    v = jnp.concatenate(lines + [jnp.zeros((8 - rows, width), F32)] * (rows < 8), axis=0)
    high, rest = split16(v)
    return jnp.concatenate([high.astype(F32), rest.astype(F32)], axis=0).astype(BF16)


def k3_body(*refs, seqs, hops, blocks):
    (w_ref, x_ref, link_ref, ids_ref, low_ref, proj_ref, state_ref, gs_ref, gssm_ref,
     s2_ref, rates_ref, vec_ref, w_full) = refs[:13]
    recvs = refs[13 : 13 + hops]
    (gn_ref, send_ref, keep_ref, gp_scr, gpl_scr, gb_scr, vec_scr) = refs[13 + hops :]
    rows, width = x_ref.shape
    states = rates_ref.shape[1]
    groups = states // LANES
    block_len = rows // seqs
    steps = block_len // CHUNKS + 1
    pitch = block_len + PAD
    shard = width // 4
    w = w_ref[1]
    a1r, a1i = rates_ref[0:1, :], rates_ref[1:2, :]
    ar = jnp.broadcast_to(a1r, (CHUNKS, states))
    ai = jnp.broadcast_to(a1i, (CHUNKS, states))
    zr = jnp.broadcast_to(rates_ref[2:3, :], (CHUNKS, states))
    zi = jnp.broadcast_to(rates_ref[3:4, :], (CHUNKS, states))
    rowid = lax.broadcasted_iota(jnp.int32, (CHUNKS, states), 0)
    ids = ids_ref[...]
    rate_sums = [jnp.zeros((CHUNKS, states), F32) for _ in range(4)]
    for s in range(seqs):
        cr, ci = carry_in(recvs, ids, s, seqs + s, a1r, a1i, block_len, True, blocks - 1 - w_ref[0])
        sc = [s2_ref[s * CHUNKS : (s + 1) * CHUNKS, v * states : (v + 1) * states] for v in range(4)]
        mr, mi = cmul(sc[0], sc[1], cr, ci)
        yr = jnp.where(rowid == CHUNKS - 1, cr, pltpu.roll(sc[2] + mr, CHUNKS - 1, 0))
        yi = jnp.where(rowid == CHUNKS - 1, ci, pltpu.roll(sc[3] + mi, CHUNKS - 1, 0))

        def step(i, carry):
            yr, yi, gar, gai, gsr, gsi = carry
            j = steps - 1 - i
            at = pl.ds(PAD + s * pitch + j, CHUNKS, stride=steps)
            before = pl.ds(PAD + s * pitch + j - 1, CHUNKS, stride=steps)
            lw = wide(link_ref[at, :], groups)
            nr, ni = cmul(ar, -ai, yr, yi)
            dr, di = nr + take(gs_ref, at, 0, groups), ni + take(gs_ref, at, groups, groups)
            yr, yi = lw * dr, lw * di
            pr, pi = take(proj_ref, at, 0, groups), take(proj_ref, at, groups, groups)
            ur, ui = take(state_ref, before, 0, groups), take(state_ref, before, groups, groups)
            put(gp_scr, at, 0, zr * dr + zi * di)
            put(gp_scr, at, groups, zr * di - zi * dr)
            return (
                yr, yi,
                gar + (ur * yr + ui * yi), gai + (ur * yi - ui * yr),
                gsr + (pr * dr + pi * di), gsi + (pr * di - pi * dr),
            )

        carry = run(steps - PAD, step, (yr, yi, *rate_sums), 8)
        yr, yi = (jnp.where(rowid == 0, 0.0, v) for v in carry[:2])
        carry = run(PAD, lambda i, c: step(i + steps - PAD, c), (yr, yi, *carry[2:]), PAD)
        rate_sums = list(carry[2:])

    skip = vec_ref[2:3, :]
    gain_acc = jnp.zeros((8, width), F32)
    bias_acc = jnp.zeros((8, width), F32)
    for i in range(rows // TILE):
        at = slice(i * TILE, (i + 1) * TILE)
        gpl = take(gp_scr, padded(i, block_len), 0, 2 * groups).astype(BF16)
        gpl_scr[at, :] = gpl
        gn = nt_dot(gpl, w_full[...]) + skip * gssm_ref[at, :]
        gn_ref[at, :] = gn.astype(BF16)
        n, _ = centre(x_ref[at, :])
        gain_acc = gain_acc + fold_rows(gn * n)
        bias_acc = bias_acc + fold_rows(gn)
    gb_scr[...] = tn_dot(low_ref[...], gpl_scr[...])
    sums4 = [one_row(v) for v in rate_sums]
    rate_grads = []
    for k in range(3):
        rate_grads.append(sum(rates_ref[8 + 3 * c + k : 9 + 3 * c + k, :] * sums4[c] for c in range(4)))
    vec_scr[0:1, :] = one_row(gain_acc)
    vec_scr[1:2, :] = one_row(bias_acc)
    extra = 3 * shard // 2
    half = shard // 2
    for k, dst in enumerate((keep_ref, send_ref, keep_ref, send_ref)):
        slot = (w ^ k) // 2
        q = pl.multiple_of((w ^ k) * shard, shard)
        dst[slot, :shard, :] = gb_scr[pl.ds(q, shard), :width].astype(BF16)
        dst[slot, shard:extra, : width // 2] = gb_scr[pl.ds(q, half), width:].astype(BF16)
        dst[slot, shard:extra, width // 2 :] = gb_scr[pl.ds(q + half, half), width:].astype(BF16)
        mine = [vec_scr[v : v + 1, pl.ds(q, shard)] for v in range(2)] + [jnp.zeros((1, shard), F32)]
        dst[slot, extra:, :] = split_rows([jnp.concatenate(p, axis=1) for p in zip(rate_grads, mine)])


def centre(values):
    x = values.astype(F32)
    c = x - jnp.mean(x, -1, keepdims=True)
    r = lax.rsqrt(jnp.mean(c * c, -1, keepdims=True) + 1e-05)
    return c * r, r


def sum_body(c0, c1, c2, c3, sum_ref):
    sum_ref[...] = total((c0, c1, c2, c3), slice(0, sum_ref.shape[0]))


def quarter_body(w_ref, keep_ref, got_ref, *outs):
    half = outs[0].shape[0] - 16
    x, y = w_ref[0] % 2, w_ref[1] // 2
    for out, slot, side in zip(outs, (y, 1 - y, y, 1 - y), (x, x, 1 - x, 1 - x)):
        def both(rows):
            return keep_ref[slot, rows, :].astype(F32) + got_ref[slot, rows, :].astype(F32)

        out[:half, :] = both(pl.ds(pl.multiple_of(side * half, half), half)).astype(BF16)
        v = both(slice(2 * half, 2 * half + 16))
        out[half:, :] = split_rows([v[:8] + v[8:]])


def total(refs, rows):
    return sum([r[rows, :].astype(F32) for r in refs[1:]], refs[0][rows, :].astype(F32))


def deal_body(w_ref, *refs):
    n = len(refs) - 6
    bs, c_sum, outs, b_scr = refs[:4], refs[4], refs[5 : 5 + n], refs[5 + n]
    b_half, c_half = b_scr.shape[0], c_sum.shape[0] - 16
    b_part, c_part = b_half // n, c_half // n
    b_scr[...] = total(bs, slice(0, b_half))
    tail = total(bs, slice(b_half, b_half + 16)) + c_sum[c_half:, :]
    ends = split_rows([tail[:8] + tail[8:]]).astype(F32)
    for k, out in enumerate(outs):
        at = (w_ref[0] // 2) ^ k
        rows = [
            b_scr[pl.ds(pl.multiple_of(at * b_part, 8), b_part), :],
            c_sum[pl.ds(pl.multiple_of(at * c_part, 8), c_part), :],
            ends[:4], ends[8:12],
        ]
        out[...] = jnp.concatenate(rows, axis=0).astype(BF16)


def close_body(*refs):
    parts, (piece_ref, tail_ref) = refs[:-2], refs[-2:]
    bulk = piece_ref.shape[0]
    v = total(parts, slice(0, bulk + 8))
    piece_ref[...] = v[:bulk].astype(BF16)
    tail_ref[...] = jnp.concatenate([v[bulk : bulk + 4] + v[bulk + 4 :], jnp.zeros((4, v.shape[1]), F32)], axis=0)


def scale_of(tail, tokens):
    return tokens / tail[3:4, 3 * LANES : 3 * LANES + 1]


def finish_body(w_ref, tail_ref, x_ref, gn_ref, gres_ref, vec_ref,
                out_ref, loss_ref, gain_ref, bias_ref, skip_ref, gate_ref, real_ref, imag_ref, step_ref, *, tokens):
    rows, width = x_ref.shape
    states = width - gain_ref.shape[1]
    own = real_ref.shape[1]
    tail = tail_ref[...]
    scale = scale_of(tail, tokens)
    gain = vec_ref[0:1, :]
    for i in range(rows // TILE):
        at = slice(i * TILE, (i + 1) * TILE)
        n, r = centre(x_ref[at, :])
        q = gn_ref[at, :].astype(F32) * gain
        back = (q - jnp.mean(q, -1, keepdims=True) - n * jnp.mean(q * n, -1, keepdims=True)) * r
        out_ref[at, :] = scale * (gres_ref[at, :].astype(F32) + back)
    scaled = tail * scale
    gain_ref[...] = scaled[0:1, states:]
    bias_ref[...] = scaled[1:2, states:]
    skip_ref[...] = scaled[3:4, :LANES]
    gate_ref[...] = scaled[3:4, LANES : 2 * LANES]
    loss_ref[...] = tail[3:4, 2 * LANES : 2 * LANES + 1] * scale * (1.0 / (tokens * width))
    rates = pltpu.roll(scaled[:, :states], states - w_ref[0] * own, 1)
    for k, ref in enumerate((real_ref, imag_ref, step_ref)):
        ref[...] = rates[k : k + 1, :own]


def unpack_body(w_ref, tail_ref, *refs, tokens):
    pieces, (gb_ref, gc_ref, gg_ref, b_scr, c_scr) = refs[:-5], refs[-5:]
    scale = scale_of(tail_ref[...], tokens)
    S = len(pieces)
    b_rows, c_rows = b_scr.shape[0] // S, c_scr.shape[0] // S
    for k, piece in enumerate(pieces):
        s = w_ref[0] ^ k
        v = piece[...].astype(F32) * scale
        b_at = s % 2 * (b_scr.shape[0] // 2) + s // 2 * b_rows
        c_at = s % 2 * (c_scr.shape[0] // 2) + s // 2 * c_rows
        b_scr[pl.ds(pl.multiple_of(b_at, 8), b_rows), :] = v[:b_rows, :]
        c_scr[pl.ds(pl.multiple_of(c_at, 8), c_rows), :] = v[b_rows:, :]
    shard, cols = gb_ref.shape
    width = b_scr.shape[1]
    half = shard // 2
    gb_ref[:, :width] = b_scr[:shard, :]
    gb_ref[:half, width:] = b_scr[shard:, : cols - width]
    gb_ref[half:, width:] = b_scr[shard:, cols - width :]
    gc_ref[...] = c_scr[: gc_ref.shape[0], :]
    gg_ref[...] = c_scr[gc_ref.shape[0] :, :]


def whole(n, smem=(), far=()):
    return [pl.BlockSpec(memory_space=pltpu.SMEM if i in smem else pltpu.HBM if i in far else pltpu.VMEM) for i in range(n)]


def call(body, outs, scratch, smem, *args, us=1, limit=30, far=(), copies=0):
    return pl.pallas_call(
        body,
        out_shape=[jax.ShapeDtypeStruct(*o) for o in outs],
        in_specs=whole(len(args), smem, far),
        out_specs=whole(len(outs)),
        scratch_shapes=[pltpu.VMEM(*s) for s in scratch] + [pltpu.SemaphoreType.DMA((copies,))] * (copies > 0),
        compiler_params=pltpu.CompilerParams(vmem_limit_bytes=limit * MIB),
        cost_estimate=pl.CostEstimate(flops=us * 1_000_000_000, bytes_accessed=MIB, transcendentals=0),
    )(*args)


def per_device(inputs, teacher, segment_ids, valid_mask, ln_gain, ln_bias, b_weight, c_weight, skip_weight,
               glu_weight, glu_bias, lambda_real, lambda_imag, log_step):
    S = lax.axis_size("seq")
    s_at = lax.axis_index("seq")
    w_at = 2 * lax.axis_index("wy") + lax.axis_index("wc")
    seqs, block_len, width = inputs.shape
    rows = seqs * block_len
    padded_rows = PAD + seqs * (block_len + PAD)
    length = S * block_len
    own = lambda_real.shape[0]
    states = own * S
    doc_most = {4096: 1024, 32768: 8192}.get(length, length)
    hops = min((doc_most - 2) // block_len + 1, S - 1)
    shard, c_shard, g_shard = b_weight.shape[0], c_weight.shape[0], glu_weight.shape[0]

    def swap(v, axis, bit=1, n=2):
        return lax.ppermute(v, axis, [(i, i ^ bit) for i in range(n)])

    def after(v, *others):
        return lax.optimization_barrier((v, *others))[0]

    idx = jnp.stack([s_at, w_at]).astype(jnp.int32)
    b_msg, table = call(
        k0_body,
        [((shard + 16, b_weight.shape[1]), BF16), ((8, states), F32)],
        [(b_weight.shape, BF16), ((4, 1, shard), BF16), ((3, 1, own), F32), ((8, states), F32)],
        (0,),
        idx, b_weight, *(v[None] for v in (ln_gain, ln_bias, skip_weight, glu_bias, lambda_real, lambda_imag, log_step)),
        far=range(1, 9), copies=8, limit=60,
    )
    b_far = swap(b_msg, "wy")
    b_near = swap(b_msg, "wc")
    (c_msg,) = call(
        k0b_body,
        [((c_shard + g_shard, width), BF16)],
        [(c_weight.shape, BF16), (glu_weight.shape, BF16)],
        (),
        c_weight, glu_weight, far=range(2), copies=2, limit=4,
    )
    c_far = swap(c_msg, "wy")
    bit = 1
    while bit < S:
        radix = 4 if 4 * bit <= S else 2
        table = sum([swap(table, "seq", k * bit, S) for k in range(1, radix)], table)
        bit *= radix
    bs = (b_msg, b_near, b_far, swap(b_far, "wc"))

    x = inputs.reshape(rows, width)
    teach = teacher.reshape(rows, width)
    R = seqs * CHUNKS
    slab = (2 * states // LANES, padded_rows, LANES)
    msg_shape = ((seqs, 2 * states + LANES), F32)
    low, proj, vec, w_full, s1, fwd, rates, link, valid, ids = call(
        functools.partial(k1_body, seqs=seqs),
        [((rows, width), BF16), (slab, F32), ((8, width), F32), ((width, 2 * states), BF16),
         ((R, 4 * states), F32), msg_shape, ((24, states), F32),
         ((padded_rows, LANES), F32), ((rows, LANES), F32), ((2 * seqs, LANES), F32)],
        [],
        (0,),
        idx, x, *bs, table, segment_ids, valid_mask, us=4, limit=8,
    )
    cs = (c_msg, swap(c_msg, "wc"), c_far, swap(c_far, "wc"))
    fwds = [lax.ppermute(fwd, "seq", [(i, (i + k) % S) for i in range(S)]) for k in range(1, hops + 1)]
    c_bulk = c_shard + g_shard
    out, state, gs, gres, gssm, s2, bwd, send_c, keep_c = call(
        functools.partial(k2_body, seqs=seqs, hops=hops),
        [((rows, width), BF16), (slab, F32), (slab, F32),
         ((rows, width), BF16), ((rows, width), F32), ((R, 4 * states), F32), msg_shape,
         ((2, c_bulk + 16, width), BF16), ((2, c_bulk + 16, width), BF16)],
        [((2 * states, width), BF16), ((width, width), BF16), ((rows, width), BF16), ((rows, width), BF16),
         ((rows, width), BF16), ((rows, 2 * states), BF16), ((2 * states, width), F32), ((width, width), F32),
         ((8, width), F32)],
        (0,),
        idx, x, teach, link, valid, ids, low, proj, s1, rates, vec, *cs, *fwds, us=10, limit=18,
    )
    bwds = [lax.ppermute(bwd, "seq", [((i + k) % S, i) for i in range(S)]) for k in range(1, hops + 1)]
    def cross(v, flip_x, flip_y):
        return lax.ppermute(
            v, ("seq", "wy"), [(2 * a + b, 2 * (a ^ flip_x) + (b ^ flip_y)) for a in range(S) for b in range(2)])

    def quarters(keep, got):
        shape = ((keep.shape[1] - 16) // 2 + 16, width)
        return call(quarter_body, [(shape, BF16)] * 4, [], (0,), idx, keep, got, limit=4)

    def exchange(q):
        return (q[0], cross(q[1], 0, 1), cross(q[2], 1, 0), cross(q[3], 1, 1))

    q_c = quarters(keep_c, swap(send_c, "wc"))
    q_c, bwds = lax.optimization_barrier((q_c, bwds))
    part_c = exchange(q_c)
    b_bulk = 3 * shard // 2
    b_part, c_part = b_bulk // S, c_bulk // S
    gn, send_b, keep_b = call(
        functools.partial(k3_body, seqs=seqs, hops=hops, blocks=S),
        [((rows, width), BF16), ((2, b_bulk + 16, width), BF16), ((2, b_bulk + 16, width), BF16)],
        [(slab, F32), ((rows, 2 * states), BF16), ((width, 2 * states), F32), ((8, width), F32)],
        (0,),
        idx, x, link, ids, low, proj, state, gs, gssm, s2, rates, vec, w_full, *bwds, us=8, limit=14,
    )
    (c_sum,) = call(sum_body, [((c_bulk // 2 + 16, width), F32)], [], (), *part_c, limit=4)
    send_b, c_sum = lax.optimization_barrier((send_b, c_sum))
    part_b = exchange(quarters(keep_b, swap(send_b, "wc")))
    tokens = float(length * seqs * lax.axis_size(("wy", "wc")))
    deal = S // 2
    if b_part % 8 == 0 and c_part % 8 == 0:
        dealt = call(
            deal_body, [((b_part + c_part + 8, width), BF16)] * deal,
            [((b_bulk // 2, width), F32)], (0,), idx, *part_b, c_sum, limit=4,
        )
        parts = [dealt[0]] + [swap(dealt[k], "seq", 2 * k, S) for k in range(1, deal)]
        piece, tail = call(
            close_body, [((b_part + c_part, width), BF16), ((8, width), F32)], [], (), *parts, limit=4,
        )
        pieces = {0: piece}
        for k in range(1, deal):
            pieces[2 * k] = swap(piece, "seq", 2 * k, S)
        for k in range(deal):
            pieces[2 * k + 1] = swap(pieces[2 * k], "seq", 1, S)
        pieces = [pieces[k] for k in range(S)]
    else:
        piece, tail, pieces = sum_by_all_to_all(part_b, c_sum, S, s_at)
    ingrad, loss, *lines = call(
        functools.partial(finish_body, tokens=tokens),
        [((rows, width), F32), ((1, 1), F32)] + [((1, shard), F32)] * 4 + [((1, own), F32)] * 3,
        [], (0,), idx, tail, x, gn, gres, vec, us=3, limit=8,
    )
    gb, gc, gg = call(
        functools.partial(unpack_body, tokens=tokens),
        [((shard, 2 * states), F32), ((c_shard, width), F32), ((g_shard, width), F32)],
        [((b_bulk, width), F32), ((c_bulk, width), F32)],
        (0,),
        idx, tail, *pieces, limit=8,
    )
    gain, bias, skip, gate, real, imag, step = (v[0] for v in lines)
    return (
        out.reshape(inputs.shape), loss[0, 0], ingrad.reshape(inputs.shape), gain, bias, gb, gc, skip, gg, gate,
        real, imag, step,
    )


def sum_by_all_to_all(part_b, v_c, S, s_at):
    v_b = sum([p.astype(F32) for p in part_b[1:]], part_b[0].astype(F32))
    width = v_b.shape[1]
    tail = v_b[-16:-8] + v_b[-8:] + v_c[-16:-8] + v_c[-8:]
    high = lax.reduce_precision(tail, 8, 7)
    ends = jnp.concatenate([high, tail - high], 0).astype(BF16)
    both = jnp.concatenate([v[:-16].astype(BF16).reshape(S // 2, -1, width) for v in (v_b, v_c)], 1)
    bulk = both.shape[1]
    both = jnp.concatenate([both, jnp.broadcast_to(ends[None], (S // 2, 16, width))], 1)
    empty = jnp.zeros_like(both)
    mine = (lax.iota(jnp.int32, S) % 2 == s_at % 2)[:, None, None]
    sent = jnp.where(mine, jnp.stack([both, both], 1).reshape(S, bulk + 16, width), jnp.stack([empty, empty], 1).reshape(S, bulk + 16, width))
    v = jnp.sum(lax.all_to_all(sent, "seq", 0, 0, tiled=True).astype(F32), 0)
    piece, tail = v[:bulk].astype(BF16), v[bulk : bulk + 8] + v[bulk + 8 :]
    back = lax.all_to_all(jnp.broadcast_to(piece[None], (S, bulk, width)), "seq", 0, 0, tiled=True)
    order = lax.iota(jnp.int32, S) ^ s_at
    return piece, tail, [lax.dynamic_index_in_dim(back, order[k], 0, keepdims=False) for k in range(S)]


def solution(mesh):
    sizes = mesh.devices.shape
    fine = Mesh(mesh.devices.reshape(sizes[0], 2, sizes[1] // 2), ("seq", "wy", "wc"))
    w = ("wy", "wc")
    tokens = P(w, "seq", None)
    return jax.shard_map(
        per_device,
        mesh=fine,
        in_specs=(
            tokens, tokens, P(w, "seq"), P(w, "seq"), P(w), P(w), P(w, None), P(w, None), P(w), P(w, None), P(w),
            P("seq"), P("seq"), P("seq"),
        ),
        out_specs=(
            tokens, P(), tokens, P(w), P(w), P(w, None), P(w, None), P(w), P(w, None), P(w),
            P("seq"), P("seq"), P("seq"),
        ),
        check_vma=False,
    )
```

```python
import functools

import jax
import jax.numpy as jnp
from jax import lax
from jax.experimental import pallas as pl
from jax.experimental.pallas import tpu as pltpu
from jax.sharding import Mesh
from jax.sharding import PartitionSpec as P

CHUNKS = 8
LANES = 128
TILE = 512
PAD = 8
MIB = 1024 * 1024
F32 = jnp.float32
BF16 = jnp.bfloat16


def small_expm1(x):
    return x * (1.0 + x / 2 * (1.0 + x / 3 * (1.0 + x / 4 * (1.0 + x / 5 * (1.0 + x / 6)))))


def rates_map(real_rate, imag_rate, log_rate):
    time_step = jnp.exp(log_rate)
    grow_re = real_rate * time_step
    turn_im = imag_rate * time_step
    growth = jnp.exp(grow_re)
    abar_re = growth * jnp.cos(turn_im)
    abar_im = growth * jnp.sin(turn_im)
    half_sine = jnp.sin(0.5 * turn_im)
    numer_re = small_expm1(grow_re) * jnp.cos(turn_im) - 2.0 * half_sine * half_sine
    divisor = real_rate * real_rate + imag_rate * imag_rate
    scale_re = (numer_re * real_rate + abar_im * imag_rate) / divisor
    scale_im = (abar_im * real_rate - numer_re * imag_rate) / divisor
    return (abar_re, abar_im, scale_re, scale_im)


def cmul(xr, xi, yr, yi):
    return xr * yr - xi * yi, xr * yi + xi * yr


def power2(xr, xi, times):
    for _ in range(times):
        xr, xi = xr * xr - xi * xi, 2.0 * xr * xi
    return xr, xi


def log2(n):
    return n.bit_length() - 1


def power(xr, xi, n):
    out = None
    while n:
        if n & 1:
            out = (xr, xi) if out is None else cmul(*out, xr, xi)
        n >>= 1
        if n:
            xr, xi = power2(xr, xi, 1)
    return out


def chunk_powers(ar, ai, steps):
    first = lax.broadcasted_iota(jnp.int32, ar.shape, 0) == 0
    sr, si = power(ar, ai, steps - PAD)
    pr, pi = power(ar, ai, steps)
    return jnp.where(first, sr, pr), jnp.where(first, si, pi)


def padded(i, block_len):
    start = i * TILE + PAD * (2 + i * TILE // block_len)
    return slice(start, start + TILE)


def add_to(ref, i, v):
    ref[...] = v if i == 0 else ref[...] + v


def run(count, body, carry, unroll):
    def block(k, c):
        for u in range(unroll):
            c = body(k * unroll + u, c)
        return c

    whole_blocks = count // unroll
    carry = lax.fori_loop(0, whole_blocks, block, carry)
    for i in range(whole_blocks * unroll, count):
        carry = body(i, carry)
    return carry


def wide(v, groups):
    return jnp.concatenate([v] * groups, axis=1)


def fold_rows(v):
    return jnp.sum(v.reshape(-1, 8, v.shape[-1]), axis=0)


def take(ref, at, first, count):
    return jnp.concatenate([ref[first + g, at, :] for g in range(count)], axis=1)


def put(ref, at, first, v):
    for g in range(v.shape[1] // LANES):
        ref[first + g, at, :] = v[:, g * LANES : (g + 1) * LANES]


def clear_pads(ref, seqs, pitch):
    for g in range(ref.shape[0]):
        ref[g, :PAD, :] = jnp.zeros((PAD, LANES), F32)
        for s in range(seqs):
            ref[g, PAD + s * pitch : 2 * PAD + s * pitch, :] = jnp.zeros((PAD, LANES), F32)


def own_w():
    return 2 * lax.axis_index("wy") + lax.axis_index("wc")


def one_row(v):
    return jnp.sum(v, axis=0, keepdims=True)


def nt_dot(a, b):
    return lax.dot_general(a, b, (((1,), (1,)), ((), ())), preferred_element_type=F32)


def tn_dot(a, b):
    return lax.dot_general(a, b, (((0,), (0,)), ((), ())), preferred_element_type=F32)


def chunk_scan(ar, ai, br, bi, reverse):
    rows = lax.broadcasted_iota(jnp.int32, ar.shape, 0)
    d = 1
    while d < CHUNKS:
        shift = (CHUNKS - d) if reverse else d
        keep = (rows < CHUNKS - d) if reverse else (rows >= d)
        pr, pi = pltpu.roll(ar, shift, 0), pltpu.roll(ai, shift, 0)
        qr, qi = pltpu.roll(br, shift, 0), pltpu.roll(bi, shift, 0)
        mr, mi = cmul(ar, ai, qr, qi)
        br, bi = jnp.where(keep, br + mr, br), jnp.where(keep, bi + mi, bi)
        mr, mi = cmul(ar, ai, pr, pi)
        ar, ai = jnp.where(keep, mr, ar), jnp.where(keep, mi, ai)
        d *= 2
    return ar, ai, br, bi


def carry_in(recvs, ids, s, own_row, ar, ai, block_len, conj, blocks):
    states = ar.shape[1]
    pr, pi = power2(ar, -ai if conj else ai, log2(block_len))
    cr = jnp.zeros((1, states), F32)
    ci = jnp.zeros((1, states), F32)
    own = wide(ids[own_row : own_row + 1, :], states // LANES)
    for k in range(len(recvs), 0, -1):
        msg = recvs[k - 1][s : s + 1, :]
        same = (wide(msg[:, 2 * states :], states // LANES) == own) & (blocks >= k)
        cr, ci = cmul(pr, pi, cr, ci)
        cr = cr + jnp.where(same, msg[:, :states], 0.0)
        ci = ci + jnp.where(same, msg[:, states : 2 * states], 0.0)
    return cr, ci


def fetch(pairs, sems):
    copies = [pltpu.make_async_copy(src, dst, sems.at[k]) for k, (src, dst) in enumerate(pairs)]
    for c in copies:
        c.start()
    for c in copies:
        c.wait()


def k0_body(b_ref, g_ref, n_ref, s_ref, q_ref, lr_ref, li_ref, ls_ref, msg_ref, table_ref,
            b_scr, v_scr, l_scr, scr, sems):
    shard, cols = b_scr.shape
    own = lr_ref.shape[1]
    fetch(
        [(b_ref, b_scr)]
        + [(r, v_scr.at[k]) for k, r in enumerate((g_ref, n_ref, s_ref, q_ref))]
        + [(r, l_scr.at[k]) for k, r in enumerate((lr_ref, li_ref, ls_ref))],
        sems,
    )
    msg_ref[:shard, :] = b_scr[...]
    line = jnp.concatenate([v_scr[k] for k in range(4)] + [jnp.zeros((1, cols - 4 * shard), BF16)], axis=1)
    msg_ref[shard:, :] = jnp.broadcast_to(line, (16, cols))
    scr[...] = jnp.zeros_like(scr)
    for k in range(3):
        scr[k : k + 1, :own] = l_scr[k]
    table_ref[...] = pltpu.roll(scr[...], lax.axis_index("seq") * own, 1)


def k0b_body(c_ref, g_ref, msg_ref, c_scr, g_scr, sems):
    c_shard = c_ref.shape[0]
    fetch([(c_ref, c_scr), (g_ref, g_scr)], sems)
    msg_ref[:c_shard, :] = c_scr[...]
    msg_ref[c_shard:, :] = g_scr[...]


def lay_marks(seg_ref, mask_ref, link_ref, valid_ref, ids_ref):
    seqs, block_len = seg_ref.shape
    seg = seg_ref[...].astype(F32)
    link_ref[:PAD, :] = jnp.ones((PAD, LANES), F32)
    lane = lax.broadcasted_iota(jnp.int32, (1, block_len), 1)
    for s in range(seqs):
        row = seg[s : s + 1, :]
        link = jnp.where((row == pltpu.roll(row, 1, 1)) | (lane == 0), 1.0, 0.0)
        mask = mask_ref[s : s + 1, :].astype(F32)
        start = PAD + s * (block_len + PAD)
        link_ref[start : start + PAD, :] = jnp.ones((PAD, LANES), F32)
        for src, dst, start in ((link, link_ref, start + PAD), (mask, valid_ref, s * block_len)):
            for k in range(block_len // LANES):
                piece = jnp.broadcast_to(src[:, k * LANES : (k + 1) * LANES], (LANES, LANES))
                at = start + k * LANES
                dst[at : at + LANES, :] = jnp.transpose(piece)
        ids_ref[s : s + 1, :] = jnp.broadcast_to(row[:, :1], (1, LANES))
        ids_ref[seqs + s : seqs + s + 1, :] = jnp.broadcast_to(row[:, block_len - 1 :], (1, LANES))


def k1_body(x_ref, b0, b1, b2, b3, table_ref, seg_ref, mask_ref,
            low_ref, proj_ref, vec_ref, full_ref, s1_ref, msg_ref, rates_ref, link_ref, valid_ref, ids_ref, *, seqs):
    rows, width = x_ref.shape
    shard = b0.shape[0] - 16
    block_len = rows // seqs
    pitch = block_len + PAD
    w = own_w()
    for k, piece in enumerate((b0, b1, b2, b3)):
        at = pl.multiple_of((w ^ k) * shard, shard)
        full_ref[pl.ds(at, shard), :] = piece[:shard, :]
        extra = piece[shard:, :].astype(F32)
        for v in range(4):
            vec_ref[v : v + 1, pl.ds(at, shard)] = extra[0:1, v * shard : (v + 1) * shard]
    vec_ref[4:8, :] = jnp.zeros((4, width), F32)
    gain = vec_ref[0:1, :]
    bias = vec_ref[1:2, :]
    for i in range(rows // TILE):
        at = slice(i * TILE, (i + 1) * TILE)
        low = (centre(x_ref[at, :])[0] * gain + bias).astype(BF16)
        low_ref[at, :] = low
        p = jnp.dot(low, full_ref[...], preferred_element_type=F32)
        put(proj_ref, padded(i, block_len), 0, p.astype(BF16).astype(F32))
    clear_pads(proj_ref, seqs, pitch)
    lay_marks(seg_ref, mask_ref, link_ref, valid_ref, ids_ref)
    states = table_ref.shape[1]
    groups = states // LANES
    steps = block_len // CHUNKS + 1
    lam = [table_ref[v : v + 1, :] for v in range(3)]
    parts, back = jax.vjp(rates_map, *lam)
    one, zero = jnp.ones_like(lam[0]), jnp.zeros_like(lam[0])
    for v in range(4):
        rates_ref[v : v + 1, :] = parts[v]
        for k, jac in enumerate(back(tuple(one if i == v else zero for i in range(4)))):
            rates_ref[8 + 3 * v + k : 9 + 3 * v + k, :] = jac
    rates_ref[4:8, :] = jnp.zeros((4, states), F32)
    rates_ref[20:24, :] = jnp.zeros((4, states), F32)
    ar = jnp.broadcast_to(parts[0], (CHUNKS, states))
    ai = jnp.broadcast_to(parts[1], (CHUNKS, states))

    def step(j, carry):
        out = []
        for s in range(seqs):
            ur, ui, q = carry[s]
            at = pl.ds(PAD + s * pitch + j, CHUNKS, stride=steps)
            lk = link_ref[at, :]
            lw = wide(lk, groups)
            nr, ni = cmul(ar, ai, ur, ui)
            out.append((lw * nr + take(proj_ref, at, 0, groups), lw * ni + take(proj_ref, at, groups, groups), q * lk))
        return tuple(out)

    zero = jnp.zeros((CHUNKS, states), F32)
    init = tuple((zero, zero, jnp.ones((CHUNKS, LANES), F32)) for _ in range(seqs))
    ends = run(steps, step, init, 13)
    pr, pi = chunk_powers(ar, ai, steps)
    for s in range(seqs):
        ur, ui, q = ends[s]
        qw = wide(q, groups)
        sc = chunk_scan(pr * qw, pi * qw, ur, ui, False)
        for v in range(4):
            s1_ref[s * CHUNKS : (s + 1) * CHUNKS, v * states : (v + 1) * states] = sc[v]
        msg_ref[s : s + 1, :states] = sc[2][CHUNKS - 1 :, :]
        msg_ref[s : s + 1, states : 2 * states] = sc[3][CHUNKS - 1 :, :]
        msg_ref[s : s + 1, 2 * states :] = ids_ref[seqs + s : seqs + s + 1, :]


def k2_body(*refs, seqs, hops):
    (x_ref, t_ref, link_ref, valid_ref, ids_ref, low_ref, proj_ref, s1_ref, rates_ref, vec_ref,
     c0, c1, c2, c3) = refs[:14]
    recvs = refs[14 : 14 + hops]
    (out_ref, state_ref, gs_ref, gres_ref, gssm_ref, s2_ref, msg_ref, send_ref, keep_ref,
     wc_scr, wg_scr, gc_scr, gg_scr, sum_scr) = refs[14 + hops :]
    rows, width = x_ref.shape
    states = rates_ref.shape[1]
    groups = states // LANES
    block_len = rows // seqs
    steps = block_len // CHUNKS + 1
    pitch = block_len + PAD
    g_shard = width // 4
    c_shard = 2 * states // 4
    w = own_w()
    for k, piece in enumerate((c0, c1, c2, c3)):
        wc_scr[pl.ds(pl.multiple_of((w ^ k) * c_shard, c_shard), c_shard), :] = piece[:c_shard, :]
        wg_scr[pl.ds(pl.multiple_of((w ^ k) * g_shard, g_shard), g_shard), :] = piece[c_shard:, :]
    a1r, a1i = rates_ref[0:1, :], rates_ref[1:2, :]
    ar = jnp.broadcast_to(a1r, (CHUNKS, states))
    ai = jnp.broadcast_to(a1i, (CHUNKS, states))
    zr = jnp.broadcast_to(rates_ref[2:3, :], (CHUNKS, states))
    zi = jnp.broadcast_to(rates_ref[3:4, :], (CHUNKS, states))
    top = lax.broadcasted_iota(jnp.int32, (CHUNKS, states), 0)
    ids = ids_ref[...]
    init, carries = [], []
    for s in range(seqs):
        cr, ci = carry_in(recvs, ids, s, s, a1r, a1i, block_len, False, lax.axis_index("seq"))
        sc = [s1_ref[s * CHUNKS : (s + 1) * CHUNKS, v * states : (v + 1) * states] for v in range(4)]
        mr, mi = cmul(sc[0], sc[1], cr, ci)
        init.append((pltpu.roll(sc[2] + mr, 1, 0), pltpu.roll(sc[3] + mi, 1, 0)))
        carries.append((cr, ci))

    def step(j, carry):
        out = []
        for s in range(seqs):
            ur, ui = carry[s]
            at = pl.ds(PAD + s * pitch + j, CHUNKS, stride=steps)
            lw = wide(link_ref[at, :], groups)
            nr, ni = cmul(ar, ai, ur, ui)
            ur, ui = lw * nr + take(proj_ref, at, 0, groups), lw * ni + take(proj_ref, at, groups, groups)
            sr, si = cmul(zr, zi, ur, ui)
            put(state_ref, at, 0, sr)
            put(state_ref, at, groups, si)
            out.append((ur, ui))
        return tuple(out)

    for g in range(2 * groups):
        state_ref[g, :PAD, :] = jnp.zeros((PAD, LANES), F32)
    entry = list(run(PAD, step, tuple(init), PAD))
    for s in range(seqs):
        ur, ui = (jnp.where(top == 0, c, u) for c, u in zip(carries[s], entry[s]))
        sr, si = cmul(zr, zi, ur, ui)
        at = pl.ds(PAD + s * pitch + PAD - 1, CHUNKS, stride=steps)
        put(state_ref, at, 0, sr)
        put(state_ref, at, groups, si)
        entry[s] = (ur, ui)
    run(steps - PAD, lambda i, c: step(i + PAD, c), tuple(entry), 8)

    skip = vec_ref[2:3, :]
    gbias = 0.5 * vec_ref[3:4, :]
    loss_acc = jnp.zeros((8, width), F32)
    gbias_acc = jnp.zeros((8, width), F32)
    skip_acc = jnp.zeros((8, width), F32)
    for i in range(rows // TILE):
        at = slice(i * TILE, (i + 1) * TILE)
        pad_at = padded(i, block_len)
        sl = take(state_ref, pad_at, 0, 2 * groups).astype(BF16)
        so = jnp.dot(sl, wc_scr[...], preferred_element_type=F32) + skip * low_ref[at, :].astype(F32)
        e = jnp.exp2(so * so * -0.7213475204444817)
        t = 1.0 / (1.0 + 0.23164189 * jnp.abs(so))
        tail = e * t * (0.127414796 + t * (-0.142248368 + t * (0.7107068705 + t * (-0.7265760135 + t * 0.5307027145))))
        phi = jnp.where(so >= 0.0, 1.0 - tail, tail)
        act = (so * phi).astype(BF16)
        dgelu = phi + so * e * 0.3989422804014327
        g = 0.5 * jnp.tanh(0.5 * jnp.dot(act, wg_scr[...], preferred_element_type=F32) + gbias) + 0.5
        gated = act.astype(F32) * g
        res = x_ref[at, :].astype(F32) + gated
        out_ref[at, :] = res.astype(BF16)
        err = res - t_ref[at, :].astype(F32)
        gr = err * wide(valid_ref[at, :], width // LANES)
        loss_acc = loss_acc + fold_rows(gr * err)
        gres_ref[at, :] = gr.astype(BF16)
        gg = gr * gated * (1.0 - g)
        gbias_acc = gbias_acc + fold_rows(gg)
        gl = gg.astype(BF16)
        add_to(gg_scr, i, tn_dot(act, gl))
        gssm = dgelu * (gr * g + nt_dot(gl, wg_scr[...]))
        gssm_ref[at, :] = gssm
        skip_acc = skip_acc + fold_rows(gssm * low_ref[at, :].astype(F32))
        ssl = gssm.astype(BF16)
        put(gs_ref, pad_at, 0, nt_dot(ssl, wc_scr[...]).astype(BF16).astype(F32))
        add_to(gc_scr, i, tn_dot(sl, ssl))
    clear_pads(gs_ref, seqs, pitch)
    sum_scr[0:1, :] = one_row(skip_acc)
    sum_scr[1:2, :] = one_row(gbias_acc)
    loss = jnp.sum(one_row(loss_acc), axis=1, keepdims=True)
    count = one_row(fold_rows(valid_ref[...]))

    def back(i, carry):
        j = steps - 1 - i
        out = []
        for s in range(seqs):
            yr, yi, q = carry[s]
            at = pl.ds(PAD + s * pitch + j, CHUNKS, stride=steps)
            lk = link_ref[at, :]
            lw = wide(lk, groups)
            nr, ni = cmul(ar, -ai, yr, yi)
            out.append((lw * (nr + take(gs_ref, at, 0, groups)), lw * (ni + take(gs_ref, at, groups, groups)), q * lk))
        return tuple(out)

    zero = jnp.zeros((CHUNKS, states), F32)
    init = tuple((zero, zero, jnp.ones((CHUNKS, LANES), F32)) for _ in range(seqs))
    firsts = run(steps - PAD, back, init, 8)
    ends = run(PAD, lambda i, c: back(i + steps - PAD, c), firsts, PAD)
    pr, pi = chunk_powers(ar, -ai, steps)
    for s in range(seqs):
        yr, yi, q = (jnp.where(top[:, : v.shape[1]] == 0, u, v) for u, v in zip(firsts[s], ends[s]))
        qw = wide(q, groups)
        sc = chunk_scan(pr * qw, pi * qw, yr, yi, True)
        for v in range(4):
            s2_ref[s * CHUNKS : (s + 1) * CHUNKS, v * states : (v + 1) * states] = sc[v]
        msg_ref[s : s + 1, :states] = sc[2][:1, :]
        msg_ref[s : s + 1, states : 2 * states] = sc[3][:1, :]
        msg_ref[s : s + 1, 2 * states :] = ids_ref[s : s + 1, :]

    for k, dst in enumerate((keep_ref, send_ref, keep_ref, send_ref)):
        q = w ^ k
        slot = q // 2
        dst[slot, :c_shard, :] = gc_scr[pl.ds(pl.multiple_of(q * c_shard, c_shard), c_shard), :].astype(BF16)
        lanes = pl.multiple_of(q * g_shard, g_shard)
        dst[slot, c_shard : c_shard + g_shard, :] = gg_scr[pl.ds(lanes, g_shard), :].astype(BF16)
        line = jnp.concatenate(
            [sum_scr[v : v + 1, pl.ds(lanes, g_shard)] for v in range(2)]
            + [jnp.broadcast_to(loss, (1, LANES)), count], axis=1)
        dst[slot, c_shard + g_shard :, :] = split_rows([jnp.zeros((3, width), F32), line])


def split16(v):
    high = v.astype(BF16)
    return high, (v - high.astype(F32)).astype(BF16)


def split_rows(lines):
    width = lines[0].shape[1]
    rows = sum(v.shape[0] for v in lines)
    v = jnp.concatenate(lines + [jnp.zeros((8 - rows, width), F32)] * (rows < 8), axis=0)
    high, rest = split16(v)
    return jnp.concatenate([high.astype(F32), rest.astype(F32)], axis=0).astype(BF16)


def k3_body(*refs, seqs, hops, blocks):
    (x_ref, link_ref, ids_ref, low_ref, proj_ref, state_ref, gs_ref, gssm_ref,
     s2_ref, rates_ref, vec_ref, w_full) = refs[:12]
    recvs = refs[12 : 12 + hops]
    (gn_ref, send_ref, keep_ref, gp_scr, gpl_scr, gb_scr, vec_scr) = refs[12 + hops :]
    rows, width = x_ref.shape
    states = rates_ref.shape[1]
    groups = states // LANES
    block_len = rows // seqs
    steps = block_len // CHUNKS + 1
    pitch = block_len + PAD
    shard = width // 4
    w = own_w()
    a1r, a1i = rates_ref[0:1, :], rates_ref[1:2, :]
    ar = jnp.broadcast_to(a1r, (CHUNKS, states))
    ai = jnp.broadcast_to(a1i, (CHUNKS, states))
    zr = jnp.broadcast_to(rates_ref[2:3, :], (CHUNKS, states))
    zi = jnp.broadcast_to(rates_ref[3:4, :], (CHUNKS, states))
    rowid = lax.broadcasted_iota(jnp.int32, (CHUNKS, states), 0)
    ids = ids_ref[...]
    rate_sums = [jnp.zeros((CHUNKS, states), F32) for _ in range(4)]
    for s in range(seqs):
        cr, ci = carry_in(recvs, ids, s, seqs + s, a1r, a1i, block_len, True, blocks - 1 - lax.axis_index("seq"))
        sc = [s2_ref[s * CHUNKS : (s + 1) * CHUNKS, v * states : (v + 1) * states] for v in range(4)]
        mr, mi = cmul(sc[0], sc[1], cr, ci)
        yr = jnp.where(rowid == CHUNKS - 1, cr, pltpu.roll(sc[2] + mr, CHUNKS - 1, 0))
        yi = jnp.where(rowid == CHUNKS - 1, ci, pltpu.roll(sc[3] + mi, CHUNKS - 1, 0))

        def step(i, carry):
            yr, yi, gar, gai, gsr, gsi = carry
            j = steps - 1 - i
            at = pl.ds(PAD + s * pitch + j, CHUNKS, stride=steps)
            before = pl.ds(PAD + s * pitch + j - 1, CHUNKS, stride=steps)
            lw = wide(link_ref[at, :], groups)
            nr, ni = cmul(ar, -ai, yr, yi)
            dr, di = nr + take(gs_ref, at, 0, groups), ni + take(gs_ref, at, groups, groups)
            yr, yi = lw * dr, lw * di
            pr, pi = take(proj_ref, at, 0, groups), take(proj_ref, at, groups, groups)
            ur, ui = take(state_ref, before, 0, groups), take(state_ref, before, groups, groups)
            put(gp_scr, at, 0, zr * dr + zi * di)
            put(gp_scr, at, groups, zr * di - zi * dr)
            return (
                yr, yi,
                gar + (ur * yr + ui * yi), gai + (ur * yi - ui * yr),
                gsr + (pr * dr + pi * di), gsi + (pr * di - pi * dr),
            )

        carry = run(steps - PAD, step, (yr, yi, *rate_sums), 8)
        yr, yi = (jnp.where(rowid == 0, 0.0, v) for v in carry[:2])
        carry = run(PAD, lambda i, c: step(i + steps - PAD, c), (yr, yi, *carry[2:]), PAD)
        rate_sums = list(carry[2:])

    skip = vec_ref[2:3, :]
    gain_acc = jnp.zeros((8, width), F32)
    bias_acc = jnp.zeros((8, width), F32)
    for i in range(rows // TILE):
        at = slice(i * TILE, (i + 1) * TILE)
        gpl = take(gp_scr, padded(i, block_len), 0, 2 * groups).astype(BF16)
        gpl_scr[at, :] = gpl
        gn = nt_dot(gpl, w_full[...]) + skip * gssm_ref[at, :]
        gn_ref[at, :] = gn.astype(BF16)
        n, _ = centre(x_ref[at, :])
        gain_acc = gain_acc + fold_rows(gn * n)
        bias_acc = bias_acc + fold_rows(gn)
    gb_scr[...] = tn_dot(low_ref[...], gpl_scr[...])
    sums4 = [one_row(v) for v in rate_sums]
    rate_grads = []
    for k in range(3):
        rate_grads.append(sum(rates_ref[8 + 3 * c + k : 9 + 3 * c + k, :] * sums4[c] for c in range(4)))
    vec_scr[0:1, :] = one_row(gain_acc)
    vec_scr[1:2, :] = one_row(bias_acc)
    extra = 3 * shard // 2
    half = shard // 2
    for k, dst in enumerate((keep_ref, send_ref, keep_ref, send_ref)):
        slot = (w ^ k) // 2
        q = pl.multiple_of((w ^ k) * shard, shard)
        dst[slot, :shard, :] = gb_scr[pl.ds(q, shard), :width].astype(BF16)
        dst[slot, shard:extra, : width // 2] = gb_scr[pl.ds(q, half), width:].astype(BF16)
        dst[slot, shard:extra, width // 2 :] = gb_scr[pl.ds(q + half, half), width:].astype(BF16)
        mine = [vec_scr[v : v + 1, pl.ds(q, shard)] for v in range(2)] + [jnp.zeros((1, shard), F32)]
        dst[slot, extra:, :] = split_rows([jnp.concatenate(p, axis=1) for p in zip(rate_grads, mine)])


def centre(values):
    x = values.astype(F32)
    c = x - jnp.mean(x, -1, keepdims=True)
    r = lax.rsqrt(jnp.mean(c * c, -1, keepdims=True) + 1e-05)
    return c * r, r


def sum_body(c0, c1, c2, c3, sum_ref):
    sum_ref[...] = total((c0, c1, c2, c3), slice(0, sum_ref.shape[0]))


def quarter_body(keep_ref, got_ref, *outs):
    half = outs[0].shape[0] - 16
    x, y = lax.axis_index("seq") % 2, lax.axis_index("wy")
    for out, slot, side in zip(outs, (y, 1 - y, y, 1 - y), (x, x, 1 - x, 1 - x)):
        def both(rows):
            return keep_ref[slot, rows, :].astype(F32) + got_ref[slot, rows, :].astype(F32)

        out[:half, :] = both(pl.ds(pl.multiple_of(side * half, half), half)).astype(BF16)
        v = both(slice(2 * half, 2 * half + 16))
        out[half:, :] = split_rows([v[:8] + v[8:]])


def total(refs, rows):
    return sum([r[rows, :].astype(F32) for r in refs[1:]], refs[0][rows, :].astype(F32))


def deal_body(*refs):
    n = len(refs) - 6
    bs, c_sum, outs, b_scr = refs[:4], refs[4], refs[5 : 5 + n], refs[5 + n]
    b_half, c_half = b_scr.shape[0], c_sum.shape[0] - 16
    b_part, c_part = b_half // n, c_half // n
    b_scr[...] = total(bs, slice(0, b_half))
    tail = total(bs, slice(b_half, b_half + 16)) + c_sum[c_half:, :]
    ends = split_rows([tail[:8] + tail[8:]]).astype(F32)
    for k, out in enumerate(outs):
        at = (lax.axis_index("seq") // 2) ^ k
        rows = [
            b_scr[pl.ds(pl.multiple_of(at * b_part, 8), b_part), :],
            c_sum[pl.ds(pl.multiple_of(at * c_part, 8), c_part), :],
            ends[:4], ends[8:12],
        ]
        out[...] = jnp.concatenate(rows, axis=0).astype(BF16)


def close_body(*refs):
    parts, (piece_ref, tail_ref) = refs[:-2], refs[-2:]
    bulk = piece_ref.shape[0]
    v = total(parts, slice(0, bulk + 8))
    piece_ref[...] = v[:bulk].astype(BF16)
    tail_ref[...] = jnp.concatenate([v[bulk : bulk + 4] + v[bulk + 4 :], jnp.zeros((4, v.shape[1]), F32)], axis=0)


def scale_of(tail, tokens):
    return tokens / tail[3:4, 3 * LANES : 3 * LANES + 1]


def norm_body(x_ref, gn_ref, gres_ref, vec_ref, ig_ref):
    gain = vec_ref[0:1, :]
    for i in range(x_ref.shape[0] // TILE):
        at = slice(i * TILE, (i + 1) * TILE)
        n, r = centre(x_ref[at, :])
        q = gn_ref[at, :].astype(F32) * gain
        back = (q - jnp.mean(q, -1, keepdims=True) - n * jnp.mean(q * n, -1, keepdims=True)) * r
        ig_ref[at, :] = (gres_ref[at, :].astype(F32) + back).astype(BF16)


def finish_body(tail_ref, ig_ref,
                out_ref, loss_ref, gain_ref, bias_ref, skip_ref, gate_ref, real_ref, imag_ref, step_ref, *, tokens):
    width = ig_ref.shape[1]
    states = width - gain_ref.shape[1]
    own = real_ref.shape[1]
    tail = tail_ref[...]
    scale = scale_of(tail, tokens)
    out_ref[...] = scale * ig_ref[...].astype(F32)
    scaled = tail * scale
    gain_ref[...] = scaled[0:1, states:]
    bias_ref[...] = scaled[1:2, states:]
    skip_ref[...] = scaled[3:4, :LANES]
    gate_ref[...] = scaled[3:4, LANES : 2 * LANES]
    loss_ref[...] = tail[3:4, 2 * LANES : 2 * LANES + 1] * scale * (1.0 / (tokens * width))
    rates = pltpu.roll(scaled[:, :states], states - lax.axis_index("seq") * own, 1)
    for k, ref in enumerate((real_ref, imag_ref, step_ref)):
        ref[...] = rates[k : k + 1, :own]


def unpack_body(tail_ref, *refs, tokens):
    pieces, (gb_ref, gc_ref, gg_ref, b_scr, c_scr) = refs[:-5], refs[-5:]
    scale = scale_of(tail_ref[...], tokens)
    S = len(pieces)
    b_rows, c_rows = b_scr.shape[0] // S, c_scr.shape[0] // S
    for k, piece in enumerate(pieces):
        s = lax.axis_index("seq") ^ k
        v = piece[...].astype(F32) * scale
        b_at = s % 2 * (b_scr.shape[0] // 2) + s // 2 * b_rows
        c_at = s % 2 * (c_scr.shape[0] // 2) + s // 2 * c_rows
        b_scr[pl.ds(pl.multiple_of(b_at, 8), b_rows), :] = v[:b_rows, :]
        c_scr[pl.ds(pl.multiple_of(c_at, 8), c_rows), :] = v[b_rows:, :]
    shard, cols = gb_ref.shape
    width = b_scr.shape[1]
    half = shard // 2
    gb_ref[:, :width] = b_scr[:shard, :]
    gb_ref[:half, width:] = b_scr[shard:, : cols - width]
    gb_ref[half:, width:] = b_scr[shard:, cols - width :]
    gc_ref[...] = c_scr[: gc_ref.shape[0], :]
    gg_ref[...] = c_scr[gc_ref.shape[0] :, :]


def whole(n, far=()):
    return [pl.BlockSpec(memory_space=pltpu.HBM if i in far else pltpu.VMEM) for i in range(n)]


def call(body, outs, scratch, *args, us=1, limit=30, far=(), copies=0):
    return pl.pallas_call(
        body,
        out_shape=[jax.ShapeDtypeStruct(*o) for o in outs],
        in_specs=whole(len(args), far),
        out_specs=whole(len(outs)),
        scratch_shapes=[pltpu.VMEM(*s) for s in scratch] + [pltpu.SemaphoreType.DMA((copies,))] * (copies > 0),
        compiler_params=pltpu.CompilerParams(vmem_limit_bytes=limit * MIB),
        cost_estimate=pl.CostEstimate(flops=us * 1_000_000_000, bytes_accessed=MIB, transcendentals=0),
    )(*args)


def per_device(inputs, teacher, segment_ids, valid_mask, ln_gain, ln_bias, b_weight, c_weight, skip_weight,
               glu_weight, glu_bias, lambda_real, lambda_imag, log_step):
    S = lax.axis_size("seq")
    s_at = lax.axis_index("seq")
    seqs, block_len, width = inputs.shape
    rows = seqs * block_len
    padded_rows = PAD + seqs * (block_len + PAD)
    length = S * block_len
    own = lambda_real.shape[0]
    states = own * S
    doc_most = {4096: 1024, 32768: 8192}.get(length, length)
    hops = min((doc_most - 2) // block_len + 1, S - 1)
    shard, c_shard, g_shard = b_weight.shape[0], c_weight.shape[0], glu_weight.shape[0]

    def swap(v, axis, bit=1, n=2):
        return lax.ppermute(v, axis, [(i, i ^ bit) for i in range(n)])

    def after(v, *others):
        return lax.optimization_barrier((v, *others))[0]

    b_msg, table = call(
        k0_body,
        [((shard + 16, b_weight.shape[1]), BF16), ((8, states), F32)],
        [(b_weight.shape, BF16), ((4, 1, shard), BF16), ((3, 1, own), F32), ((8, states), F32)],
        b_weight, *(v[None] for v in (ln_gain, ln_bias, skip_weight, glu_bias, lambda_real, lambda_imag, log_step)),
        far=range(8), copies=8, limit=60,
    )
    b_far = swap(b_msg, "wy")
    b_near = swap(b_msg, "wc")
    (c_msg,) = call(
        k0b_body,
        [((c_shard + g_shard, width), BF16)],
        [(c_weight.shape, BF16), (glu_weight.shape, BF16)],
        c_weight, glu_weight, far=range(2), copies=2, limit=4,
    )
    c_far = swap(after(c_msg, b_far), "wy")
    bit = 1
    while bit < S:
        radix = 4 if 4 * bit <= S else 2
        table = sum([swap(table, "seq", k * bit, S) for k in range(1, radix)], table)
        bit *= radix
    bs = (b_msg, b_near, b_far, swap(b_far, "wc"))

    x = inputs.reshape(rows, width)
    teach = teacher.reshape(rows, width)
    R = seqs * CHUNKS
    slab = (2 * states // LANES, padded_rows, LANES)
    msg_shape = ((seqs, 2 * states + LANES), F32)
    low, proj, vec, w_full, s1, fwd, rates, link, valid, ids = call(
        functools.partial(k1_body, seqs=seqs),
        [((rows, width), BF16), (slab, F32), ((8, width), F32), ((width, 2 * states), BF16),
         ((R, 4 * states), F32), msg_shape, ((24, states), F32),
         ((padded_rows, LANES), F32), ((rows, LANES), F32), ((2 * seqs, LANES), F32)],
        [],
        x, *bs, table, segment_ids, valid_mask, us=2, limit=8,
    )
    cs = (c_msg, swap(c_msg, "wc"), c_far, swap(after(c_far, fwd), "wc"))
    fwds = [lax.ppermute(fwd, "seq", [(i, (i + k) % S) for i in range(S)]) for k in range(1, hops + 1)]
    c_bulk = c_shard + g_shard
    out, state, gs, gres, gssm, s2, bwd, send_c, keep_c = call(
        functools.partial(k2_body, seqs=seqs, hops=hops),
        [((rows, width), BF16), (slab, F32), (slab, F32),
         ((rows, width), BF16), ((rows, width), F32), ((R, 4 * states), F32), msg_shape,
         ((2, c_bulk + 16, width), BF16), ((2, c_bulk + 16, width), BF16)],
        [((2 * states, width), BF16), ((width, width), BF16), ((2 * states, width), F32), ((width, width), F32),
         ((8, width), F32)],
        x, teach, link, valid, ids, low, proj, s1, rates, vec, *cs, *fwds, us=10, limit=18,
    )
    bwds = [lax.ppermute(bwd, "seq", [((i + k) % S, i) for i in range(S)]) for k in range(1, hops + 1)]
    def cross(v, flip_x, flip_y):
        return lax.ppermute(
            v, ("seq", "wy"), [(2 * a + b, 2 * (a ^ flip_x) + (b ^ flip_y)) for a in range(S) for b in range(2)])

    def quarters(keep, got):
        shape = ((keep.shape[1] - 16) // 2 + 16, width)
        return call(quarter_body, [(shape, BF16)] * 4, [], keep, got, limit=4)

    def exchange(q):
        return (q[0], cross(q[1], 0, 1), cross(q[2], 1, 0), cross(q[3], 1, 1))

    q_c = quarters(keep_c, swap(send_c, "wc"))
    bwds = lax.optimization_barrier((bwds, q_c))[0]
    part_c = exchange(q_c)
    b_bulk = 3 * shard // 2
    b_part, c_part = b_bulk // S, c_bulk // S
    gn, send_b, keep_b = call(
        functools.partial(k3_body, seqs=seqs, hops=hops, blocks=S),
        [((rows, width), BF16), ((2, b_bulk + 16, width), BF16), ((2, b_bulk + 16, width), BF16)],
        [(slab, F32), ((rows, 2 * states), BF16), ((width, 2 * states), F32), ((8, width), F32)],
        x, link, ids, low, proj, state, gs, gssm, s2, rates, vec, w_full, *bwds, us=8, limit=14,
    )
    (c_sum,) = call(sum_body, [((c_bulk // 2 + 16, width), F32)], [], *part_c, limit=4)
    send_b, c_sum = lax.optimization_barrier((send_b, c_sum))
    part_b = exchange(quarters(keep_b, swap(send_b, "wc")))
    (ig,) = call(norm_body, [((rows, width), BF16)], [], x, gn, gres, vec, us=3, limit=8)
    part_b, ig = lax.optimization_barrier((part_b, ig))
    tokens = float(length * seqs * lax.axis_size(("wy", "wc")))
    deal = S // 2
    if b_part % 8 == 0 and c_part % 8 == 0:
        dealt = call(
            deal_body, [((b_part + c_part + 8, width), BF16)] * deal,
            [((b_bulk // 2, width), F32)], *part_b, c_sum, limit=4,
        )
        parts = [dealt[0]] + [swap(dealt[k], "seq", 2 * k, S) for k in range(1, deal)]
        piece, tail = call(
            close_body, [((b_part + c_part, width), BF16), ((8, width), F32)], [], *parts, limit=4,
        )
        pieces = {0: piece}
        for k in range(1, deal):
            pieces[2 * k] = swap(piece, "seq", 2 * k, S)
        for k in range(deal):
            pieces[2 * k + 1] = swap(pieces[2 * k], "seq", 1, S)
        pieces = [pieces[k] for k in range(S)]
    else:
        piece, tail, pieces = sum_by_all_to_all(part_b, c_sum, S, s_at)
    ingrad, loss, *lines = call(
        functools.partial(finish_body, tokens=tokens),
        [((rows, width), F32), ((1, 1), F32)] + [((1, shard), F32)] * 4 + [((1, own), F32)] * 3,
        [], tail, ig, limit=8,
    )
    gb, gc, gg = call(
        functools.partial(unpack_body, tokens=tokens),
        [((shard, 2 * states), F32), ((c_shard, width), F32), ((g_shard, width), F32)],
        [((b_bulk, width), F32), ((c_bulk, width), F32)],
        tail, *pieces, limit=8,
    )
    gain, bias, skip, gate, real, imag, step = (v[0] for v in lines)
    return (
        out.reshape(inputs.shape), loss[0, 0], ingrad.reshape(inputs.shape), gain, bias, gb, gc, skip, gg, gate,
        real, imag, step,
    )


def sum_by_all_to_all(part_b, v_c, S, s_at):
    v_b = sum([p.astype(F32) for p in part_b[1:]], part_b[0].astype(F32))
    width = v_b.shape[1]
    tail = v_b[-16:-8] + v_b[-8:] + v_c[-16:-8] + v_c[-8:]
    high = lax.reduce_precision(tail, 8, 7)
    ends = jnp.concatenate([high, tail - high], 0).astype(BF16)
    both = jnp.concatenate([v[:-16].astype(BF16).reshape(S // 2, -1, width) for v in (v_b, v_c)], 1)
    bulk = both.shape[1]
    both = jnp.concatenate([both, jnp.broadcast_to(ends[None], (S // 2, 16, width))], 1)
    empty = jnp.zeros_like(both)
    mine = (lax.iota(jnp.int32, S) % 2 == s_at % 2)[:, None, None]
    sent = jnp.where(mine, jnp.stack([both, both], 1).reshape(S, bulk + 16, width), jnp.stack([empty, empty], 1).reshape(S, bulk + 16, width))
    v = jnp.sum(lax.all_to_all(sent, "seq", 0, 0, tiled=True).astype(F32), 0)
    piece, tail = v[:bulk].astype(BF16), v[bulk : bulk + 8] + v[bulk + 8 :]
    back = lax.all_to_all(jnp.broadcast_to(piece[None], (S, bulk, width)), "seq", 0, 0, tiled=True)
    order = lax.iota(jnp.int32, S) ^ s_at
    return piece, tail, [lax.dynamic_index_in_dim(back, order[k], 0, keepdims=False) for k in range(S)]


def solution(mesh):
    sizes = mesh.devices.shape
    fine = Mesh(mesh.devices.reshape(sizes[0], 2, sizes[1] // 2), ("seq", "wy", "wc"))
    w = ("wy", "wc")
    tokens = P(w, "seq", None)
    return jax.shard_map(
        per_device,
        mesh=fine,
        in_specs=(
            tokens, tokens, P(w, "seq"), P(w, "seq"), P(w), P(w), P(w, None), P(w, None), P(w), P(w, None), P(w),
            P("seq"), P("seq"), P("seq"),
        ),
        out_specs=(
            tokens, P(), tokens, P(w), P(w), P(w, None), P(w, None), P(w), P(w, None), P(w),
            P("seq"), P("seq"), P("seq"),
        ),
        check_vma=False,
    )
```

```python
import functools

import jax
import jax.numpy as jnp
from jax import lax
from jax.experimental import pallas as pl
from jax.experimental.pallas import tpu as pltpu
from jax.sharding import Mesh
from jax.sharding import PartitionSpec as P

CHUNKS = 8
LANES = 128
TILE = 512
PAD = 8
MIB = 1024 * 1024
F32 = jnp.float32
BF16 = jnp.bfloat16


def small_expm1(x):
    return x * (1.0 + x / 2 * (1.0 + x / 3 * (1.0 + x / 4 * (1.0 + x / 5 * (1.0 + x / 6)))))


def rates_map(real_rate, imag_rate, log_rate):
    time_step = jnp.exp(log_rate)
    grow_re = real_rate * time_step
    turn_im = imag_rate * time_step
    growth = jnp.exp(grow_re)
    abar_re = growth * jnp.cos(turn_im)
    abar_im = growth * jnp.sin(turn_im)
    half_sine = jnp.sin(0.5 * turn_im)
    numer_re = small_expm1(grow_re) * jnp.cos(turn_im) - 2.0 * half_sine * half_sine
    divisor = real_rate * real_rate + imag_rate * imag_rate
    scale_re = (numer_re * real_rate + abar_im * imag_rate) / divisor
    scale_im = (abar_im * real_rate - numer_re * imag_rate) / divisor
    return (abar_re, abar_im, scale_re, scale_im)


def cmul(xr, xi, yr, yi):
    return xr * yr - xi * yi, xr * yi + xi * yr


def power2(xr, xi, times):
    for _ in range(times):
        xr, xi = xr * xr - xi * xi, 2.0 * xr * xi
    return xr, xi


def log2(n):
    return n.bit_length() - 1


def power(xr, xi, n):
    out = None
    while n:
        if n & 1:
            out = (xr, xi) if out is None else cmul(*out, xr, xi)
        n >>= 1
        if n:
            xr, xi = power2(xr, xi, 1)
    return out


def chunk_powers(ar, ai, steps):
    first = lax.broadcasted_iota(jnp.int32, ar.shape, 0) == 0
    sr, si = power(ar, ai, steps - PAD)
    pr, pi = power(ar, ai, steps)
    return jnp.where(first, sr, pr), jnp.where(first, si, pi)


def padded(i, block_len):
    start = i * TILE + PAD * (2 + i * TILE // block_len)
    return slice(start, start + TILE)


def add_to(ref, i, v):
    ref[...] = v if i == 0 else ref[...] + v


def run(count, body, carry, unroll):
    def block(k, c):
        for u in range(unroll):
            c = body(k * unroll + u, c)
        return c

    whole_blocks = count // unroll
    carry = lax.fori_loop(0, whole_blocks, block, carry)
    for i in range(whole_blocks * unroll, count):
        carry = body(i, carry)
    return carry


def wide(v, groups):
    return jnp.concatenate([v] * groups, axis=1)


def fold_rows(v):
    return jnp.sum(v.reshape(-1, 8, v.shape[-1]), axis=0)


def take(ref, at, first, count):
    return jnp.concatenate([ref[first + g, at, :] for g in range(count)], axis=1)


def put(ref, at, first, v):
    for g in range(v.shape[1] // LANES):
        ref[first + g, at, :] = v[:, g * LANES : (g + 1) * LANES]


def clear_pads(ref, seqs, pitch):
    for g in range(ref.shape[0]):
        ref[g, :PAD, :] = jnp.zeros((PAD, LANES), F32)
        for s in range(seqs):
            ref[g, PAD + s * pitch : 2 * PAD + s * pitch, :] = jnp.zeros((PAD, LANES), F32)


def own_w():
    return 2 * lax.axis_index("wy") + lax.axis_index("wc")


def one_row(v):
    return jnp.sum(v, axis=0, keepdims=True)


def nt_dot(a, b):
    return lax.dot_general(a, b, (((1,), (1,)), ((), ())), preferred_element_type=F32)


def tn_dot(a, b):
    return lax.dot_general(a, b, (((0,), (0,)), ((), ())), preferred_element_type=F32)


def chunk_scan(ar, ai, br, bi, reverse):
    rows = lax.broadcasted_iota(jnp.int32, ar.shape, 0)
    d = 1
    while d < CHUNKS:
        shift = (CHUNKS - d) if reverse else d
        keep = (rows < CHUNKS - d) if reverse else (rows >= d)
        pr, pi = pltpu.roll(ar, shift, 0), pltpu.roll(ai, shift, 0)
        qr, qi = pltpu.roll(br, shift, 0), pltpu.roll(bi, shift, 0)
        mr, mi = cmul(ar, ai, qr, qi)
        br, bi = jnp.where(keep, br + mr, br), jnp.where(keep, bi + mi, bi)
        mr, mi = cmul(ar, ai, pr, pi)
        ar, ai = jnp.where(keep, mr, ar), jnp.where(keep, mi, ai)
        d *= 2
    return ar, ai, br, bi


def carry_in(recvs, ids, s, own_row, ar, ai, block_len, conj, blocks):
    states = ar.shape[1]
    pr, pi = power2(ar, -ai if conj else ai, log2(block_len))
    cr = jnp.zeros((1, states), F32)
    ci = jnp.zeros((1, states), F32)
    own = wide(ids[own_row : own_row + 1, :], states // LANES)
    for k in range(len(recvs), 0, -1):
        msg = recvs[k - 1][s : s + 1, :]
        same = (wide(msg[:, 2 * states :], states // LANES) == own) & (blocks >= k)
        cr, ci = cmul(pr, pi, cr, ci)
        cr = cr + jnp.where(same, msg[:, :states], 0.0)
        ci = ci + jnp.where(same, msg[:, states : 2 * states], 0.0)
    return cr, ci


def fetch(pairs, sems):
    copies = [pltpu.make_async_copy(src, dst, sems.at[k]) for k, (src, dst) in enumerate(pairs)]
    for c in copies:
        c.start()
    for c in copies:
        c.wait()


def k0_body(b_ref, g_ref, n_ref, s_ref, q_ref, lr_ref, li_ref, ls_ref, msg_ref, table_ref,
            b_scr, v_scr, l_scr, scr, sems):
    shard, cols = b_scr.shape
    own = lr_ref.shape[1]
    fetch(
        [(b_ref, b_scr)]
        + [(r, v_scr.at[k]) for k, r in enumerate((g_ref, n_ref, s_ref, q_ref))]
        + [(r, l_scr.at[k]) for k, r in enumerate((lr_ref, li_ref, ls_ref))],
        sems,
    )
    msg_ref[:shard, :] = b_scr[...]
    line = jnp.concatenate([v_scr[k] for k in range(4)] + [jnp.zeros((1, cols - 4 * shard), BF16)], axis=1)
    msg_ref[shard:, :] = jnp.broadcast_to(line, (16, cols))
    scr[...] = jnp.zeros_like(scr)
    for k in range(3):
        scr[k : k + 1, :own] = l_scr[k]
    table_ref[...] = pltpu.roll(scr[...], lax.axis_index("seq") * own, 1)


def k0b_body(c_ref, g_ref, msg_ref, c_scr, g_scr, sems):
    c_shard = c_ref.shape[0]
    fetch([(c_ref, c_scr), (g_ref, g_scr)], sems)
    msg_ref[:c_shard, :] = c_scr[...]
    msg_ref[c_shard:, :] = g_scr[...]


def lay_marks(seg_ref, mask_ref, link_ref, valid_ref, ids_ref):
    seqs, block_len = seg_ref.shape
    seg = seg_ref[...].astype(F32)
    link_ref[:PAD, :] = jnp.ones((PAD, LANES), F32)
    lane = lax.broadcasted_iota(jnp.int32, (1, block_len), 1)
    for s in range(seqs):
        row = seg[s : s + 1, :]
        link = jnp.where((row == pltpu.roll(row, 1, 1)) | (lane == 0), 1.0, 0.0)
        mask = mask_ref[s : s + 1, :].astype(F32)
        start = PAD + s * (block_len + PAD)
        link_ref[start : start + PAD, :] = jnp.ones((PAD, LANES), F32)
        for src, dst, start in ((link, link_ref, start + PAD), (mask, valid_ref, s * block_len)):
            for k in range(block_len // LANES):
                piece = jnp.broadcast_to(src[:, k * LANES : (k + 1) * LANES], (LANES, LANES))
                at = start + k * LANES
                dst[at : at + LANES, :] = jnp.transpose(piece)
        ids_ref[s : s + 1, :] = jnp.broadcast_to(row[:, :1], (1, LANES))
        ids_ref[seqs + s : seqs + s + 1, :] = jnp.broadcast_to(row[:, block_len - 1 :], (1, LANES))


def k1_body(x_ref, b0, b1, b2, b3, table_ref, seg_ref, mask_ref,
            low_ref, n_ref, proj_ref, vec_ref, full_ref, s1_ref, msg_ref, rates_ref, link_ref, valid_ref, ids_ref, *, seqs):
    rows, width = x_ref.shape
    shard = b0.shape[0] - 16
    block_len = rows // seqs
    pitch = block_len + PAD
    w = own_w()
    for k, piece in enumerate((b0, b1, b2, b3)):
        at = pl.multiple_of((w ^ k) * shard, shard)
        full_ref[pl.ds(at, shard), :] = piece[:shard, :]
        extra = piece[shard:, :].astype(F32)
        for v in range(4):
            vec_ref[v : v + 1, pl.ds(at, shard)] = extra[0:1, v * shard : (v + 1) * shard]
    vec_ref[4:8, :] = jnp.zeros((4, width), F32)
    gain = vec_ref[0:1, :]
    bias = vec_ref[1:2, :]
    for i in range(rows // TILE):
        at = slice(i * TILE, (i + 1) * TILE)
        n = centre(x_ref[at, :])[0]
        n_ref[at, :] = n.astype(BF16)
        low = (n * gain + bias).astype(BF16)
        low_ref[at, :] = low
        p = jnp.dot(low, full_ref[...], preferred_element_type=F32)
        put(proj_ref, padded(i, block_len), 0, p.astype(BF16).astype(F32))
    clear_pads(proj_ref, seqs, pitch)
    lay_marks(seg_ref, mask_ref, link_ref, valid_ref, ids_ref)
    states = table_ref.shape[1]
    groups = states // LANES
    steps = block_len // CHUNKS + 1
    lam = [table_ref[v : v + 1, :] for v in range(3)]
    parts, back = jax.vjp(rates_map, *lam)
    one, zero = jnp.ones_like(lam[0]), jnp.zeros_like(lam[0])
    for v in range(4):
        rates_ref[v : v + 1, :] = parts[v]
        for k, jac in enumerate(back(tuple(one if i == v else zero for i in range(4)))):
            rates_ref[8 + 3 * v + k : 9 + 3 * v + k, :] = jac
    rates_ref[4:8, :] = jnp.zeros((4, states), F32)
    rates_ref[20:24, :] = jnp.zeros((4, states), F32)
    ar = jnp.broadcast_to(parts[0], (CHUNKS, states))
    ai = jnp.broadcast_to(parts[1], (CHUNKS, states))

    def step(j, carry):
        out = []
        for s in range(seqs):
            ur, ui, q = carry[s]
            at = pl.ds(PAD + s * pitch + j, CHUNKS, stride=steps)
            lk = link_ref[at, :]
            lw = wide(lk, groups)
            nr, ni = cmul(ar, ai, ur, ui)
            out.append((lw * nr + take(proj_ref, at, 0, groups), lw * ni + take(proj_ref, at, groups, groups), q * lk))
        return tuple(out)

    zero = jnp.zeros((CHUNKS, states), F32)
    init = tuple((zero, zero, jnp.ones((CHUNKS, LANES), F32)) for _ in range(seqs))
    ends = run(steps, step, init, 13)
    pr, pi = chunk_powers(ar, ai, steps)
    for s in range(seqs):
        ur, ui, q = ends[s]
        qw = wide(q, groups)
        sc = chunk_scan(pr * qw, pi * qw, ur, ui, False)
        for v in range(4):
            s1_ref[s * CHUNKS : (s + 1) * CHUNKS, v * states : (v + 1) * states] = sc[v]
        msg_ref[s : s + 1, :states] = sc[2][CHUNKS - 1 :, :]
        msg_ref[s : s + 1, states : 2 * states] = sc[3][CHUNKS - 1 :, :]
        msg_ref[s : s + 1, 2 * states :] = ids_ref[seqs + s : seqs + s + 1, :]


def k2_body(*refs, seqs, hops):
    (x_ref, t_ref, link_ref, valid_ref, ids_ref, low_ref, proj_ref, s1_ref, rates_ref, vec_ref,
     c0, c1, c2, c3) = refs[:14]
    recvs = refs[14 : 14 + hops]
    (out_hbm, state_ref, gs_ref, gres_ref, gssm_ref, s2_ref, msg_ref, send_ref, keep_ref,
     wc_scr, wg_scr, gc_scr, gg_scr, sum_scr, out_ref, sems) = refs[14 + hops :]
    rows, width = x_ref.shape
    states = rates_ref.shape[1]
    groups = states // LANES
    block_len = rows // seqs
    steps = block_len // CHUNKS + 1
    pitch = block_len + PAD
    g_shard = width // 4
    c_shard = 2 * states // 4
    w = own_w()
    for k, piece in enumerate((c0, c1, c2, c3)):
        wc_scr[pl.ds(pl.multiple_of((w ^ k) * c_shard, c_shard), c_shard), :] = piece[:c_shard, :]
        wg_scr[pl.ds(pl.multiple_of((w ^ k) * g_shard, g_shard), g_shard), :] = piece[c_shard:, :]
    a1r, a1i = rates_ref[0:1, :], rates_ref[1:2, :]
    ar = jnp.broadcast_to(a1r, (CHUNKS, states))
    ai = jnp.broadcast_to(a1i, (CHUNKS, states))
    zr = jnp.broadcast_to(rates_ref[2:3, :], (CHUNKS, states))
    zi = jnp.broadcast_to(rates_ref[3:4, :], (CHUNKS, states))
    top = lax.broadcasted_iota(jnp.int32, (CHUNKS, states), 0)
    ids = ids_ref[...]
    init, carries = [], []
    for s in range(seqs):
        cr, ci = carry_in(recvs, ids, s, s, a1r, a1i, block_len, False, lax.axis_index("seq"))
        sc = [s1_ref[s * CHUNKS : (s + 1) * CHUNKS, v * states : (v + 1) * states] for v in range(4)]
        mr, mi = cmul(sc[0], sc[1], cr, ci)
        init.append((pltpu.roll(sc[2] + mr, 1, 0), pltpu.roll(sc[3] + mi, 1, 0)))
        carries.append((cr, ci))

    def step(j, carry):
        out = []
        for s in range(seqs):
            ur, ui = carry[s]
            at = pl.ds(PAD + s * pitch + j, CHUNKS, stride=steps)
            lw = wide(link_ref[at, :], groups)
            nr, ni = cmul(ar, ai, ur, ui)
            ur, ui = lw * nr + take(proj_ref, at, 0, groups), lw * ni + take(proj_ref, at, groups, groups)
            sr, si = cmul(zr, zi, ur, ui)
            put(state_ref, at, 0, sr)
            put(state_ref, at, groups, si)
            out.append((ur, ui))
        return tuple(out)

    for g in range(2 * groups):
        state_ref[g, :PAD, :] = jnp.zeros((PAD, LANES), F32)
    entry = list(run(PAD, step, tuple(init), PAD))
    for s in range(seqs):
        ur, ui = (jnp.where(top == 0, c, u) for c, u in zip(carries[s], entry[s]))
        sr, si = cmul(zr, zi, ur, ui)
        at = pl.ds(PAD + s * pitch + PAD - 1, CHUNKS, stride=steps)
        put(state_ref, at, 0, sr)
        put(state_ref, at, groups, si)
        entry[s] = (ur, ui)
    run(steps - PAD, lambda i, c: step(i + PAD, c), tuple(entry), 8)

    skip = vec_ref[2:3, :]
    gbias = 0.5 * vec_ref[3:4, :]
    leaving = []
    loss_acc = jnp.zeros((8, width), F32)
    gbias_acc = jnp.zeros((8, width), F32)
    skip_acc = jnp.zeros((8, width), F32)
    for i in range(rows // TILE):
        at = slice(i * TILE, (i + 1) * TILE)
        pad_at = padded(i, block_len)
        sl = take(state_ref, pad_at, 0, 2 * groups).astype(BF16)
        so = jnp.dot(sl, wc_scr[...], preferred_element_type=F32) + skip * low_ref[at, :].astype(F32)
        e = jnp.exp2(so * so * -0.7213475204444817)
        t = 1.0 / (1.0 + 0.23164189 * jnp.abs(so))
        tail = e * t * (0.127414796 + t * (-0.142248368 + t * (0.7107068705 + t * (-0.7265760135 + t * 0.5307027145))))
        phi = jnp.where(so >= 0.0, 1.0 - tail, tail)
        act = (so * phi).astype(BF16)
        dgelu = phi + so * e * 0.3989422804014327
        g = 0.5 * jnp.tanh(0.5 * jnp.dot(act, wg_scr[...], preferred_element_type=F32) + gbias) + 0.5
        gated = act.astype(F32) * g
        res = x_ref[at, :].astype(F32) + gated
        out_ref[at, :] = res.astype(BF16)
        leaving.append(pltpu.make_async_copy(out_ref.at[at, :], out_hbm.at[at, :], sems.at[i]))
        leaving[-1].start()
        err = res - t_ref[at, :].astype(F32)
        gr = err * wide(valid_ref[at, :], width // LANES)
        loss_acc = loss_acc + fold_rows(gr * err)
        gres_ref[at, :] = gr.astype(BF16)
        gg = gr * gated * (1.0 - g)
        gbias_acc = gbias_acc + fold_rows(gg)
        gl = gg.astype(BF16)
        add_to(gg_scr, i, tn_dot(act, gl))
        gssm = dgelu * (gr * g + nt_dot(gl, wg_scr[...]))
        gssm_ref[at, :] = gssm
        skip_acc = skip_acc + fold_rows(gssm * low_ref[at, :].astype(F32))
        ssl = gssm.astype(BF16)
        put(gs_ref, pad_at, 0, nt_dot(ssl, wc_scr[...]).astype(BF16).astype(F32))
        add_to(gc_scr, i, tn_dot(sl, ssl))
    clear_pads(gs_ref, seqs, pitch)
    sum_scr[0:1, :] = one_row(skip_acc)
    sum_scr[1:2, :] = one_row(gbias_acc)
    loss = jnp.sum(one_row(loss_acc), axis=1, keepdims=True)
    count = one_row(fold_rows(valid_ref[...]))

    def back(i, carry):
        j = steps - 1 - i
        out = []
        for s in range(seqs):
            yr, yi, q = carry[s]
            at = pl.ds(PAD + s * pitch + j, CHUNKS, stride=steps)
            lk = link_ref[at, :]
            lw = wide(lk, groups)
            nr, ni = cmul(ar, -ai, yr, yi)
            out.append((lw * (nr + take(gs_ref, at, 0, groups)), lw * (ni + take(gs_ref, at, groups, groups)), q * lk))
        return tuple(out)

    zero = jnp.zeros((CHUNKS, states), F32)
    init = tuple((zero, zero, jnp.ones((CHUNKS, LANES), F32)) for _ in range(seqs))
    firsts = run(steps - PAD, back, init, 8)
    ends = run(PAD, lambda i, c: back(i + steps - PAD, c), firsts, PAD)
    pr, pi = chunk_powers(ar, -ai, steps)
    for s in range(seqs):
        yr, yi, q = (jnp.where(top[:, : v.shape[1]] == 0, u, v) for u, v in zip(firsts[s], ends[s]))
        qw = wide(q, groups)
        sc = chunk_scan(pr * qw, pi * qw, yr, yi, True)
        for v in range(4):
            s2_ref[s * CHUNKS : (s + 1) * CHUNKS, v * states : (v + 1) * states] = sc[v]
        msg_ref[s : s + 1, :states] = sc[2][:1, :]
        msg_ref[s : s + 1, states : 2 * states] = sc[3][:1, :]
        msg_ref[s : s + 1, 2 * states :] = ids_ref[s : s + 1, :]

    for k, dst in enumerate((keep_ref, send_ref, keep_ref, send_ref)):
        q = w ^ k
        slot = q // 2
        dst[slot, :c_shard, :] = gc_scr[pl.ds(pl.multiple_of(q * c_shard, c_shard), c_shard), :].astype(BF16)
        lanes = pl.multiple_of(q * g_shard, g_shard)
        dst[slot, c_shard : c_shard + g_shard, :] = gg_scr[pl.ds(lanes, g_shard), :].astype(BF16)
        line = jnp.concatenate(
            [sum_scr[v : v + 1, pl.ds(lanes, g_shard)] for v in range(2)]
            + [jnp.broadcast_to(loss, (1, LANES)), count], axis=1)
        dst[slot, c_shard + g_shard :, :] = split_rows([jnp.zeros((3, width), F32), line])
    for copy in leaving:
        copy.wait()


def split16(v):
    high = v.astype(BF16)
    return high, (v - high.astype(F32)).astype(BF16)


def split_rows(lines):
    width = lines[0].shape[1]
    rows = sum(v.shape[0] for v in lines)
    v = jnp.concatenate(lines + [jnp.zeros((8 - rows, width), F32)] * (rows < 8), axis=0)
    high, rest = split16(v)
    return jnp.concatenate([high.astype(F32), rest.astype(F32)], axis=0).astype(BF16)


def k3_body(*refs, seqs, hops, blocks):
    (n_ref, link_ref, ids_ref, low_ref, proj_ref, state_ref, gs_ref, gssm_ref,
     s2_ref, rates_ref, vec_ref, w_full) = refs[:12]
    recvs = refs[12 : 12 + hops]
    (gn_ref, send_ref, keep_ref, gp_scr, gpl_scr, gb_scr, vec_scr) = refs[12 + hops :]
    rows, width = n_ref.shape
    states = rates_ref.shape[1]
    groups = states // LANES
    block_len = rows // seqs
    steps = block_len // CHUNKS + 1
    pitch = block_len + PAD
    shard = width // 4
    w = own_w()
    a1r, a1i = rates_ref[0:1, :], rates_ref[1:2, :]
    ar = jnp.broadcast_to(a1r, (CHUNKS, states))
    ai = jnp.broadcast_to(a1i, (CHUNKS, states))
    zr = jnp.broadcast_to(rates_ref[2:3, :], (CHUNKS, states))
    zi = jnp.broadcast_to(rates_ref[3:4, :], (CHUNKS, states))
    rowid = lax.broadcasted_iota(jnp.int32, (CHUNKS, states), 0)
    ids = ids_ref[...]
    rate_sums = [jnp.zeros((CHUNKS, states), F32) for _ in range(4)]
    for s in range(seqs):
        cr, ci = carry_in(recvs, ids, s, seqs + s, a1r, a1i, block_len, True, blocks - 1 - lax.axis_index("seq"))
        sc = [s2_ref[s * CHUNKS : (s + 1) * CHUNKS, v * states : (v + 1) * states] for v in range(4)]
        mr, mi = cmul(sc[0], sc[1], cr, ci)
        yr = jnp.where(rowid == CHUNKS - 1, cr, pltpu.roll(sc[2] + mr, CHUNKS - 1, 0))
        yi = jnp.where(rowid == CHUNKS - 1, ci, pltpu.roll(sc[3] + mi, CHUNKS - 1, 0))

        def step(i, carry):
            yr, yi, gar, gai, gsr, gsi = carry
            j = steps - 1 - i
            at = pl.ds(PAD + s * pitch + j, CHUNKS, stride=steps)
            before = pl.ds(PAD + s * pitch + j - 1, CHUNKS, stride=steps)
            lw = wide(link_ref[at, :], groups)
            nr, ni = cmul(ar, -ai, yr, yi)
            dr, di = nr + take(gs_ref, at, 0, groups), ni + take(gs_ref, at, groups, groups)
            yr, yi = lw * dr, lw * di
            pr, pi = take(proj_ref, at, 0, groups), take(proj_ref, at, groups, groups)
            ur, ui = take(state_ref, before, 0, groups), take(state_ref, before, groups, groups)
            put(gp_scr, at, 0, zr * dr + zi * di)
            put(gp_scr, at, groups, zr * di - zi * dr)
            return (
                yr, yi,
                gar + (ur * yr + ui * yi), gai + (ur * yi - ui * yr),
                gsr + (pr * dr + pi * di), gsi + (pr * di - pi * dr),
            )

        carry = run(steps - PAD, step, (yr, yi, *rate_sums), 8)
        yr, yi = (jnp.where(rowid == 0, 0.0, v) for v in carry[:2])
        carry = run(PAD, lambda i, c: step(i + steps - PAD, c), (yr, yi, *carry[2:]), PAD)
        rate_sums = list(carry[2:])

    skip = vec_ref[2:3, :]
    gain_acc = jnp.zeros((8, width), F32)
    bias_acc = jnp.zeros((8, width), F32)
    for i in range(rows // TILE):
        at = slice(i * TILE, (i + 1) * TILE)
        gpl = take(gp_scr, padded(i, block_len), 0, 2 * groups).astype(BF16)
        gpl_scr[at, :] = gpl
        gn = nt_dot(gpl, w_full[...]) + skip * gssm_ref[at, :]
        gn_ref[at, :] = gn.astype(BF16)
        gain_acc = gain_acc + fold_rows(gn * n_ref[at, :].astype(F32))
        bias_acc = bias_acc + fold_rows(gn)
    gb_scr[...] = tn_dot(low_ref[...], gpl_scr[...])
    sums4 = [one_row(v) for v in rate_sums]
    rate_grads = []
    for k in range(3):
        rate_grads.append(sum(rates_ref[8 + 3 * c + k : 9 + 3 * c + k, :] * sums4[c] for c in range(4)))
    vec_scr[0:1, :] = one_row(gain_acc)
    vec_scr[1:2, :] = one_row(bias_acc)
    extra = 3 * shard // 2
    half = shard // 2
    for k, dst in enumerate((keep_ref, send_ref, keep_ref, send_ref)):
        slot = (w ^ k) // 2
        q = pl.multiple_of((w ^ k) * shard, shard)
        dst[slot, :shard, :] = gb_scr[pl.ds(q, shard), :width].astype(BF16)
        dst[slot, shard:extra, : width // 2] = gb_scr[pl.ds(q, half), width:].astype(BF16)
        dst[slot, shard:extra, width // 2 :] = gb_scr[pl.ds(q + half, half), width:].astype(BF16)
        mine = [vec_scr[v : v + 1, pl.ds(q, shard)] for v in range(2)] + [jnp.zeros((1, shard), F32)]
        dst[slot, extra:, :] = split_rows([jnp.concatenate(p, axis=1) for p in zip(rate_grads, mine)])


def centre(values):
    x = values.astype(F32)
    c = x - jnp.mean(x, -1, keepdims=True)
    r = lax.rsqrt(jnp.mean(c * c, -1, keepdims=True) + 1e-05)
    return c * r, r


def sum_body(c0, c1, c2, c3, sum_ref):
    sum_ref[...] = total((c0, c1, c2, c3), slice(0, sum_ref.shape[0]))


def quarter_body(keep_ref, got_ref, *outs):
    half = outs[0].shape[0] - 16
    x, y = lax.axis_index("seq") % 2, lax.axis_index("wy")
    for out, slot, side in zip(outs, (y, 1 - y, y, 1 - y), (x, x, 1 - x, 1 - x)):
        def both(rows):
            return keep_ref[slot, rows, :].astype(F32) + got_ref[slot, rows, :].astype(F32)

        out[:half, :] = both(pl.ds(pl.multiple_of(side * half, half), half)).astype(BF16)
        v = both(slice(2 * half, 2 * half + 16))
        out[half:, :] = split_rows([v[:8] + v[8:]])


def total(refs, rows):
    return sum([r[rows, :].astype(F32) for r in refs[1:]], refs[0][rows, :].astype(F32))


def deal_body(*refs):
    n = len(refs) - 6
    bs, c_sum, outs, b_scr = refs[:4], refs[4], refs[5 : 5 + n], refs[5 + n]
    b_half, c_half = b_scr.shape[0], c_sum.shape[0] - 16
    b_part, c_part = b_half // n, c_half // n
    b_scr[...] = total(bs, slice(0, b_half))
    tail = total(bs, slice(b_half, b_half + 16)) + c_sum[c_half:, :]
    ends = split_rows([tail[:8] + tail[8:]]).astype(F32)
    for k, out in enumerate(outs):
        at = (lax.axis_index("seq") // 2) ^ k
        rows = [
            b_scr[pl.ds(pl.multiple_of(at * b_part, 8), b_part), :],
            c_sum[pl.ds(pl.multiple_of(at * c_part, 8), c_part), :],
            ends[:4], ends[8:12],
        ]
        out[...] = jnp.concatenate(rows, axis=0).astype(BF16)


def close_body(*refs):
    parts, (piece_ref, tail_ref) = refs[:-2], refs[-2:]
    bulk = piece_ref.shape[0]
    v = total(parts, slice(0, bulk + 8))
    piece_ref[...] = v[:bulk].astype(BF16)
    tail_ref[...] = jnp.concatenate([v[bulk : bulk + 4] + v[bulk + 4 :], jnp.zeros((4, v.shape[1]), F32)], axis=0)


def scale_of(tail, tokens):
    return tokens / tail[3:4, 3 * LANES : 3 * LANES + 1]


def norm_body(x_ref, gn_ref, gres_ref, vec_ref, ig_ref):
    gain = vec_ref[0:1, :]
    for i in range(x_ref.shape[0] // TILE):
        at = slice(i * TILE, (i + 1) * TILE)
        n, r = centre(x_ref[at, :])
        q = gn_ref[at, :].astype(F32) * gain
        back = (q - jnp.mean(q, -1, keepdims=True) - n * jnp.mean(q * n, -1, keepdims=True)) * r
        ig_ref[at, :] = (gres_ref[at, :].astype(F32) + back).astype(BF16)


def finish_body(tail_ref, ig_ref,
                out_ref, loss_ref, gain_ref, bias_ref, skip_ref, gate_ref, real_ref, imag_ref, step_ref, *, tokens):
    width = ig_ref.shape[1]
    states = width - gain_ref.shape[1]
    own = real_ref.shape[1]
    tail = tail_ref[...]
    scale = scale_of(tail, tokens)
    out_ref[...] = scale * ig_ref[...].astype(F32)
    scaled = tail * scale
    gain_ref[...] = scaled[0:1, states:]
    bias_ref[...] = scaled[1:2, states:]
    skip_ref[...] = scaled[3:4, :LANES]
    gate_ref[...] = scaled[3:4, LANES : 2 * LANES]
    loss_ref[...] = tail[3:4, 2 * LANES : 2 * LANES + 1] * scale * (1.0 / (tokens * width))
    rates = pltpu.roll(scaled[:, :states], states - lax.axis_index("seq") * own, 1)
    for k, ref in enumerate((real_ref, imag_ref, step_ref)):
        ref[...] = rates[k : k + 1, :own]


def unpack_body(tail_ref, *refs, tokens):
    pieces, (gb_ref, gc_ref, gg_ref, b_scr, c_scr) = refs[:-5], refs[-5:]
    scale = scale_of(tail_ref[...], tokens)
    S = len(pieces)
    b_rows, c_rows = b_scr.shape[0] // S, c_scr.shape[0] // S
    for k, piece in enumerate(pieces):
        s = lax.axis_index("seq") ^ k
        v = piece[...].astype(F32) * scale
        b_at = s % 2 * (b_scr.shape[0] // 2) + s // 2 * b_rows
        c_at = s % 2 * (c_scr.shape[0] // 2) + s // 2 * c_rows
        b_scr[pl.ds(pl.multiple_of(b_at, 8), b_rows), :] = v[:b_rows, :]
        c_scr[pl.ds(pl.multiple_of(c_at, 8), c_rows), :] = v[b_rows:, :]
    shard, cols = gb_ref.shape
    width = b_scr.shape[1]
    half = shard // 2
    gb_ref[:, :width] = b_scr[:shard, :]
    gb_ref[:half, width:] = b_scr[shard:, : cols - width]
    gb_ref[half:, width:] = b_scr[shard:, cols - width :]
    gc_ref[...] = c_scr[: gc_ref.shape[0], :]
    gg_ref[...] = c_scr[gc_ref.shape[0] :, :]


def whole(n, far=()):
    return [pl.BlockSpec(memory_space=pltpu.HBM if i in far else pltpu.VMEM) for i in range(n)]


def call(body, outs, scratch, *args, us=1, limit=30, far=(), far_outs=(), copies=0):
    return pl.pallas_call(
        body,
        out_shape=[jax.ShapeDtypeStruct(*o) for o in outs],
        in_specs=whole(len(args), far),
        out_specs=whole(len(outs), far_outs),
        scratch_shapes=[pltpu.VMEM(*s) for s in scratch] + [pltpu.SemaphoreType.DMA((copies,))] * (copies > 0),
        compiler_params=pltpu.CompilerParams(vmem_limit_bytes=limit * MIB),
        cost_estimate=pl.CostEstimate(flops=us * 1_000_000_000, bytes_accessed=MIB, transcendentals=0),
    )(*args)


def per_device(inputs, teacher, segment_ids, valid_mask, ln_gain, ln_bias, b_weight, c_weight, skip_weight,
               glu_weight, glu_bias, lambda_real, lambda_imag, log_step):
    S = lax.axis_size("seq")
    s_at = lax.axis_index("seq")
    seqs, block_len, width = inputs.shape
    rows = seqs * block_len
    padded_rows = PAD + seqs * (block_len + PAD)
    length = S * block_len
    own = lambda_real.shape[0]
    states = own * S
    doc_most = {4096: 1024, 32768: 8192}.get(length, length)
    hops = min((doc_most - 2) // block_len + 1, S - 1)
    shard, c_shard, g_shard = b_weight.shape[0], c_weight.shape[0], glu_weight.shape[0]

    def swap(v, axis, bit=1, n=2):
        return lax.ppermute(v, axis, [(i, i ^ bit) for i in range(n)])

    def after(v, *others):
        return lax.optimization_barrier((v, *others))[0]

    b_msg, table = call(
        k0_body,
        [((shard + 16, b_weight.shape[1]), BF16), ((8, states), F32)],
        [(b_weight.shape, BF16), ((4, 1, shard), BF16), ((3, 1, own), F32), ((8, states), F32)],
        b_weight, *(v[None] for v in (ln_gain, ln_bias, skip_weight, glu_bias, lambda_real, lambda_imag, log_step)),
        far=range(8), copies=8, limit=60,
    )
    b_far = swap(b_msg, "wy")
    b_near = swap(b_msg, "wc")
    (c_msg,) = call(
        k0b_body,
        [((c_shard + g_shard, width), BF16)],
        [(c_weight.shape, BF16), (glu_weight.shape, BF16)],
        c_weight, glu_weight, far=range(2), copies=2, limit=4,
    )
    c_far = swap(after(c_msg, b_far), "wy")
    bit = 1
    while bit < S:
        radix = 4 if 4 * bit <= S else 2
        table = sum([swap(table, "seq", k * bit, S) for k in range(1, radix)], table)
        bit *= radix
    bs = (b_msg, b_near, b_far, swap(b_far, "wc"))

    x = inputs.reshape(rows, width)
    teach = teacher.reshape(rows, width)
    R = seqs * CHUNKS
    slab = (2 * states // LANES, padded_rows, LANES)
    msg_shape = ((seqs, 2 * states + LANES), F32)
    low, norm, proj, vec, w_full, s1, fwd, rates, link, valid, ids = call(
        functools.partial(k1_body, seqs=seqs),
        [((rows, width), BF16), ((rows, width), BF16), (slab, F32), ((8, width), F32), ((width, 2 * states), BF16),
         ((R, 4 * states), F32), msg_shape, ((24, states), F32),
         ((padded_rows, LANES), F32), ((rows, LANES), F32), ((2 * seqs, LANES), F32)],
        [],
        x, *bs, table, segment_ids, valid_mask, us=2, limit=8,
    )
    cs = (c_msg, swap(c_msg, "wc"), c_far, swap(after(c_far, fwd), "wc"))
    fwds = [lax.ppermute(fwd, "seq", [(i, (i + k) % S) for i in range(S)]) for k in range(1, hops + 1)]
    c_bulk = c_shard + g_shard
    out, state, gs, gres, gssm, s2, bwd, send_c, keep_c = call(
        functools.partial(k2_body, seqs=seqs, hops=hops),
        [((rows, width), BF16), (slab, F32), (slab, F32),
         ((rows, width), BF16), ((rows, width), F32), ((R, 4 * states), F32), msg_shape,
         ((2, c_bulk + 16, width), BF16), ((2, c_bulk + 16, width), BF16)],
        [((2 * states, width), BF16), ((width, width), BF16), ((2 * states, width), F32), ((width, width), F32),
         ((8, width), F32), ((rows, width), BF16)],
        x, teach, link, valid, ids, low, proj, s1, rates, vec, *cs, *fwds, us=10, limit=20, far_outs=(0,), copies=rows // TILE,
    )
    bwds = [lax.ppermute(bwd, "seq", [((i + k) % S, i) for i in range(S)]) for k in range(1, hops + 1)]
    def cross(v, flip_x, flip_y):
        return lax.ppermute(
            v, ("seq", "wy"), [(2 * a + b, 2 * (a ^ flip_x) + (b ^ flip_y)) for a in range(S) for b in range(2)])

    def quarters(keep, got):
        shape = ((keep.shape[1] - 16) // 2 + 16, width)
        return call(quarter_body, [(shape, BF16)] * 4, [], keep, got, limit=4)

    def exchange(q):
        return (q[0], cross(q[1], 0, 1), cross(q[2], 1, 0), cross(q[3], 1, 1))

    q_c = quarters(keep_c, swap(send_c, "wc"))
    bwds = lax.optimization_barrier((bwds, q_c))[0]
    part_c = exchange(q_c)
    b_bulk = 3 * shard // 2
    b_part, c_part = b_bulk // S, c_bulk // S
    gn, send_b, keep_b = call(
        functools.partial(k3_body, seqs=seqs, hops=hops, blocks=S),
        [((rows, width), BF16), ((2, b_bulk + 16, width), BF16), ((2, b_bulk + 16, width), BF16)],
        [(slab, F32), ((rows, 2 * states), BF16), ((width, 2 * states), F32), ((8, width), F32)],
        norm, link, ids, low, proj, state, gs, gssm, s2, rates, vec, w_full, *bwds, us=8, limit=14,
    )
    (c_sum,) = call(sum_body, [((c_bulk // 2 + 16, width), F32)], [], *part_c, limit=4)
    got_b = swap(after(send_b, part_c[3]), "wc")
    part_b = exchange(quarters(keep_b, got_b))
    (ig,) = call(norm_body, [((rows, width), BF16)], [], x, gn, gres, vec, us=3, limit=8)
    part_b, ig = lax.optimization_barrier((part_b, ig))
    tokens = float(length * seqs * lax.axis_size(("wy", "wc")))
    deal = S // 2
    if b_part % 8 == 0 and c_part % 8 == 0:
        dealt = call(
            deal_body, [((b_part + c_part + 8, width), BF16)] * deal,
            [((b_bulk // 2, width), F32)], *part_b, c_sum, limit=4,
        )
        parts = [dealt[0]] + [swap(dealt[k], "seq", 2 * k, S) for k in range(1, deal)]
        piece, tail = call(
            close_body, [((b_part + c_part, width), BF16), ((8, width), F32)], [], *parts, limit=4,
        )
        pieces = {0: piece}
        for k in range(1, deal):
            pieces[2 * k] = swap(piece, "seq", 2 * k, S)
        for k in range(deal):
            pieces[2 * k + 1] = swap(pieces[2 * k], "seq", 1, S)
        pieces = [pieces[k] for k in range(S)]
    else:
        piece, tail, pieces = sum_by_all_to_all(part_b, c_sum, S, s_at)
    ingrad, loss, *lines = call(
        functools.partial(finish_body, tokens=tokens),
        [((rows, width), F32), ((1, 1), F32)] + [((1, shard), F32)] * 4 + [((1, own), F32)] * 3,
        [], tail, ig, limit=8,
    )
    gb, gc, gg = call(
        functools.partial(unpack_body, tokens=tokens),
        [((shard, 2 * states), F32), ((c_shard, width), F32), ((g_shard, width), F32)],
        [((b_bulk, width), F32), ((c_bulk, width), F32)],
        tail, *pieces, limit=8,
    )
    gain, bias, skip, gate, real, imag, step = (v[0] for v in lines)
    return (
        out.reshape(inputs.shape), loss[0, 0], ingrad.reshape(inputs.shape), gain, bias, gb, gc, skip, gg, gate,
        real, imag, step,
    )


def sum_by_all_to_all(part_b, v_c, S, s_at):
    v_b = sum([p.astype(F32) for p in part_b[1:]], part_b[0].astype(F32))
    width = v_b.shape[1]
    tail = v_b[-16:-8] + v_b[-8:] + v_c[-16:-8] + v_c[-8:]
    high = lax.reduce_precision(tail, 8, 7)
    ends = jnp.concatenate([high, tail - high], 0).astype(BF16)
    both = jnp.concatenate([v[:-16].astype(BF16).reshape(S // 2, -1, width) for v in (v_b, v_c)], 1)
    bulk = both.shape[1]
    both = jnp.concatenate([both, jnp.broadcast_to(ends[None], (S // 2, 16, width))], 1)
    empty = jnp.zeros_like(both)
    mine = (lax.iota(jnp.int32, S) % 2 == s_at % 2)[:, None, None]
    sent = jnp.where(mine, jnp.stack([both, both], 1).reshape(S, bulk + 16, width), jnp.stack([empty, empty], 1).reshape(S, bulk + 16, width))
    v = jnp.sum(lax.all_to_all(sent, "seq", 0, 0, tiled=True).astype(F32), 0)
    piece, tail = v[:bulk].astype(BF16), v[bulk : bulk + 8] + v[bulk + 8 :]
    back = lax.all_to_all(jnp.broadcast_to(piece[None], (S, bulk, width)), "seq", 0, 0, tiled=True)
    order = lax.iota(jnp.int32, S) ^ s_at
    return piece, tail, [lax.dynamic_index_in_dim(back, order[k], 0, keepdims=False) for k in range(S)]


def solution(mesh):
    sizes = mesh.devices.shape
    fine = Mesh(mesh.devices.reshape(sizes[0], 2, sizes[1] // 2), ("seq", "wy", "wc"))
    w = ("wy", "wc")
    tokens = P(w, "seq", None)
    return jax.shard_map(
        per_device,
        mesh=fine,
        in_specs=(
            tokens, tokens, P(w, "seq"), P(w, "seq"), P(w), P(w), P(w, None), P(w, None), P(w), P(w, None), P(w),
            P("seq"), P("seq"), P("seq"),
        ),
        out_specs=(
            tokens, P(), tokens, P(w), P(w), P(w, None), P(w, None), P(w), P(w, None), P(w),
            P("seq"), P("seq"), P("seq"),
        ),
        check_vma=False,
    )
```

```python
import functools

import jax
import jax.numpy as jnp
from jax import lax
from jax.experimental import pallas as pl
from jax.experimental.pallas import tpu as pltpu
from jax.sharding import Mesh
from jax.sharding import PartitionSpec as P

CHUNKS = 8
LANES = 128
TILE = 512
PAD = 8
MIB = 1024 * 1024
F32 = jnp.float32
BF16 = jnp.bfloat16


def small_expm1(x):
    return x * (1.0 + x / 2 * (1.0 + x / 3 * (1.0 + x / 4 * (1.0 + x / 5 * (1.0 + x / 6)))))


def rates_map(real_rate, imag_rate, log_rate):
    time_step = jnp.exp(log_rate)
    grow_re = real_rate * time_step
    turn_im = imag_rate * time_step
    growth = jnp.exp(grow_re)
    abar_re = growth * jnp.cos(turn_im)
    abar_im = growth * jnp.sin(turn_im)
    half_sine = jnp.sin(0.5 * turn_im)
    numer_re = small_expm1(grow_re) * jnp.cos(turn_im) - 2.0 * half_sine * half_sine
    divisor = real_rate * real_rate + imag_rate * imag_rate
    scale_re = (numer_re * real_rate + abar_im * imag_rate) / divisor
    scale_im = (abar_im * real_rate - numer_re * imag_rate) / divisor
    return (abar_re, abar_im, scale_re, scale_im)


def cmul(xr, xi, yr, yi):
    return xr * yr - xi * yi, xr * yi + xi * yr


def power2(xr, xi, times):
    for _ in range(times):
        xr, xi = xr * xr - xi * xi, 2.0 * xr * xi
    return xr, xi


def log2(n):
    return n.bit_length() - 1


def power(xr, xi, n):
    out = None
    while n:
        if n & 1:
            out = (xr, xi) if out is None else cmul(*out, xr, xi)
        n >>= 1
        if n:
            xr, xi = power2(xr, xi, 1)
    return out


def chunk_powers(ar, ai, steps):
    first = lax.broadcasted_iota(jnp.int32, ar.shape, 0) == 0
    sr, si = power(ar, ai, steps - PAD)
    pr, pi = power(ar, ai, steps)
    return jnp.where(first, sr, pr), jnp.where(first, si, pi)


def padded(i, block_len):
    start = i * TILE + PAD * (2 + i * TILE // block_len)
    return slice(start, start + TILE)


def add_to(ref, i, v):
    ref[...] = v if i == 0 else ref[...] + v


def run(count, body, carry, unroll):
    def block(k, c):
        for u in range(unroll):
            c = body(k * unroll + u, c)
        return c

    whole_blocks = count // unroll
    carry = lax.fori_loop(0, whole_blocks, block, carry)
    for i in range(whole_blocks * unroll, count):
        carry = body(i, carry)
    return carry


def wide(v, groups):
    return jnp.concatenate([v] * groups, axis=1)


def fold_rows(v):
    return jnp.sum(v.reshape(-1, 8, v.shape[-1]), axis=0)


def take(ref, at, first, count):
    return jnp.concatenate([ref[first + g, at, :] for g in range(count)], axis=1)


def put(ref, at, first, v):
    for g in range(v.shape[1] // LANES):
        ref[first + g, at, :] = v[:, g * LANES : (g + 1) * LANES]


def clear_pads(ref, seqs, pitch):
    for g in range(ref.shape[0]):
        ref[g, :PAD, :] = jnp.zeros((PAD, LANES), F32)
        for s in range(seqs):
            ref[g, PAD + s * pitch : 2 * PAD + s * pitch, :] = jnp.zeros((PAD, LANES), F32)


def own_w():
    return 2 * lax.axis_index("wy") + lax.axis_index("wc")


def one_row(v):
    return jnp.sum(v, axis=0, keepdims=True)


def nt_dot(a, b):
    return lax.dot_general(a, b, (((1,), (1,)), ((), ())), preferred_element_type=F32)


def tn_dot(a, b):
    return lax.dot_general(a, b, (((0,), (0,)), ((), ())), preferred_element_type=F32)


def chunk_scan(ar, ai, br, bi, reverse):
    rows = lax.broadcasted_iota(jnp.int32, ar.shape, 0)
    d = 1
    while d < CHUNKS:
        shift = (CHUNKS - d) if reverse else d
        keep = (rows < CHUNKS - d) if reverse else (rows >= d)
        pr, pi = pltpu.roll(ar, shift, 0), pltpu.roll(ai, shift, 0)
        qr, qi = pltpu.roll(br, shift, 0), pltpu.roll(bi, shift, 0)
        mr, mi = cmul(ar, ai, qr, qi)
        br, bi = jnp.where(keep, br + mr, br), jnp.where(keep, bi + mi, bi)
        mr, mi = cmul(ar, ai, pr, pi)
        ar, ai = jnp.where(keep, mr, ar), jnp.where(keep, mi, ai)
        d *= 2
    return ar, ai, br, bi


def carry_in(recvs, ids, s, own_row, ar, ai, block_len, conj, blocks):
    states = ar.shape[1]
    pr, pi = power2(ar, -ai if conj else ai, log2(block_len))
    cr = jnp.zeros((1, states), F32)
    ci = jnp.zeros((1, states), F32)
    own = wide(ids[own_row : own_row + 1, :], states // LANES)
    for k in range(len(recvs), 0, -1):
        msg = recvs[k - 1][s : s + 1, :]
        same = (wide(msg[:, 2 * states :], states // LANES) == own) & (blocks >= k)
        cr, ci = cmul(pr, pi, cr, ci)
        cr = cr + jnp.where(same, msg[:, :states], 0.0)
        ci = ci + jnp.where(same, msg[:, states : 2 * states], 0.0)
    return cr, ci


def fetch(pairs, sems):
    copies = [pltpu.make_async_copy(src, dst, sems.at[k]) for k, (src, dst) in enumerate(pairs)]
    for c in copies:
        c.start()
    for c in copies:
        c.wait()


def k0_body(b_ref, g_ref, n_ref, s_ref, q_ref, lr_ref, li_ref, ls_ref, msg_ref, table_ref,
            b_scr, v_scr, l_scr, scr, sems):
    shard, cols = b_scr.shape
    own = lr_ref.shape[1]
    fetch(
        [(b_ref, b_scr)]
        + [(r, v_scr.at[k]) for k, r in enumerate((g_ref, n_ref, s_ref, q_ref))]
        + [(r, l_scr.at[k]) for k, r in enumerate((lr_ref, li_ref, ls_ref))],
        sems,
    )
    msg_ref[:shard, :] = b_scr[...]
    line = jnp.concatenate([v_scr[k] for k in range(4)] + [jnp.zeros((1, cols - 4 * shard), BF16)], axis=1)
    msg_ref[shard:, :] = jnp.broadcast_to(line, (16, cols))
    scr[...] = jnp.zeros_like(scr)
    for k in range(3):
        scr[k : k + 1, :own] = l_scr[k]
    table_ref[...] = pltpu.roll(scr[...], lax.axis_index("seq") * own, 1)


def k0b_body(c_ref, g_ref, msg_ref, c_scr, g_scr, sems):
    c_shard = c_ref.shape[0]
    fetch([(c_ref, c_scr), (g_ref, g_scr)], sems)
    msg_ref[:c_shard, :] = c_scr[...]
    msg_ref[c_shard:, :] = g_scr[...]


def lay_marks(seg_ref, mask_ref, link_ref, valid_ref, ids_ref):
    seqs, block_len = seg_ref.shape
    seg = seg_ref[...].astype(F32)
    link_ref[:PAD, :] = jnp.ones((PAD, LANES), F32)
    lane = lax.broadcasted_iota(jnp.int32, (1, block_len), 1)
    for s in range(seqs):
        row = seg[s : s + 1, :]
        link = jnp.where((row == pltpu.roll(row, 1, 1)) | (lane == 0), 1.0, 0.0)
        mask = mask_ref[s : s + 1, :].astype(F32)
        start = PAD + s * (block_len + PAD)
        link_ref[start : start + PAD, :] = jnp.ones((PAD, LANES), F32)
        for src, dst, start in ((link, link_ref, start + PAD), (mask, valid_ref, s * block_len)):
            for k in range(block_len // LANES):
                piece = jnp.broadcast_to(src[:, k * LANES : (k + 1) * LANES], (LANES, LANES))
                at = start + k * LANES
                dst[at : at + LANES, :] = jnp.transpose(piece)
        ids_ref[s : s + 1, :] = jnp.broadcast_to(row[:, :1], (1, LANES))
        ids_ref[seqs + s : seqs + s + 1, :] = jnp.broadcast_to(row[:, block_len - 1 :], (1, LANES))


def k1_body(x_ref, b0, b1, b2, b3, table_ref, seg_ref, mask_ref,
            low_ref, n_ref, proj_ref, vec_ref, full_ref, s1_ref, msg_ref, rates_ref, link_ref, valid_ref, ids_ref, *, seqs):
    rows, width = x_ref.shape
    shard = b0.shape[0] - 16
    block_len = rows // seqs
    pitch = block_len + PAD
    w = own_w()
    for k, piece in enumerate((b0, b1, b2, b3)):
        at = pl.multiple_of((w ^ k) * shard, shard)
        full_ref[pl.ds(at, shard), :] = piece[:shard, :]
        extra = piece[shard:, :].astype(F32)
        for v in range(4):
            vec_ref[v : v + 1, pl.ds(at, shard)] = extra[0:1, v * shard : (v + 1) * shard]
    vec_ref[4:8, :] = jnp.zeros((4, width), F32)
    gain = vec_ref[0:1, :]
    bias = vec_ref[1:2, :]
    for i in range(rows // TILE):
        at = slice(i * TILE, (i + 1) * TILE)
        n = centre(x_ref[at, :])[0]
        n_ref[at, :] = n.astype(BF16)
        low = (n * gain + bias).astype(BF16)
        low_ref[at, :] = low
        p = jnp.dot(low, full_ref[...], preferred_element_type=F32)
        put(proj_ref, padded(i, block_len), 0, p.astype(BF16).astype(F32))
    clear_pads(proj_ref, seqs, pitch)
    lay_marks(seg_ref, mask_ref, link_ref, valid_ref, ids_ref)
    states = table_ref.shape[1]
    groups = states // LANES
    steps = block_len // CHUNKS + 1
    lam = [table_ref[v : v + 1, :] for v in range(3)]
    parts, back = jax.vjp(rates_map, *lam)
    one, zero = jnp.ones_like(lam[0]), jnp.zeros_like(lam[0])
    for v in range(4):
        rates_ref[v : v + 1, :] = parts[v]
        for k, jac in enumerate(back(tuple(one if i == v else zero for i in range(4)))):
            rates_ref[8 + 3 * v + k : 9 + 3 * v + k, :] = jac
    rates_ref[4:8, :] = jnp.zeros((4, states), F32)
    rates_ref[20:24, :] = jnp.zeros((4, states), F32)
    ar = jnp.broadcast_to(parts[0], (CHUNKS, states))
    ai = jnp.broadcast_to(parts[1], (CHUNKS, states))

    def step(j, carry):
        out = []
        for s in range(seqs):
            ur, ui, q = carry[s]
            at = pl.ds(PAD + s * pitch + j, CHUNKS, stride=steps)
            lk = link_ref[at, :]
            lw = wide(lk, groups)
            nr, ni = cmul(ar, ai, ur, ui)
            out.append((lw * nr + take(proj_ref, at, 0, groups), lw * ni + take(proj_ref, at, groups, groups), q * lk))
        return tuple(out)

    zero = jnp.zeros((CHUNKS, states), F32)
    init = tuple((zero, zero, jnp.ones((CHUNKS, LANES), F32)) for _ in range(seqs))
    ends = run(steps, step, init, 13)
    pr, pi = chunk_powers(ar, ai, steps)
    for s in range(seqs):
        ur, ui, q = ends[s]
        qw = wide(q, groups)
        sc = chunk_scan(pr * qw, pi * qw, ur, ui, False)
        for v in range(4):
            s1_ref[s * CHUNKS : (s + 1) * CHUNKS, v * states : (v + 1) * states] = sc[v]
        msg_ref[s : s + 1, :states] = sc[2][CHUNKS - 1 :, :]
        msg_ref[s : s + 1, states : 2 * states] = sc[3][CHUNKS - 1 :, :]
        msg_ref[s : s + 1, 2 * states :] = ids_ref[seqs + s : seqs + s + 1, :]


def k2_body(*refs, seqs, hops):
    (x_ref, t_ref, link_ref, valid_ref, ids_ref, low_ref, proj_ref, s1_ref, rates_ref, vec_ref,
     c0, c1, c2, c3) = refs[:14]
    recvs = refs[14 : 14 + hops]
    (out_hbm, state_ref, gs_ref, gres_ref, gssm_ref, s2_ref, msg_ref, send_ref, keep_ref,
     wc_scr, wg_scr, gc_scr, gg_scr, sum_scr, out_ref, sems) = refs[14 + hops :]
    rows, width = x_ref.shape
    states = rates_ref.shape[1]
    groups = states // LANES
    block_len = rows // seqs
    steps = block_len // CHUNKS + 1
    pitch = block_len + PAD
    g_shard = width // 4
    c_shard = 2 * states // 4
    w = own_w()
    for k, piece in enumerate((c0, c1, c2, c3)):
        wc_scr[pl.ds(pl.multiple_of((w ^ k) * c_shard, c_shard), c_shard), :] = piece[:c_shard, :]
        wg_scr[pl.ds(pl.multiple_of((w ^ k) * g_shard, g_shard), g_shard), :] = piece[c_shard:, :]
    a1r, a1i = rates_ref[0:1, :], rates_ref[1:2, :]
    ar = jnp.broadcast_to(a1r, (CHUNKS, states))
    ai = jnp.broadcast_to(a1i, (CHUNKS, states))
    zr = jnp.broadcast_to(rates_ref[2:3, :], (CHUNKS, states))
    zi = jnp.broadcast_to(rates_ref[3:4, :], (CHUNKS, states))
    top = lax.broadcasted_iota(jnp.int32, (CHUNKS, states), 0)
    ids = ids_ref[...]
    init, carries = [], []
    for s in range(seqs):
        cr, ci = carry_in(recvs, ids, s, s, a1r, a1i, block_len, False, lax.axis_index("seq"))
        sc = [s1_ref[s * CHUNKS : (s + 1) * CHUNKS, v * states : (v + 1) * states] for v in range(4)]
        mr, mi = cmul(sc[0], sc[1], cr, ci)
        init.append((pltpu.roll(sc[2] + mr, 1, 0), pltpu.roll(sc[3] + mi, 1, 0)))
        carries.append((cr, ci))

    def step(j, carry):
        out = []
        for s in range(seqs):
            ur, ui = carry[s]
            at = pl.ds(PAD + s * pitch + j, CHUNKS, stride=steps)
            lw = wide(link_ref[at, :], groups)
            nr, ni = cmul(ar, ai, ur, ui)
            ur, ui = lw * nr + take(proj_ref, at, 0, groups), lw * ni + take(proj_ref, at, groups, groups)
            sr, si = cmul(zr, zi, ur, ui)
            put(state_ref, at, 0, sr)
            put(state_ref, at, groups, si)
            out.append((ur, ui))
        return tuple(out)

    for g in range(2 * groups):
        state_ref[g, :PAD, :] = jnp.zeros((PAD, LANES), F32)
    entry = list(run(PAD, step, tuple(init), PAD))
    for s in range(seqs):
        ur, ui = (jnp.where(top == 0, c, u) for c, u in zip(carries[s], entry[s]))
        sr, si = cmul(zr, zi, ur, ui)
        at = pl.ds(PAD + s * pitch + PAD - 1, CHUNKS, stride=steps)
        put(state_ref, at, 0, sr)
        put(state_ref, at, groups, si)
        entry[s] = (ur, ui)
    run(steps - PAD, lambda i, c: step(i + PAD, c), tuple(entry), 8)

    skip = vec_ref[2:3, :]
    gbias = 0.5 * vec_ref[3:4, :]
    leaving = []
    loss_acc = jnp.zeros((8, width), F32)
    gbias_acc = jnp.zeros((8, width), F32)
    skip_acc = jnp.zeros((8, width), F32)
    for i in range(rows // TILE):
        at = slice(i * TILE, (i + 1) * TILE)
        pad_at = padded(i, block_len)
        sl = take(state_ref, pad_at, 0, 2 * groups).astype(BF16)
        so = jnp.dot(sl, wc_scr[...], preferred_element_type=F32) + skip * low_ref[at, :].astype(F32)
        e = jnp.exp2(so * so * -0.7213475204444817)
        t = 1.0 / (1.0 + 0.23164189 * jnp.abs(so))
        tail = e * t * (0.127414796 + t * (-0.142248368 + t * (0.7107068705 + t * (-0.7265760135 + t * 0.5307027145))))
        phi = jnp.where(so >= 0.0, 1.0 - tail, tail)
        act = (so * phi).astype(BF16)
        dgelu = phi + so * e * 0.3989422804014327
        g = 0.5 * jnp.tanh(0.5 * jnp.dot(act, wg_scr[...], preferred_element_type=F32) + gbias) + 0.5
        gated = act.astype(F32) * g
        res = x_ref[at, :].astype(F32) + gated
        out_ref[at, :] = res.astype(BF16)
        leaving.append(pltpu.make_async_copy(out_ref.at[at, :], out_hbm.at[at, :], sems.at[i]))
        leaving[-1].start()
        err = res - t_ref[at, :].astype(F32)
        gr = err * wide(valid_ref[at, :], width // LANES)
        loss_acc = loss_acc + fold_rows(gr * err)
        gres_ref[at, :] = gr.astype(BF16)
        gg = gr * gated * (1.0 - g)
        gbias_acc = gbias_acc + fold_rows(gg)
        gl = gg.astype(BF16)
        add_to(gg_scr, i, tn_dot(act, gl))
        gssm = dgelu * (gr * g + nt_dot(gl, wg_scr[...]))
        gssm_ref[at, :] = gssm
        skip_acc = skip_acc + fold_rows(gssm * low_ref[at, :].astype(F32))
        ssl = gssm.astype(BF16)
        put(gs_ref, pad_at, 0, nt_dot(ssl, wc_scr[...]).astype(BF16).astype(F32))
        add_to(gc_scr, i, tn_dot(sl, ssl))
    clear_pads(gs_ref, seqs, pitch)
    sum_scr[0:1, :] = one_row(skip_acc)
    sum_scr[1:2, :] = one_row(gbias_acc)
    loss = jnp.sum(one_row(loss_acc), axis=1, keepdims=True)
    count = one_row(fold_rows(valid_ref[...]))

    def back(i, carry):
        j = steps - 1 - i
        out = []
        for s in range(seqs):
            yr, yi, q = carry[s]
            at = pl.ds(PAD + s * pitch + j, CHUNKS, stride=steps)
            lk = link_ref[at, :]
            lw = wide(lk, groups)
            nr, ni = cmul(ar, -ai, yr, yi)
            out.append((lw * (nr + take(gs_ref, at, 0, groups)), lw * (ni + take(gs_ref, at, groups, groups)), q * lk))
        return tuple(out)

    zero = jnp.zeros((CHUNKS, states), F32)
    init = tuple((zero, zero, jnp.ones((CHUNKS, LANES), F32)) for _ in range(seqs))
    firsts = run(steps - PAD, back, init, 8)
    ends = run(PAD, lambda i, c: back(i + steps - PAD, c), firsts, PAD)
    pr, pi = chunk_powers(ar, -ai, steps)
    for s in range(seqs):
        yr, yi, q = (jnp.where(top[:, : v.shape[1]] == 0, u, v) for u, v in zip(firsts[s], ends[s]))
        qw = wide(q, groups)
        sc = chunk_scan(pr * qw, pi * qw, yr, yi, True)
        for v in range(4):
            s2_ref[s * CHUNKS : (s + 1) * CHUNKS, v * states : (v + 1) * states] = sc[v]
        msg_ref[s : s + 1, :states] = sc[2][:1, :]
        msg_ref[s : s + 1, states : 2 * states] = sc[3][:1, :]
        msg_ref[s : s + 1, 2 * states :] = ids_ref[s : s + 1, :]

    for k, dst in enumerate((keep_ref, send_ref, keep_ref, send_ref)):
        q = w ^ k
        slot = q // 2
        dst[slot, :c_shard, :] = gc_scr[pl.ds(pl.multiple_of(q * c_shard, c_shard), c_shard), :].astype(BF16)
        lanes = pl.multiple_of(q * g_shard, g_shard)
        dst[slot, c_shard : c_shard + g_shard, :] = gg_scr[pl.ds(lanes, g_shard), :].astype(BF16)
        line = jnp.concatenate(
            [sum_scr[v : v + 1, pl.ds(lanes, g_shard)] for v in range(2)]
            + [jnp.broadcast_to(loss, (1, LANES)), count], axis=1)
        dst[slot, c_shard + g_shard :, :] = split_rows([jnp.zeros((3, width), F32), line])
    for copy in leaving:
        copy.wait()


def split16(v):
    high = v.astype(BF16)
    return high, (v - high.astype(F32)).astype(BF16)


def split_rows(lines):
    width = lines[0].shape[1]
    rows = sum(v.shape[0] for v in lines)
    v = jnp.concatenate(lines + [jnp.zeros((8 - rows, width), F32)] * (rows < 8), axis=0)
    high, rest = split16(v)
    return jnp.concatenate([high.astype(F32), rest.astype(F32)], axis=0).astype(BF16)


def k3_body(*refs, seqs, hops, blocks):
    (n_ref, link_ref, ids_ref, low_ref, proj_ref, state_ref, gs_ref, gssm_ref,
     s2_ref, rates_ref, vec_ref, w_full) = refs[:12]
    recvs = refs[12 : 12 + hops]
    (gn_ref, send_ref, keep_ref, gp_scr, gpl_scr, gb_scr, vec_scr) = refs[12 + hops :]
    rows, width = n_ref.shape
    states = rates_ref.shape[1]
    groups = states // LANES
    block_len = rows // seqs
    steps = block_len // CHUNKS + 1
    pitch = block_len + PAD
    shard = width // 4
    w = own_w()
    a1r, a1i = rates_ref[0:1, :], rates_ref[1:2, :]
    ar = jnp.broadcast_to(a1r, (CHUNKS, states))
    ai = jnp.broadcast_to(a1i, (CHUNKS, states))
    zr = jnp.broadcast_to(rates_ref[2:3, :], (CHUNKS, states))
    zi = jnp.broadcast_to(rates_ref[3:4, :], (CHUNKS, states))
    rowid = lax.broadcasted_iota(jnp.int32, (CHUNKS, states), 0)
    ids = ids_ref[...]
    rate_sums = [jnp.zeros((CHUNKS, states), F32) for _ in range(4)]
    for s in range(seqs):
        cr, ci = carry_in(recvs, ids, s, seqs + s, a1r, a1i, block_len, True, blocks - 1 - lax.axis_index("seq"))
        sc = [s2_ref[s * CHUNKS : (s + 1) * CHUNKS, v * states : (v + 1) * states] for v in range(4)]
        mr, mi = cmul(sc[0], sc[1], cr, ci)
        yr = jnp.where(rowid == CHUNKS - 1, cr, pltpu.roll(sc[2] + mr, CHUNKS - 1, 0))
        yi = jnp.where(rowid == CHUNKS - 1, ci, pltpu.roll(sc[3] + mi, CHUNKS - 1, 0))

        def step(i, carry):
            yr, yi, gar, gai, gsr, gsi = carry
            j = steps - 1 - i
            at = pl.ds(PAD + s * pitch + j, CHUNKS, stride=steps)
            before = pl.ds(PAD + s * pitch + j - 1, CHUNKS, stride=steps)
            lw = wide(link_ref[at, :], groups)
            nr, ni = cmul(ar, -ai, yr, yi)
            dr, di = nr + take(gs_ref, at, 0, groups), ni + take(gs_ref, at, groups, groups)
            yr, yi = lw * dr, lw * di
            pr, pi = take(proj_ref, at, 0, groups), take(proj_ref, at, groups, groups)
            ur, ui = take(state_ref, before, 0, groups), take(state_ref, before, groups, groups)
            put(gp_scr, at, 0, zr * dr + zi * di)
            put(gp_scr, at, groups, zr * di - zi * dr)
            return (
                yr, yi,
                gar + (ur * yr + ui * yi), gai + (ur * yi - ui * yr),
                gsr + (pr * dr + pi * di), gsi + (pr * di - pi * dr),
            )

        carry = run(steps - PAD, step, (yr, yi, *rate_sums), 8)
        yr, yi = (jnp.where(rowid == 0, 0.0, v) for v in carry[:2])
        carry = run(PAD, lambda i, c: step(i + steps - PAD, c), (yr, yi, *carry[2:]), PAD)
        rate_sums = list(carry[2:])

    skip = vec_ref[2:3, :]
    gain_acc = jnp.zeros((8, width), F32)
    bias_acc = jnp.zeros((8, width), F32)
    for i in range(rows // TILE):
        at = slice(i * TILE, (i + 1) * TILE)
        gpl = take(gp_scr, padded(i, block_len), 0, 2 * groups).astype(BF16)
        gpl_scr[at, :] = gpl
        gn = nt_dot(gpl, w_full[...]) + skip * gssm_ref[at, :]
        gn_ref[at, :] = gn.astype(BF16)
        gain_acc = gain_acc + fold_rows(gn * n_ref[at, :].astype(F32))
        bias_acc = bias_acc + fold_rows(gn)
    gb_scr[...] = tn_dot(low_ref[...], gpl_scr[...])
    sums4 = [one_row(v) for v in rate_sums]
    rate_grads = []
    for k in range(3):
        rate_grads.append(sum(rates_ref[8 + 3 * c + k : 9 + 3 * c + k, :] * sums4[c] for c in range(4)))
    vec_scr[0:1, :] = one_row(gain_acc)
    vec_scr[1:2, :] = one_row(bias_acc)
    extra = 3 * shard // 2
    half = shard // 2
    for k, dst in enumerate((keep_ref, send_ref, keep_ref, send_ref)):
        slot = (w ^ k) // 2
        q = pl.multiple_of((w ^ k) * shard, shard)
        dst[slot, :shard, :] = gb_scr[pl.ds(q, shard), :width].astype(BF16)
        dst[slot, shard:extra, : width // 2] = gb_scr[pl.ds(q, half), width:].astype(BF16)
        dst[slot, shard:extra, width // 2 :] = gb_scr[pl.ds(q + half, half), width:].astype(BF16)
        mine = [vec_scr[v : v + 1, pl.ds(q, shard)] for v in range(2)] + [jnp.zeros((1, shard), F32)]
        dst[slot, extra:, :] = split_rows([jnp.concatenate(p, axis=1) for p in zip(rate_grads, mine)])


def centre(values):
    x = values.astype(F32)
    c = x - jnp.mean(x, -1, keepdims=True)
    r = lax.rsqrt(jnp.mean(c * c, -1, keepdims=True) + 1e-05)
    return c * r, r


def sum_body(c0, c1, c2, c3, sum_ref):
    sum_ref[...] = total((c0, c1, c2, c3), slice(0, sum_ref.shape[0]))


def quarter_body(keep_ref, got_ref, *outs):
    half = outs[0].shape[0] - 16
    x, y = lax.axis_index("seq") % 2, lax.axis_index("wy")
    for out, slot, side in zip(outs, (y, 1 - y, y, 1 - y), (x, x, 1 - x, 1 - x)):
        def both(rows):
            return keep_ref[slot, rows, :].astype(F32) + got_ref[slot, rows, :].astype(F32)

        out[:half, :] = both(pl.ds(pl.multiple_of(side * half, half), half)).astype(BF16)
        v = both(slice(2 * half, 2 * half + 16))
        out[half:, :] = split_rows([v[:8] + v[8:]])


def total(refs, rows):
    return sum([r[rows, :].astype(F32) for r in refs[1:]], refs[0][rows, :].astype(F32))


def deal_body(*refs):
    n = len(refs) - 6
    bs, c_sum, outs, b_scr = refs[:4], refs[4], refs[5 : 5 + n], refs[5 + n]
    b_half, c_half = b_scr.shape[0], c_sum.shape[0] - 16
    b_part, c_part = b_half // n, c_half // n
    b_scr[...] = total(bs, slice(0, b_half))
    tail = total(bs, slice(b_half, b_half + 16)) + c_sum[c_half:, :]
    ends = split_rows([tail[:8] + tail[8:]]).astype(F32)
    for k, out in enumerate(outs):
        at = (lax.axis_index("seq") // 2) ^ k
        rows = [
            b_scr[pl.ds(pl.multiple_of(at * b_part, 8), b_part), :],
            c_sum[pl.ds(pl.multiple_of(at * c_part, 8), c_part), :],
            ends[:4], ends[8:12],
        ]
        out[...] = jnp.concatenate(rows, axis=0).astype(BF16)


def close_body(*refs):
    parts, (piece_ref, tail_ref) = refs[:-2], refs[-2:]
    bulk = piece_ref.shape[0]
    v = total(parts, slice(0, bulk + 8))
    piece_ref[...] = v[:bulk].astype(BF16)
    tail_ref[...] = jnp.concatenate([v[bulk : bulk + 4] + v[bulk + 4 :], jnp.zeros((4, v.shape[1]), F32)], axis=0)


def scale_of(tail, tokens):
    return tokens / tail[3:4, 3 * LANES : 3 * LANES + 1]


def norm_body(x_ref, gn_ref, gres_ref, vec_ref, ig_ref):
    gain = vec_ref[0:1, :]
    for i in range(x_ref.shape[0] // TILE):
        at = slice(i * TILE, (i + 1) * TILE)
        n, r = centre(x_ref[at, :])
        q = gn_ref[at, :].astype(F32) * gain
        back = (q - jnp.mean(q, -1, keepdims=True) - n * jnp.mean(q * n, -1, keepdims=True)) * r
        ig_ref[at, :] = (gres_ref[at, :].astype(F32) + back).astype(BF16)


def finish_body(tail_ref, ig_ref,
                out_ref, loss_ref, gain_ref, bias_ref, skip_ref, gate_ref, real_ref, imag_ref, step_ref, *, tokens):
    width = ig_ref.shape[1]
    states = width - gain_ref.shape[1]
    own = real_ref.shape[1]
    tail = tail_ref[...]
    scale = scale_of(tail, tokens)
    out_ref[...] = scale * ig_ref[...].astype(F32)
    scaled = tail * scale
    gain_ref[...] = scaled[0:1, states:]
    bias_ref[...] = scaled[1:2, states:]
    skip_ref[...] = scaled[3:4, :LANES]
    gate_ref[...] = scaled[3:4, LANES : 2 * LANES]
    loss_ref[...] = tail[3:4, 2 * LANES : 2 * LANES + 1] * scale * (1.0 / (tokens * width))
    rates = pltpu.roll(scaled[:, :states], states - lax.axis_index("seq") * own, 1)
    for k, ref in enumerate((real_ref, imag_ref, step_ref)):
        ref[...] = rates[k : k + 1, :own]


def unpack_body(tail_ref, *refs, tokens):
    pieces, (gb_hbm, gc_hbm, gg_hbm, b_scr, c_scr, sems) = refs[:-6], refs[-6:]
    scale = scale_of(tail_ref[...], tokens)
    S = len(pieces)
    b_rows, c_rows = b_scr.shape[0] // S, c_scr.shape[0] // S
    for k, piece in enumerate(pieces):
        s = lax.axis_index("seq") ^ k
        v = piece[...].astype(F32) * scale
        b_at = s % 2 * (b_scr.shape[0] // 2) + s // 2 * b_rows
        c_at = s % 2 * (c_scr.shape[0] // 2) + s // 2 * c_rows
        b_scr[pl.ds(pl.multiple_of(b_at, 8), b_rows), :] = v[:b_rows, :]
        c_scr[pl.ds(pl.multiple_of(c_at, 8), c_rows), :] = v[b_rows:, :]
    shard, cols = gb_hbm.shape
    width = b_scr.shape[1]
    half, c_shard = shard // 2, gc_hbm.shape[0]
    fetch([
        (c_scr.at[:c_shard, :], gc_hbm),
        (c_scr.at[c_shard:, :], gg_hbm),
        (b_scr.at[:shard, :], gb_hbm.at[:, :width]),
        (b_scr.at[shard:, : cols - width], gb_hbm.at[:half, width:]),
        (b_scr.at[shard:, cols - width :], gb_hbm.at[half:, width:]),
    ], sems)


def whole(n, far=()):
    return [pl.BlockSpec(memory_space=pltpu.HBM if i in far else pltpu.VMEM) for i in range(n)]


def call(body, outs, scratch, *args, us=1, limit=30, far=(), far_outs=(), copies=0):
    return pl.pallas_call(
        body,
        out_shape=[jax.ShapeDtypeStruct(*o) for o in outs],
        in_specs=whole(len(args), far),
        out_specs=whole(len(outs), far_outs),
        scratch_shapes=[pltpu.VMEM(*s) for s in scratch] + [pltpu.SemaphoreType.DMA((copies,))] * (copies > 0),
        compiler_params=pltpu.CompilerParams(vmem_limit_bytes=limit * MIB),
        cost_estimate=pl.CostEstimate(flops=us * 1_000_000_000, bytes_accessed=MIB, transcendentals=0),
    )(*args)


def per_device(inputs, teacher, segment_ids, valid_mask, ln_gain, ln_bias, b_weight, c_weight, skip_weight,
               glu_weight, glu_bias, lambda_real, lambda_imag, log_step):
    S = lax.axis_size("seq")
    s_at = lax.axis_index("seq")
    seqs, block_len, width = inputs.shape
    rows = seqs * block_len
    padded_rows = PAD + seqs * (block_len + PAD)
    length = S * block_len
    own = lambda_real.shape[0]
    states = own * S
    doc_most = {4096: 1024, 32768: 8192}.get(length, length)
    hops = min((doc_most - 2) // block_len + 1, S - 1)
    shard, c_shard, g_shard = b_weight.shape[0], c_weight.shape[0], glu_weight.shape[0]

    def swap(v, axis, bit=1, n=2):
        return lax.ppermute(v, axis, [(i, i ^ bit) for i in range(n)])

    def after(v, *others):
        return lax.optimization_barrier((v, *others))[0]

    b_msg, table = call(
        k0_body,
        [((shard + 16, b_weight.shape[1]), BF16), ((8, states), F32)],
        [(b_weight.shape, BF16), ((4, 1, shard), BF16), ((3, 1, own), F32), ((8, states), F32)],
        b_weight, *(v[None] for v in (ln_gain, ln_bias, skip_weight, glu_bias, lambda_real, lambda_imag, log_step)),
        far=range(8), copies=8, limit=60,
    )
    b_far = swap(b_msg, "wy")
    b_near = swap(b_msg, "wc")
    (c_msg,) = call(
        k0b_body,
        [((c_shard + g_shard, width), BF16)],
        [(c_weight.shape, BF16), (glu_weight.shape, BF16)],
        c_weight, glu_weight, far=range(2), copies=2, limit=4,
    )
    c_far = swap(after(c_msg, b_far), "wy")
    bit = 1
    while bit < S:
        radix = 4 if 4 * bit <= S else 2
        table = sum([swap(table, "seq", k * bit, S) for k in range(1, radix)], table)
        bit *= radix
    bs = (b_msg, b_near, b_far, swap(b_far, "wc"))

    x = inputs.reshape(rows, width)
    teach = teacher.reshape(rows, width)
    R = seqs * CHUNKS
    slab = (2 * states // LANES, padded_rows, LANES)
    msg_shape = ((seqs, 2 * states + LANES), F32)
    low, norm, proj, vec, w_full, s1, fwd, rates, link, valid, ids = call(
        functools.partial(k1_body, seqs=seqs),
        [((rows, width), BF16), ((rows, width), BF16), (slab, F32), ((8, width), F32), ((width, 2 * states), BF16),
         ((R, 4 * states), F32), msg_shape, ((24, states), F32),
         ((padded_rows, LANES), F32), ((rows, LANES), F32), ((2 * seqs, LANES), F32)],
        [],
        x, *bs, table, segment_ids, valid_mask, us=2, limit=8,
    )
    cs = (c_msg, swap(c_msg, "wc"), c_far, swap(after(c_far, fwd), "wc"))
    fwds = [lax.ppermute(fwd, "seq", [(i, (i + k) % S) for i in range(S)]) for k in range(1, hops + 1)]
    c_bulk = c_shard + g_shard
    out, state, gs, gres, gssm, s2, bwd, send_c, keep_c = call(
        functools.partial(k2_body, seqs=seqs, hops=hops),
        [((rows, width), BF16), (slab, F32), (slab, F32),
         ((rows, width), BF16), ((rows, width), F32), ((R, 4 * states), F32), msg_shape,
         ((2, c_bulk + 16, width), BF16), ((2, c_bulk + 16, width), BF16)],
        [((2 * states, width), BF16), ((width, width), BF16), ((2 * states, width), F32), ((width, width), F32),
         ((8, width), F32), ((rows, width), BF16)],
        x, teach, link, valid, ids, low, proj, s1, rates, vec, *cs, *fwds, us=10, limit=20, far_outs=(0,), copies=rows // TILE,
    )
    bwds = [lax.ppermute(bwd, "seq", [((i + k) % S, i) for i in range(S)]) for k in range(1, hops + 1)]
    def cross(v, flip_x, flip_y):
        return lax.ppermute(
            v, ("seq", "wy"), [(2 * a + b, 2 * (a ^ flip_x) + (b ^ flip_y)) for a in range(S) for b in range(2)])

    def quarters(keep, got):
        shape = ((keep.shape[1] - 16) // 2 + 16, width)
        return call(quarter_body, [(shape, BF16)] * 4, [], keep, got, limit=4)

    def exchange(q):
        return (q[0], cross(q[1], 0, 1), cross(q[2], 1, 0), cross(q[3], 1, 1))

    q_c = quarters(keep_c, swap(send_c, "wc"))
    bwds = lax.optimization_barrier((bwds, q_c))[0]
    part_c = exchange(q_c)
    b_bulk = 3 * shard // 2
    b_part, c_part = b_bulk // S, c_bulk // S
    gn, send_b, keep_b = call(
        functools.partial(k3_body, seqs=seqs, hops=hops, blocks=S),
        [((rows, width), BF16), ((2, b_bulk + 16, width), BF16), ((2, b_bulk + 16, width), BF16)],
        [(slab, F32), ((rows, 2 * states), BF16), ((width, 2 * states), F32), ((8, width), F32)],
        norm, link, ids, low, proj, state, gs, gssm, s2, rates, vec, w_full, *bwds, us=8, limit=14,
    )
    (c_sum,) = call(sum_body, [((c_bulk // 2 + 16, width), F32)], [], *part_c, limit=4)
    got_b = swap(after(send_b, part_c[3]), "wc")
    part_b = exchange(quarters(keep_b, got_b))
    (ig,) = call(norm_body, [((rows, width), BF16)], [], x, gn, gres, vec, us=3, limit=8)
    part_b, ig = lax.optimization_barrier((part_b, ig))
    tokens = float(length * seqs * lax.axis_size(("wy", "wc")))
    deal = S // 2
    if b_part % 8 == 0 and c_part % 8 == 0:
        dealt = call(
            deal_body, [((b_part + c_part + 8, width), BF16)] * deal,
            [((b_bulk // 2, width), F32)], *part_b, c_sum, limit=4,
        )
        parts = [dealt[0]] + [swap(dealt[k], "seq", 2 * k, S) for k in range(1, deal)]
        piece, tail = call(
            close_body, [((b_part + c_part, width), BF16), ((8, width), F32)], [], *parts, limit=4,
        )
        pieces = {0: piece}
        for k in range(1, deal):
            pieces[2 * k] = swap(piece, "seq", 2 * k, S)
        for k in range(deal):
            pieces[2 * k + 1] = swap(pieces[2 * k] if k else after(piece, pieces[2]), "seq", 1, S)
        pieces = [pieces[k] for k in range(S)]
    else:
        piece, tail, pieces = sum_by_all_to_all(part_b, c_sum, S, s_at)
    ingrad, loss, *lines = call(
        functools.partial(finish_body, tokens=tokens),
        [((rows, width), F32), ((1, 1), F32)] + [((1, shard), F32)] * 4 + [((1, own), F32)] * 3,
        [], tail, ig, limit=8,
    )
    gb, gc, gg = call(
        functools.partial(unpack_body, tokens=tokens),
        [((shard, 2 * states), F32), ((c_shard, width), F32), ((g_shard, width), F32)],
        [((b_bulk, width), F32), ((c_bulk, width), F32)],
        tail, *pieces, limit=8, far_outs=range(3), copies=5,
    )
    gain, bias, skip, gate, real, imag, step = (v[0] for v in lines)
    return (
        out.reshape(inputs.shape), loss[0, 0], ingrad.reshape(inputs.shape), gain, bias, gb, gc, skip, gg, gate,
        real, imag, step,
    )


def sum_by_all_to_all(part_b, v_c, S, s_at):
    v_b = sum([p.astype(F32) for p in part_b[1:]], part_b[0].astype(F32))
    width = v_b.shape[1]
    tail = v_b[-16:-8] + v_b[-8:] + v_c[-16:-8] + v_c[-8:]
    high = lax.reduce_precision(tail, 8, 7)
    ends = jnp.concatenate([high, tail - high], 0).astype(BF16)
    both = jnp.concatenate([v[:-16].astype(BF16).reshape(S // 2, -1, width) for v in (v_b, v_c)], 1)
    bulk = both.shape[1]
    both = jnp.concatenate([both, jnp.broadcast_to(ends[None], (S // 2, 16, width))], 1)
    empty = jnp.zeros_like(both)
    mine = (lax.iota(jnp.int32, S) % 2 == s_at % 2)[:, None, None]
    sent = jnp.where(mine, jnp.stack([both, both], 1).reshape(S, bulk + 16, width), jnp.stack([empty, empty], 1).reshape(S, bulk + 16, width))
    v = jnp.sum(lax.all_to_all(sent, "seq", 0, 0, tiled=True).astype(F32), 0)
    piece, tail = v[:bulk].astype(BF16), v[bulk : bulk + 8] + v[bulk + 8 :]
    back = lax.all_to_all(jnp.broadcast_to(piece[None], (S, bulk, width)), "seq", 0, 0, tiled=True)
    order = lax.iota(jnp.int32, S) ^ s_at
    return piece, tail, [lax.dynamic_index_in_dim(back, order[k], 0, keepdims=False) for k in range(S)]


def solution(mesh):
    sizes = mesh.devices.shape
    fine = Mesh(mesh.devices.reshape(sizes[0], 2, sizes[1] // 2), ("seq", "wy", "wc"))
    w = ("wy", "wc")
    tokens = P(w, "seq", None)
    return jax.shard_map(
        per_device,
        mesh=fine,
        in_specs=(
            tokens, tokens, P(w, "seq"), P(w, "seq"), P(w), P(w), P(w, None), P(w, None), P(w), P(w, None), P(w),
            P("seq"), P("seq"), P("seq"),
        ),
        out_specs=(
            tokens, P(), tokens, P(w), P(w), P(w, None), P(w, None), P(w), P(w, None), P(w),
            P("seq"), P("seq"), P("seq"),
        ),
        check_vma=False,
    )
```

```python
import functools

import jax
import jax.numpy as jnp
from jax import lax
from jax.experimental import pallas as pl
from jax.experimental.pallas import tpu as pltpu
from jax.sharding import Mesh
from jax.sharding import PartitionSpec as P

CHUNKS = 8
LANES = 128
TILE = 512
PAD = 8
MIB = 1024 * 1024
F32 = jnp.float32
BF16 = jnp.bfloat16


def small_expm1(x):
    return x * (1.0 + x / 2 * (1.0 + x / 3 * (1.0 + x / 4 * (1.0 + x / 5 * (1.0 + x / 6)))))


def rates_map(real_rate, imag_rate, log_rate):
    time_step = jnp.exp(log_rate)
    grow_re = real_rate * time_step
    turn_im = imag_rate * time_step
    growth = jnp.exp(grow_re)
    abar_re = growth * jnp.cos(turn_im)
    abar_im = growth * jnp.sin(turn_im)
    half_sine = jnp.sin(0.5 * turn_im)
    numer_re = small_expm1(grow_re) * jnp.cos(turn_im) - 2.0 * half_sine * half_sine
    divisor = real_rate * real_rate + imag_rate * imag_rate
    scale_re = (numer_re * real_rate + abar_im * imag_rate) / divisor
    scale_im = (abar_im * real_rate - numer_re * imag_rate) / divisor
    return (abar_re, abar_im, scale_re, scale_im)


def cmul(xr, xi, yr, yi):
    return xr * yr - xi * yi, xr * yi + xi * yr


def power2(xr, xi, times):
    for _ in range(times):
        xr, xi = xr * xr - xi * xi, 2.0 * xr * xi
    return xr, xi


def log2(n):
    return n.bit_length() - 1


def power(xr, xi, n):
    out = None
    while n:
        if n & 1:
            out = (xr, xi) if out is None else cmul(*out, xr, xi)
        n >>= 1
        if n:
            xr, xi = power2(xr, xi, 1)
    return out


def chunk_powers(ar, ai, steps):
    first = lax.broadcasted_iota(jnp.int32, ar.shape, 0) == 0
    sr, si = power(ar, ai, steps - PAD)
    pr, pi = power(ar, ai, steps)
    return jnp.where(first, sr, pr), jnp.where(first, si, pi)


def padded(i, block_len):
    start = i * TILE + PAD * (2 + i * TILE // block_len)
    return slice(start, start + TILE)


def add_to(ref, i, v):
    ref[...] = v if i == 0 else ref[...] + v


def run(count, body, carry, unroll):
    def block(k, c):
        for u in range(unroll):
            c = body(k * unroll + u, c)
        return c

    whole_blocks = count // unroll
    carry = lax.fori_loop(0, whole_blocks, block, carry)
    for i in range(whole_blocks * unroll, count):
        carry = body(i, carry)
    return carry


def wide(v, groups):
    return jnp.concatenate([v] * groups, axis=1)


def fold_rows(v):
    return jnp.sum(v.reshape(-1, 8, v.shape[-1]), axis=0)


def take(ref, at, first, count):
    return jnp.concatenate([ref[first + g, at, :] for g in range(count)], axis=1)


def put(ref, at, first, v):
    for g in range(v.shape[1] // LANES):
        ref[first + g, at, :] = v[:, g * LANES : (g + 1) * LANES]


def clear_pads(ref, seqs, pitch):
    for g in range(ref.shape[0]):
        ref[g, :PAD, :] = jnp.zeros((PAD, LANES), F32)
        for s in range(seqs):
            ref[g, PAD + s * pitch : 2 * PAD + s * pitch, :] = jnp.zeros((PAD, LANES), F32)


def own_w():
    return 2 * lax.axis_index("wy") + lax.axis_index("wc")


def one_row(v):
    return jnp.sum(v, axis=0, keepdims=True)


def nt_dot(a, b):
    return lax.dot_general(a, b, (((1,), (1,)), ((), ())), preferred_element_type=F32)


def tn_dot(a, b):
    return lax.dot_general(a, b, (((0,), (0,)), ((), ())), preferred_element_type=F32)


def chunk_scan(ar, ai, br, bi, reverse):
    rows = lax.broadcasted_iota(jnp.int32, ar.shape, 0)
    d = 1
    while d < CHUNKS:
        shift = (CHUNKS - d) if reverse else d
        keep = (rows < CHUNKS - d) if reverse else (rows >= d)
        pr, pi = pltpu.roll(ar, shift, 0), pltpu.roll(ai, shift, 0)
        qr, qi = pltpu.roll(br, shift, 0), pltpu.roll(bi, shift, 0)
        mr, mi = cmul(ar, ai, qr, qi)
        br, bi = jnp.where(keep, br + mr, br), jnp.where(keep, bi + mi, bi)
        mr, mi = cmul(ar, ai, pr, pi)
        ar, ai = jnp.where(keep, mr, ar), jnp.where(keep, mi, ai)
        d *= 2
    return ar, ai, br, bi


def carry_in(recvs, ids, s, own_row, ar, ai, block_len, conj, blocks):
    states = ar.shape[1]
    pr, pi = power2(ar, -ai if conj else ai, log2(block_len))
    cr = jnp.zeros((1, states), F32)
    ci = jnp.zeros((1, states), F32)
    own = wide(ids[own_row : own_row + 1, :], states // LANES)
    for k in range(len(recvs), 0, -1):
        msg = recvs[k - 1][s : s + 1, :]
        same = (wide(msg[:, 2 * states :], states // LANES) == own) & (blocks >= k)
        cr, ci = cmul(pr, pi, cr, ci)
        cr = cr + jnp.where(same, msg[:, :states], 0.0)
        ci = ci + jnp.where(same, msg[:, states : 2 * states], 0.0)
    return cr, ci


def fetch(pairs, sems):
    copies = [pltpu.make_async_copy(src, dst, sems.at[k]) for k, (src, dst) in enumerate(pairs)]
    for c in copies:
        c.start()
    for c in copies:
        c.wait()


def k0_body(b_ref, g_ref, n_ref, s_ref, q_ref, lr_ref, li_ref, ls_ref, msg_ref, table_ref,
            b_scr, v_scr, l_scr, scr, sems):
    shard, cols = b_scr.shape
    own = lr_ref.shape[1]
    fetch(
        [(b_ref, b_scr)]
        + [(r, v_scr.at[k]) for k, r in enumerate((g_ref, n_ref, s_ref, q_ref))]
        + [(r, l_scr.at[k]) for k, r in enumerate((lr_ref, li_ref, ls_ref))],
        sems,
    )
    msg_ref[:shard, :] = b_scr[...]
    line = jnp.concatenate([v_scr[k] for k in range(4)] + [jnp.zeros((1, cols - 4 * shard), BF16)], axis=1)
    msg_ref[shard:, :] = jnp.broadcast_to(line, (16, cols))
    scr[...] = jnp.zeros_like(scr)
    for k in range(3):
        scr[k : k + 1, :own] = l_scr[k]
    table_ref[...] = pltpu.roll(scr[...], lax.axis_index("seq") * own, 1)


def k0b_body(c_ref, g_ref, msg_ref, c_scr, g_scr, sems):
    c_shard = c_ref.shape[0]
    fetch([(c_ref, c_scr), (g_ref, g_scr)], sems)
    msg_ref[:c_shard, :] = c_scr[...]
    msg_ref[c_shard:, :] = g_scr[...]


def lay_marks(seg_ref, mask_ref, link_ref, valid_ref, ids_ref):
    seqs, block_len = seg_ref.shape
    seg = seg_ref[...].astype(F32)
    link_ref[:PAD, :] = jnp.ones((PAD, LANES), F32)
    lane = lax.broadcasted_iota(jnp.int32, (1, block_len), 1)
    for s in range(seqs):
        row = seg[s : s + 1, :]
        link = jnp.where((row == pltpu.roll(row, 1, 1)) | (lane == 0), 1.0, 0.0)
        mask = mask_ref[s : s + 1, :].astype(F32)
        start = PAD + s * (block_len + PAD)
        link_ref[start : start + PAD, :] = jnp.ones((PAD, LANES), F32)
        for src, dst, start in ((link, link_ref, start + PAD), (mask, valid_ref, s * block_len)):
            for k in range(block_len // LANES):
                piece = jnp.broadcast_to(src[:, k * LANES : (k + 1) * LANES], (LANES, LANES))
                at = start + k * LANES
                dst[at : at + LANES, :] = jnp.transpose(piece)
        ids_ref[s : s + 1, :] = jnp.broadcast_to(row[:, :1], (1, LANES))
        ids_ref[seqs + s : seqs + s + 1, :] = jnp.broadcast_to(row[:, block_len - 1 :], (1, LANES))


def k1_body(x_ref, b0, b1, b2, b3, table_ref, seg_ref, mask_ref,
            low_ref, n_ref, proj_ref, vec_ref, full_ref, s1_ref, msg_ref, rates_ref, link_ref, valid_ref, ids_ref, *, seqs):
    rows, width = x_ref.shape
    shard = b0.shape[0] - 16
    block_len = rows // seqs
    pitch = block_len + PAD
    w = own_w()
    for k, piece in enumerate((b0, b1, b2, b3)):
        at = pl.multiple_of((w ^ k) * shard, shard)
        full_ref[pl.ds(at, shard), :] = piece[:shard, :]
        extra = piece[shard:, :].astype(F32)
        for v in range(4):
            vec_ref[v : v + 1, pl.ds(at, shard)] = extra[0:1, v * shard : (v + 1) * shard]
    vec_ref[4:8, :] = jnp.zeros((4, width), F32)
    gain = vec_ref[0:1, :]
    bias = vec_ref[1:2, :]
    for i in range(rows // TILE):
        at = slice(i * TILE, (i + 1) * TILE)
        n = centre(x_ref[at, :])[0]
        n_ref[at, :] = n.astype(BF16)
        low = (n * gain + bias).astype(BF16)
        low_ref[at, :] = low
        p = jnp.dot(low, full_ref[...], preferred_element_type=F32)
        put(proj_ref, padded(i, block_len), 0, p.astype(BF16).astype(F32))
    clear_pads(proj_ref, seqs, pitch)
    lay_marks(seg_ref, mask_ref, link_ref, valid_ref, ids_ref)
    states = table_ref.shape[1]
    groups = states // LANES
    steps = block_len // CHUNKS + 1
    lam = [table_ref[v : v + 1, :] for v in range(3)]
    parts, back = jax.vjp(rates_map, *lam)
    one, zero = jnp.ones_like(lam[0]), jnp.zeros_like(lam[0])
    for v in range(4):
        rates_ref[v : v + 1, :] = parts[v]
        for k, jac in enumerate(back(tuple(one if i == v else zero for i in range(4)))):
            rates_ref[8 + 3 * v + k : 9 + 3 * v + k, :] = jac
    rates_ref[4:8, :] = jnp.zeros((4, states), F32)
    rates_ref[20:24, :] = jnp.zeros((4, states), F32)
    ar = jnp.broadcast_to(parts[0], (CHUNKS, states))
    ai = jnp.broadcast_to(parts[1], (CHUNKS, states))

    def step(j, carry):
        out = []
        for s in range(seqs):
            ur, ui, q = carry[s]
            at = pl.ds(PAD + s * pitch + j, CHUNKS, stride=steps)
            lk = link_ref[at, :]
            lw = wide(lk, groups)
            nr, ni = cmul(ar, ai, ur, ui)
            out.append((lw * nr + take(proj_ref, at, 0, groups), lw * ni + take(proj_ref, at, groups, groups), q * lk))
        return tuple(out)

    zero = jnp.zeros((CHUNKS, states), F32)
    init = tuple((zero, zero, jnp.ones((CHUNKS, LANES), F32)) for _ in range(seqs))
    ends = run(steps, step, init, 13)
    pr, pi = chunk_powers(ar, ai, steps)
    for s in range(seqs):
        ur, ui, q = ends[s]
        qw = wide(q, groups)
        sc = chunk_scan(pr * qw, pi * qw, ur, ui, False)
        for v in range(4):
            s1_ref[s * CHUNKS : (s + 1) * CHUNKS, v * states : (v + 1) * states] = sc[v]
        msg_ref[s : s + 1, :states] = sc[2][CHUNKS - 1 :, :]
        msg_ref[s : s + 1, states : 2 * states] = sc[3][CHUNKS - 1 :, :]
        msg_ref[s : s + 1, 2 * states :] = ids_ref[seqs + s : seqs + s + 1, :]


def k2_body(*refs, seqs, hops):
    (x_ref, t_ref, link_ref, valid_ref, ids_ref, low_ref, proj_ref, s1_ref, rates_ref, vec_ref,
     c0, c1, c2, c3) = refs[:14]
    recvs = refs[14 : 14 + hops]
    (out_hbm, state_ref, gs_ref, gres_ref, gssm_ref, s2_ref, msg_ref, send_ref, keep_ref, sums_ref,
     wc_scr, wg_scr, gc_scr, gg_scr, out_ref, sems) = refs[14 + hops :]
    rows, width = x_ref.shape
    states = rates_ref.shape[1]
    groups = states // LANES
    block_len = rows // seqs
    steps = block_len // CHUNKS + 1
    pitch = block_len + PAD
    g_shard = width // 4
    c_shard = 2 * states // 4
    w = own_w()
    for k, piece in enumerate((c0, c1, c2, c3)):
        wc_scr[pl.ds(pl.multiple_of((w ^ k) * c_shard, c_shard), c_shard), :] = piece[:c_shard, :]
        wg_scr[pl.ds(pl.multiple_of((w ^ k) * g_shard, g_shard), g_shard), :] = piece[c_shard:, :]
    a1r, a1i = rates_ref[0:1, :], rates_ref[1:2, :]
    ar = jnp.broadcast_to(a1r, (CHUNKS, states))
    ai = jnp.broadcast_to(a1i, (CHUNKS, states))
    zr = jnp.broadcast_to(rates_ref[2:3, :], (CHUNKS, states))
    zi = jnp.broadcast_to(rates_ref[3:4, :], (CHUNKS, states))
    top = lax.broadcasted_iota(jnp.int32, (CHUNKS, states), 0)
    ids = ids_ref[...]
    init, carries = [], []
    for s in range(seqs):
        cr, ci = carry_in(recvs, ids, s, s, a1r, a1i, block_len, False, lax.axis_index("seq"))
        sc = [s1_ref[s * CHUNKS : (s + 1) * CHUNKS, v * states : (v + 1) * states] for v in range(4)]
        mr, mi = cmul(sc[0], sc[1], cr, ci)
        init.append((pltpu.roll(sc[2] + mr, 1, 0), pltpu.roll(sc[3] + mi, 1, 0)))
        carries.append((cr, ci))

    def step(j, carry):
        out = []
        for s in range(seqs):
            ur, ui = carry[s]
            at = pl.ds(PAD + s * pitch + j, CHUNKS, stride=steps)
            lw = wide(link_ref[at, :], groups)
            nr, ni = cmul(ar, ai, ur, ui)
            ur, ui = lw * nr + take(proj_ref, at, 0, groups), lw * ni + take(proj_ref, at, groups, groups)
            sr, si = cmul(zr, zi, ur, ui)
            put(state_ref, at, 0, sr)
            put(state_ref, at, groups, si)
            out.append((ur, ui))
        return tuple(out)

    for g in range(2 * groups):
        state_ref[g, :PAD, :] = jnp.zeros((PAD, LANES), F32)
    entry = list(run(PAD, step, tuple(init), PAD))
    for s in range(seqs):
        ur, ui = (jnp.where(top == 0, c, u) for c, u in zip(carries[s], entry[s]))
        sr, si = cmul(zr, zi, ur, ui)
        at = pl.ds(PAD + s * pitch + PAD - 1, CHUNKS, stride=steps)
        put(state_ref, at, 0, sr)
        put(state_ref, at, groups, si)
        entry[s] = (ur, ui)
    run(steps - PAD, lambda i, c: step(i + PAD, c), tuple(entry), 8)

    skip = vec_ref[2:3, :]
    gbias = 0.5 * vec_ref[3:4, :]
    leaving = []
    loss_acc = jnp.zeros((8, width), F32)
    gbias_acc = jnp.zeros((8, width), F32)
    skip_acc = jnp.zeros((8, width), F32)
    for i in range(rows // TILE):
        at = slice(i * TILE, (i + 1) * TILE)
        pad_at = padded(i, block_len)
        sl = take(state_ref, pad_at, 0, 2 * groups).astype(BF16)
        so = jnp.dot(sl, wc_scr[...], preferred_element_type=F32) + skip * low_ref[at, :].astype(F32)
        e = jnp.exp2(so * so * -0.7213475204444817)
        t = 1.0 / (1.0 + 0.23164189 * jnp.abs(so))
        tail = e * t * (0.127414796 + t * (-0.142248368 + t * (0.7107068705 + t * (-0.7265760135 + t * 0.5307027145))))
        phi = jnp.where(so >= 0.0, 1.0 - tail, tail)
        act = (so * phi).astype(BF16)
        dgelu = phi + so * e * 0.3989422804014327
        g = 0.5 * jnp.tanh(0.5 * jnp.dot(act, wg_scr[...], preferred_element_type=F32) + gbias) + 0.5
        gated = act.astype(F32) * g
        res = x_ref[at, :].astype(F32) + gated
        out_ref[at, :] = res.astype(BF16)
        leaving.append(pltpu.make_async_copy(out_ref.at[at, :], out_hbm.at[at, :], sems.at[i]))
        leaving[-1].start()
        err = res - t_ref[at, :].astype(F32)
        gr = err * wide(valid_ref[at, :], width // LANES)
        loss_acc = loss_acc + fold_rows(gr * err)
        gres_ref[at, :] = gr.astype(BF16)
        gg = gr * gated * (1.0 - g)
        gbias_acc = gbias_acc + fold_rows(gg)
        gl = gg.astype(BF16)
        add_to(gg_scr, i, tn_dot(act, gl))
        gssm = dgelu * (gr * g + nt_dot(gl, wg_scr[...]))
        gssm_ref[at, :] = gssm
        skip_acc = skip_acc + fold_rows(gssm * low_ref[at, :].astype(F32))
        ssl = gssm.astype(BF16)
        put(gs_ref, pad_at, 0, nt_dot(ssl, wc_scr[...]).astype(BF16).astype(F32))
        add_to(gc_scr, i, tn_dot(sl, ssl))
    clear_pads(gs_ref, seqs, pitch)
    sums_ref[0:1, :] = one_row(skip_acc)
    sums_ref[1:2, :] = one_row(gbias_acc)
    sums_ref[2:3, :] = jnp.broadcast_to(jnp.sum(one_row(loss_acc), axis=1, keepdims=True), (1, width))
    sums_ref[3:4, :] = wide(one_row(fold_rows(valid_ref[...])), width // LANES)
    sums_ref[4:8, :] = jnp.zeros((4, width), F32)

    def back(i, carry):
        j = steps - 1 - i
        out = []
        for s in range(seqs):
            yr, yi, q = carry[s]
            at = pl.ds(PAD + s * pitch + j, CHUNKS, stride=steps)
            lk = link_ref[at, :]
            lw = wide(lk, groups)
            nr, ni = cmul(ar, -ai, yr, yi)
            out.append((lw * (nr + take(gs_ref, at, 0, groups)), lw * (ni + take(gs_ref, at, groups, groups)), q * lk))
        return tuple(out)

    zero = jnp.zeros((CHUNKS, states), F32)
    init = tuple((zero, zero, jnp.ones((CHUNKS, LANES), F32)) for _ in range(seqs))
    firsts = run(steps - PAD, back, init, 8)
    ends = run(PAD, lambda i, c: back(i + steps - PAD, c), firsts, PAD)
    pr, pi = chunk_powers(ar, -ai, steps)
    for s in range(seqs):
        yr, yi, q = (jnp.where(top[:, : v.shape[1]] == 0, u, v) for u, v in zip(firsts[s], ends[s]))
        qw = wide(q, groups)
        sc = chunk_scan(pr * qw, pi * qw, yr, yi, True)
        for v in range(4):
            s2_ref[s * CHUNKS : (s + 1) * CHUNKS, v * states : (v + 1) * states] = sc[v]
        msg_ref[s : s + 1, :states] = sc[2][:1, :]
        msg_ref[s : s + 1, states : 2 * states] = sc[3][:1, :]
        msg_ref[s : s + 1, 2 * states :] = ids_ref[s : s + 1, :]

    for k, dst in enumerate((keep_ref, send_ref, keep_ref, send_ref)):
        q = w ^ k
        slot = q // 2
        dst[slot, :c_shard, :] = gc_scr[pl.ds(pl.multiple_of(q * c_shard, c_shard), c_shard), :].astype(BF16)
        lanes = pl.multiple_of(q * g_shard, g_shard)
        dst[slot, c_shard : c_shard + g_shard, :] = gg_scr[pl.ds(lanes, g_shard), :].astype(BF16)
    for copy in leaving:
        copy.wait()


def split16(v):
    high = v.astype(BF16)
    return high, (v - high.astype(F32)).astype(BF16)


def split_rows(lines):
    width = lines[0].shape[1]
    rows = sum(v.shape[0] for v in lines)
    v = jnp.concatenate(lines + [jnp.zeros((8 - rows, width), F32)] * (rows < 8), axis=0)
    high, rest = split16(v)
    return jnp.concatenate([high.astype(F32), rest.astype(F32)], axis=0).astype(BF16)


def k3_body(*refs, seqs, hops, blocks):
    (n_ref, sums_ref, link_ref, ids_ref, low_ref, proj_ref, state_ref, gs_ref, gssm_ref,
     s2_ref, rates_ref, vec_ref, w_full) = refs[:13]
    recvs = refs[13 : 13 + hops]
    (gn_ref, send_ref, keep_ref, gp_scr, gpl_scr, gb_scr, vec_scr) = refs[13 + hops :]
    rows, width = n_ref.shape
    states = rates_ref.shape[1]
    groups = states // LANES
    block_len = rows // seqs
    steps = block_len // CHUNKS + 1
    pitch = block_len + PAD
    shard = width // 4
    w = own_w()
    a1r, a1i = rates_ref[0:1, :], rates_ref[1:2, :]
    ar = jnp.broadcast_to(a1r, (CHUNKS, states))
    ai = jnp.broadcast_to(a1i, (CHUNKS, states))
    zr = jnp.broadcast_to(rates_ref[2:3, :], (CHUNKS, states))
    zi = jnp.broadcast_to(rates_ref[3:4, :], (CHUNKS, states))
    rowid = lax.broadcasted_iota(jnp.int32, (CHUNKS, states), 0)
    ids = ids_ref[...]
    rate_sums = [jnp.zeros((CHUNKS, states), F32) for _ in range(4)]
    for s in range(seqs):
        cr, ci = carry_in(recvs, ids, s, seqs + s, a1r, a1i, block_len, True, blocks - 1 - lax.axis_index("seq"))
        sc = [s2_ref[s * CHUNKS : (s + 1) * CHUNKS, v * states : (v + 1) * states] for v in range(4)]
        mr, mi = cmul(sc[0], sc[1], cr, ci)
        yr = jnp.where(rowid == CHUNKS - 1, cr, pltpu.roll(sc[2] + mr, CHUNKS - 1, 0))
        yi = jnp.where(rowid == CHUNKS - 1, ci, pltpu.roll(sc[3] + mi, CHUNKS - 1, 0))

        def step(i, carry):
            yr, yi, gar, gai, gsr, gsi = carry
            j = steps - 1 - i
            at = pl.ds(PAD + s * pitch + j, CHUNKS, stride=steps)
            before = pl.ds(PAD + s * pitch + j - 1, CHUNKS, stride=steps)
            lw = wide(link_ref[at, :], groups)
            nr, ni = cmul(ar, -ai, yr, yi)
            dr, di = nr + take(gs_ref, at, 0, groups), ni + take(gs_ref, at, groups, groups)
            yr, yi = lw * dr, lw * di
            pr, pi = take(proj_ref, at, 0, groups), take(proj_ref, at, groups, groups)
            ur, ui = take(state_ref, before, 0, groups), take(state_ref, before, groups, groups)
            put(gp_scr, at, 0, zr * dr + zi * di)
            put(gp_scr, at, groups, zr * di - zi * dr)
            return (
                yr, yi,
                gar + (ur * yr + ui * yi), gai + (ur * yi - ui * yr),
                gsr + (pr * dr + pi * di), gsi + (pr * di - pi * dr),
            )

        carry = run(steps - PAD, step, (yr, yi, *rate_sums), 8)
        yr, yi = (jnp.where(rowid == 0, 0.0, v) for v in carry[:2])
        carry = run(PAD, lambda i, c: step(i + steps - PAD, c), (yr, yi, *carry[2:]), PAD)
        rate_sums = list(carry[2:])

    skip = vec_ref[2:3, :]
    gain_acc = jnp.zeros((8, width), F32)
    bias_acc = jnp.zeros((8, width), F32)
    for i in range(rows // TILE):
        at = slice(i * TILE, (i + 1) * TILE)
        gpl = take(gp_scr, padded(i, block_len), 0, 2 * groups).astype(BF16)
        gpl_scr[at, :] = gpl
        gn = nt_dot(gpl, w_full[...]) + skip * gssm_ref[at, :]
        gn_ref[at, :] = gn.astype(BF16)
        gain_acc = gain_acc + fold_rows(gn * n_ref[at, :].astype(F32))
        bias_acc = bias_acc + fold_rows(gn)
    gb_scr[...] = tn_dot(low_ref[...], gpl_scr[...])
    sums4 = [one_row(v) for v in rate_sums]
    rate_grads = []
    for k in range(3):
        rate_grads.append(sum(rates_ref[8 + 3 * c + k : 9 + 3 * c + k, :] * sums4[c] for c in range(4)))
    vec_scr[0:1, :] = one_row(gain_acc)
    vec_scr[1:2, :] = one_row(bias_acc)
    extra = 3 * shard // 2
    half = shard // 2
    for k, dst in enumerate((keep_ref, send_ref, keep_ref, send_ref)):
        slot = (w ^ k) // 2
        q = pl.multiple_of((w ^ k) * shard, shard)
        dst[slot, :shard, :] = gb_scr[pl.ds(q, shard), :width].astype(BF16)
        dst[slot, shard:extra, : width // 2] = gb_scr[pl.ds(q, half), width:].astype(BF16)
        dst[slot, shard:extra, width // 2 :] = gb_scr[pl.ds(q + half, half), width:].astype(BF16)
        mine = [vec_scr[v : v + 1, pl.ds(q, shard)] for v in range(2)] + [jnp.zeros((1, shard), F32)]
        others = [sums_ref[v : v + 1, pl.ds(q, shard)] for v in range(2)] + [sums_ref[v : v + 1, :shard] for v in (2, 3)]
        lines = [jnp.concatenate(p, axis=1) for p in [*zip(rate_grads, mine), others]]
        dst[slot, extra:, :] = split_rows(lines)


def centre(values):
    x = values.astype(F32)
    c = x - jnp.mean(x, -1, keepdims=True)
    r = lax.rsqrt(jnp.mean(c * c, -1, keepdims=True) + 1e-05)
    return c * r, r


def sum_body(c0, c1, c2, c3, sum_ref):
    sum_ref[...] = total((c0, c1, c2, c3), slice(0, sum_ref.shape[0]))


def quarter_body(keep_ref, got_ref, *outs, extra):
    half = outs[0].shape[0] - extra
    x, y = lax.axis_index("seq") % 2, lax.axis_index("wy")
    for out, slot, side in zip(outs, (y, 1 - y, y, 1 - y), (x, x, 1 - x, 1 - x)):
        def both(rows):
            return keep_ref[slot, rows, :].astype(F32) + got_ref[slot, rows, :].astype(F32)

        out[:half, :] = both(pl.ds(pl.multiple_of(side * half, half), half)).astype(BF16)
        if extra:
            v = both(slice(2 * half, 2 * half + 16))
            out[half:, :] = split_rows([v[:8] + v[8:]])


def total(refs, rows):
    return sum([r[rows, :].astype(F32) for r in refs[1:]], refs[0][rows, :].astype(F32))


def deal_body(*refs):
    n = len(refs) - 6
    bs, c_sum, outs, b_scr = refs[:4], refs[4], refs[5 : 5 + n], refs[5 + n]
    b_half, c_half = b_scr.shape[0], c_sum.shape[0]
    b_part, c_part = b_half // n, c_half // n
    b_scr[...] = total(bs, slice(0, b_half))
    tail = total(bs, slice(b_half, b_half + 16))
    ends = split_rows([tail[:8] + tail[8:]]).astype(F32)
    for k, out in enumerate(outs):
        at = (lax.axis_index("seq") // 2) ^ k
        rows = [
            b_scr[pl.ds(pl.multiple_of(at * b_part, 8), b_part), :],
            c_sum[pl.ds(pl.multiple_of(at * c_part, 8), c_part), :],
            ends[:4], ends[8:12],
        ]
        out[...] = jnp.concatenate(rows, axis=0).astype(BF16)


def close_body(*refs):
    parts, (piece_ref, tail_ref) = refs[:-2], refs[-2:]
    bulk = piece_ref.shape[0]
    v = total(parts, slice(0, bulk + 8))
    piece_ref[...] = v[:bulk].astype(BF16)
    tail_ref[...] = jnp.concatenate([v[bulk : bulk + 4] + v[bulk + 4 :], jnp.zeros((4, v.shape[1]), F32)], axis=0)


def scale_of(tail, tokens):
    return tokens / tail[3:4, 3 * LANES : 3 * LANES + 1]


def norm_body(x_ref, gn_ref, gres_ref, vec_ref, ig_ref):
    gain = vec_ref[0:1, :]
    for i in range(x_ref.shape[0] // TILE):
        at = slice(i * TILE, (i + 1) * TILE)
        n, r = centre(x_ref[at, :])
        q = gn_ref[at, :].astype(F32) * gain
        back = (q - jnp.mean(q, -1, keepdims=True) - n * jnp.mean(q * n, -1, keepdims=True)) * r
        ig_ref[at, :] = (gres_ref[at, :].astype(F32) + back).astype(BF16)


def finish_body(tail_ref, ig_ref,
                out_ref, loss_ref, gain_ref, bias_ref, skip_ref, gate_ref, real_ref, imag_ref, step_ref, *, tokens):
    width = ig_ref.shape[1]
    states = width - gain_ref.shape[1]
    own = real_ref.shape[1]
    tail = tail_ref[...]
    scale = scale_of(tail, tokens)
    out_ref[...] = scale * ig_ref[...].astype(F32)
    scaled = tail * scale
    gain_ref[...] = scaled[0:1, states:]
    bias_ref[...] = scaled[1:2, states:]
    skip_ref[...] = scaled[3:4, :LANES]
    gate_ref[...] = scaled[3:4, LANES : 2 * LANES]
    loss_ref[...] = tail[3:4, 2 * LANES : 2 * LANES + 1] * scale * (1.0 / (tokens * width))
    rates = pltpu.roll(scaled[:, :states], states - lax.axis_index("seq") * own, 1)
    for k, ref in enumerate((real_ref, imag_ref, step_ref)):
        ref[...] = rates[k : k + 1, :own]


def unpack_body(tail_ref, *refs, tokens):
    pieces, (gb_hbm, gc_hbm, gg_hbm, b_scr, c_scr, sems) = refs[:-6], refs[-6:]
    scale = scale_of(tail_ref[...], tokens)
    S = len(pieces)
    b_rows, c_rows = b_scr.shape[0] // S, c_scr.shape[0] // S
    for k, piece in enumerate(pieces):
        s = lax.axis_index("seq") ^ k
        v = piece[...].astype(F32) * scale
        b_at = s % 2 * (b_scr.shape[0] // 2) + s // 2 * b_rows
        c_at = s % 2 * (c_scr.shape[0] // 2) + s // 2 * c_rows
        b_scr[pl.ds(pl.multiple_of(b_at, 8), b_rows), :] = v[:b_rows, :]
        c_scr[pl.ds(pl.multiple_of(c_at, 8), c_rows), :] = v[b_rows:, :]
    shard, cols = gb_hbm.shape
    width = b_scr.shape[1]
    half, c_shard = shard // 2, gc_hbm.shape[0]
    fetch([
        (c_scr.at[:c_shard, :], gc_hbm),
        (c_scr.at[c_shard:, :], gg_hbm),
        (b_scr.at[:shard, :], gb_hbm.at[:, :width]),
        (b_scr.at[shard:, : cols - width], gb_hbm.at[:half, width:]),
        (b_scr.at[shard:, cols - width :], gb_hbm.at[half:, width:]),
    ], sems)


def whole(n, far=()):
    return [pl.BlockSpec(memory_space=pltpu.HBM if i in far else pltpu.VMEM) for i in range(n)]


def call(body, outs, scratch, *args, us=1, limit=30, far=(), far_outs=(), copies=0):
    return pl.pallas_call(
        body,
        out_shape=[jax.ShapeDtypeStruct(*o) for o in outs],
        in_specs=whole(len(args), far),
        out_specs=whole(len(outs), far_outs),
        scratch_shapes=[pltpu.VMEM(*s) for s in scratch] + [pltpu.SemaphoreType.DMA((copies,))] * (copies > 0),
        compiler_params=pltpu.CompilerParams(vmem_limit_bytes=limit * MIB),
        cost_estimate=pl.CostEstimate(flops=us * 1_000_000_000, bytes_accessed=MIB, transcendentals=0),
    )(*args)


def per_device(inputs, teacher, segment_ids, valid_mask, ln_gain, ln_bias, b_weight, c_weight, skip_weight,
               glu_weight, glu_bias, lambda_real, lambda_imag, log_step):
    S = lax.axis_size("seq")
    s_at = lax.axis_index("seq")
    seqs, block_len, width = inputs.shape
    rows = seqs * block_len
    padded_rows = PAD + seqs * (block_len + PAD)
    length = S * block_len
    own = lambda_real.shape[0]
    states = own * S
    doc_most = {4096: 1024, 32768: 8192}.get(length, length)
    hops = min((doc_most - 2) // block_len + 1, S - 1)
    shard, c_shard, g_shard = b_weight.shape[0], c_weight.shape[0], glu_weight.shape[0]

    def swap(v, axis, bit=1, n=2):
        return lax.ppermute(v, axis, [(i, i ^ bit) for i in range(n)])

    def after(v, *others):
        return lax.optimization_barrier((v, *others))[0]

    b_msg, table = call(
        k0_body,
        [((shard + 16, b_weight.shape[1]), BF16), ((8, states), F32)],
        [(b_weight.shape, BF16), ((4, 1, shard), BF16), ((3, 1, own), F32), ((8, states), F32)],
        b_weight, *(v[None] for v in (ln_gain, ln_bias, skip_weight, glu_bias, lambda_real, lambda_imag, log_step)),
        far=range(8), copies=8, limit=60,
    )
    b_far = swap(b_msg, "wy")
    b_near = swap(b_msg, "wc")
    (c_msg,) = call(
        k0b_body,
        [((c_shard + g_shard, width), BF16)],
        [(c_weight.shape, BF16), (glu_weight.shape, BF16)],
        c_weight, glu_weight, far=range(2), copies=2, limit=4,
    )
    c_far = swap(after(c_msg, b_far), "wy")
    bit = 1
    while bit < S:
        radix = 4 if 4 * bit <= S else 2
        table = sum([swap(table, "seq", k * bit, S) for k in range(1, radix)], table)
        bit *= radix
    bs = (b_msg, b_near, b_far, swap(b_far, "wc"))

    x = inputs.reshape(rows, width)
    teach = teacher.reshape(rows, width)
    R = seqs * CHUNKS
    slab = (2 * states // LANES, padded_rows, LANES)
    msg_shape = ((seqs, 2 * states + LANES), F32)
    low, norm, proj, vec, w_full, s1, fwd, rates, link, valid, ids = call(
        functools.partial(k1_body, seqs=seqs),
        [((rows, width), BF16), ((rows, width), BF16), (slab, F32), ((8, width), F32), ((width, 2 * states), BF16),
         ((R, 4 * states), F32), msg_shape, ((24, states), F32),
         ((padded_rows, LANES), F32), ((rows, LANES), F32), ((2 * seqs, LANES), F32)],
        [],
        x, *bs, table, segment_ids, valid_mask, us=2, limit=8,
    )
    cs = (c_msg, swap(c_msg, "wc"), c_far, swap(after(c_far, fwd), "wc"))
    fwds = [lax.ppermute(fwd, "seq", [(i, (i + k) % S) for i in range(S)]) for k in range(1, hops + 1)]
    c_bulk = c_shard + g_shard
    out, state, gs, gres, gssm, s2, bwd, send_c, keep_c, sums = call(
        functools.partial(k2_body, seqs=seqs, hops=hops),
        [((rows, width), BF16), (slab, F32), (slab, F32),
         ((rows, width), BF16), ((rows, width), F32), ((R, 4 * states), F32), msg_shape,
         ((2, c_bulk, width), BF16), ((2, c_bulk, width), BF16), ((8, width), F32)],
        [((2 * states, width), BF16), ((width, width), BF16), ((2 * states, width), F32), ((width, width), F32),
         ((rows, width), BF16)],
        x, teach, link, valid, ids, low, proj, s1, rates, vec, *cs, *fwds, us=10, limit=20, far_outs=(0,), copies=rows // TILE,
    )
    bwds = [lax.ppermute(bwd, "seq", [((i + k) % S, i) for i in range(S)]) for k in range(1, hops + 1)]
    def cross(v, flip_x, flip_y):
        return lax.ppermute(
            v, ("seq", "wy"), [(2 * a + b, 2 * (a ^ flip_x) + (b ^ flip_y)) for a in range(S) for b in range(2)])

    def quarters(keep, got, extra):
        shape = ((keep.shape[1] - extra) // 2 + extra, width)
        return call(functools.partial(quarter_body, extra=extra), [(shape, BF16)] * 4, [], keep, got, limit=4)

    def exchange(q):
        return (q[0], cross(q[1], 0, 1), cross(q[2], 1, 0), cross(q[3], 1, 1))

    q_c = quarters(keep_c, swap(send_c, "wc"), 0)
    bwds = lax.optimization_barrier((bwds, q_c))[0]
    part_c = exchange(q_c)
    b_bulk = 3 * shard // 2
    b_part, c_part = b_bulk // S, c_bulk // S
    gn, send_b, keep_b = call(
        functools.partial(k3_body, seqs=seqs, hops=hops, blocks=S),
        [((rows, width), BF16), ((2, b_bulk + 16, width), BF16), ((2, b_bulk + 16, width), BF16)],
        [(slab, F32), ((rows, 2 * states), BF16), ((width, 2 * states), F32), ((8, width), F32)],
        norm, sums, link, ids, low, proj, state, gs, gssm, s2, rates, vec, w_full, *bwds, us=8, limit=14,
    )
    (c_sum,) = call(sum_body, [((c_bulk // 2, width), F32)], [], *part_c, limit=4)
    got_b = swap(after(send_b, part_c[3]), "wc")
    part_b = exchange(quarters(keep_b, got_b, 16))
    (ig,) = call(norm_body, [((rows, width), BF16)], [], x, gn, gres, vec, us=3, limit=8)
    part_b, ig = lax.optimization_barrier((part_b, ig))
    tokens = float(length * seqs * lax.axis_size(("wy", "wc")))
    deal = S // 2
    if b_part % 8 == 0 and c_part % 8 == 0:
        dealt = call(
            deal_body, [((b_part + c_part + 8, width), BF16)] * deal,
            [((b_bulk // 2, width), F32)], *part_b, c_sum, limit=4,
        )
        parts = [dealt[0]] + [swap(dealt[k], "seq", 2 * k, S) for k in range(1, deal)]
        piece, tail = call(
            close_body, [((b_part + c_part, width), BF16), ((8, width), F32)], [], *parts, limit=4,
        )
        pieces = {0: piece}
        for k in range(1, deal):
            pieces[2 * k] = swap(piece, "seq", 2 * k, S)
        for k in range(deal):
            pieces[2 * k + 1] = swap(pieces[2 * k] if k else after(piece, pieces[2]), "seq", 1, S)
        pieces = [pieces[k] for k in range(S)]
    else:
        piece, tail, pieces = sum_by_all_to_all(part_b, c_sum, S, s_at)
    ingrad, loss, *lines = call(
        functools.partial(finish_body, tokens=tokens),
        [((rows, width), F32), ((1, 1), F32)] + [((1, shard), F32)] * 4 + [((1, own), F32)] * 3,
        [], tail, ig, limit=8,
    )
    gb, gc, gg = call(
        functools.partial(unpack_body, tokens=tokens),
        [((shard, 2 * states), F32), ((c_shard, width), F32), ((g_shard, width), F32)],
        [((b_bulk, width), F32), ((c_bulk, width), F32)],
        tail, *pieces, limit=8, far_outs=range(3), copies=5,
    )
    gain, bias, skip, gate, real, imag, step = (v[0] for v in lines)
    return (
        out.reshape(inputs.shape), loss[0, 0], ingrad.reshape(inputs.shape), gain, bias, gb, gc, skip, gg, gate,
        real, imag, step,
    )


def sum_by_all_to_all(part_b, v_c, S, s_at):
    v_b = sum([p.astype(F32) for p in part_b[1:]], part_b[0].astype(F32))
    width = v_b.shape[1]
    tail = v_b[-16:-8] + v_b[-8:]
    high = lax.reduce_precision(tail, 8, 7)
    ends = jnp.concatenate([high, tail - high], 0).astype(BF16)
    both = jnp.concatenate([v.astype(BF16).reshape(S // 2, -1, width) for v in (v_b[:-16], v_c)], 1)
    bulk = both.shape[1]
    both = jnp.concatenate([both, jnp.broadcast_to(ends[None], (S // 2, 16, width))], 1)
    empty = jnp.zeros_like(both)
    mine = (lax.iota(jnp.int32, S) % 2 == s_at % 2)[:, None, None]
    sent = jnp.where(mine, jnp.stack([both, both], 1).reshape(S, bulk + 16, width), jnp.stack([empty, empty], 1).reshape(S, bulk + 16, width))
    v = jnp.sum(lax.all_to_all(sent, "seq", 0, 0, tiled=True).astype(F32), 0)
    piece, tail = v[:bulk].astype(BF16), v[bulk : bulk + 8] + v[bulk + 8 :]
    back = lax.all_to_all(jnp.broadcast_to(piece[None], (S, bulk, width)), "seq", 0, 0, tiled=True)
    order = lax.iota(jnp.int32, S) ^ s_at
    return piece, tail, [lax.dynamic_index_in_dim(back, order[k], 0, keepdims=False) for k in range(S)]


def solution(mesh):
    sizes = mesh.devices.shape
    fine = Mesh(mesh.devices.reshape(sizes[0], 2, sizes[1] // 2), ("seq", "wy", "wc"))
    w = ("wy", "wc")
    tokens = P(w, "seq", None)
    return jax.shard_map(
        per_device,
        mesh=fine,
        in_specs=(
            tokens, tokens, P(w, "seq"), P(w, "seq"), P(w), P(w), P(w, None), P(w, None), P(w), P(w, None), P(w),
            P("seq"), P("seq"), P("seq"),
        ),
        out_specs=(
            tokens, P(), tokens, P(w), P(w), P(w, None), P(w, None), P(w), P(w, None), P(w),
            P("seq"), P("seq"), P("seq"),
        ),
        check_vma=False,
    )
```

```python
import functools

import jax
import jax.numpy as jnp
from jax import lax
from jax.experimental import pallas as pl
from jax.experimental.pallas import tpu as pltpu
from jax.sharding import Mesh
from jax.sharding import PartitionSpec as P

CHUNKS = 8
LANES = 128
TILE = 512
PAD = 8
MIB = 1024 * 1024
F32 = jnp.float32
BF16 = jnp.bfloat16


def small_expm1(x):
    return x * (1.0 + x / 2 * (1.0 + x / 3 * (1.0 + x / 4 * (1.0 + x / 5 * (1.0 + x / 6)))))


def rates_map(real_rate, imag_rate, log_rate):
    time_step = jnp.exp(log_rate)
    grow_re = real_rate * time_step
    turn_im = imag_rate * time_step
    growth = jnp.exp(grow_re)
    abar_re = growth * jnp.cos(turn_im)
    abar_im = growth * jnp.sin(turn_im)
    half_sine = jnp.sin(0.5 * turn_im)
    numer_re = small_expm1(grow_re) * jnp.cos(turn_im) - 2.0 * half_sine * half_sine
    divisor = real_rate * real_rate + imag_rate * imag_rate
    scale_re = (numer_re * real_rate + abar_im * imag_rate) / divisor
    scale_im = (abar_im * real_rate - numer_re * imag_rate) / divisor
    return (abar_re, abar_im, scale_re, scale_im)


def cmul(xr, xi, yr, yi):
    return xr * yr - xi * yi, xr * yi + xi * yr


def power2(xr, xi, times):
    for _ in range(times):
        xr, xi = xr * xr - xi * xi, 2.0 * xr * xi
    return xr, xi


def log2(n):
    return n.bit_length() - 1


def power(xr, xi, n):
    out = None
    while n:
        if n & 1:
            out = (xr, xi) if out is None else cmul(*out, xr, xi)
        n >>= 1
        if n:
            xr, xi = power2(xr, xi, 1)
    return out


def chunk_powers(ar, ai, steps):
    first = lax.broadcasted_iota(jnp.int32, ar.shape, 0) == 0
    sr, si = power(ar, ai, steps - PAD)
    pr, pi = power(ar, ai, steps)
    return jnp.where(first, sr, pr), jnp.where(first, si, pi)


def padded(i, block_len):
    start = i * TILE + PAD * (2 + i * TILE // block_len)
    return slice(start, start + TILE)


def add_to(ref, i, v):
    ref[...] = v if i == 0 else ref[...] + v


def run(count, body, carry, unroll):
    def block(k, c):
        for u in range(unroll):
            c = body(k * unroll + u, c)
        return c

    whole_blocks = count // unroll
    carry = lax.fori_loop(0, whole_blocks, block, carry)
    for i in range(whole_blocks * unroll, count):
        carry = body(i, carry)
    return carry


def wide(v, groups):
    return jnp.concatenate([v] * groups, axis=1)


def fold_rows(v):
    return jnp.sum(v.reshape(-1, 8, v.shape[-1]), axis=0)


def take(ref, at, first, count):
    return jnp.concatenate([ref[first + g, at, :] for g in range(count)], axis=1)


def put(ref, at, first, v):
    for g in range(v.shape[1] // LANES):
        ref[first + g, at, :] = v[:, g * LANES : (g + 1) * LANES]


def clear_pads(ref, seqs, pitch):
    for g in range(ref.shape[0]):
        ref[g, :PAD, :] = jnp.zeros((PAD, LANES), F32)
        for s in range(seqs):
            ref[g, PAD + s * pitch : 2 * PAD + s * pitch, :] = jnp.zeros((PAD, LANES), F32)


def own_w():
    return 2 * lax.axis_index("wy") + lax.axis_index("wc")


def one_row(v):
    return jnp.sum(v, axis=0, keepdims=True)


def nt_dot(a, b):
    return lax.dot_general(a, b, (((1,), (1,)), ((), ())), preferred_element_type=F32)


def tn_dot(a, b):
    return lax.dot_general(a, b, (((0,), (0,)), ((), ())), preferred_element_type=F32)


def chunk_scan(ar, ai, br, bi, reverse):
    rows = lax.broadcasted_iota(jnp.int32, ar.shape, 0)
    d = 1
    while d < CHUNKS:
        shift = (CHUNKS - d) if reverse else d
        keep = (rows < CHUNKS - d) if reverse else (rows >= d)
        pr, pi = pltpu.roll(ar, shift, 0), pltpu.roll(ai, shift, 0)
        qr, qi = pltpu.roll(br, shift, 0), pltpu.roll(bi, shift, 0)
        mr, mi = cmul(ar, ai, qr, qi)
        br, bi = jnp.where(keep, br + mr, br), jnp.where(keep, bi + mi, bi)
        mr, mi = cmul(ar, ai, pr, pi)
        ar, ai = jnp.where(keep, mr, ar), jnp.where(keep, mi, ai)
        d *= 2
    return ar, ai, br, bi


def carry_in(recvs, ids, s, own_row, ar, ai, block_len, conj, blocks):
    states = ar.shape[1]
    pr, pi = power2(ar, -ai if conj else ai, log2(block_len))
    cr = jnp.zeros((1, states), F32)
    ci = jnp.zeros((1, states), F32)
    own = wide(ids[own_row : own_row + 1, :], states // LANES)
    for k in range(len(recvs), 0, -1):
        msg = recvs[k - 1][s : s + 1, :]
        same = (wide(msg[:, 2 * states :], states // LANES) == own) & (blocks >= k)
        cr, ci = cmul(pr, pi, cr, ci)
        cr = cr + jnp.where(same, msg[:, :states], 0.0)
        ci = ci + jnp.where(same, msg[:, states : 2 * states], 0.0)
    return cr, ci


def fetch(pairs, sems):
    copies = [pltpu.make_async_copy(src, dst, sems.at[k]) for k, (src, dst) in enumerate(pairs)]
    for c in copies:
        c.start()
    for c in copies:
        c.wait()


def k0_body(b_ref, g_ref, n_ref, s_ref, q_ref, lr_ref, li_ref, ls_ref, msg_ref, table_ref,
            b_scr, v_scr, l_scr, scr, sems):
    shard, cols = b_scr.shape
    own = lr_ref.shape[1]
    fetch(
        [(b_ref, b_scr)]
        + [(r, v_scr.at[k]) for k, r in enumerate((g_ref, n_ref, s_ref, q_ref))]
        + [(r, l_scr.at[k]) for k, r in enumerate((lr_ref, li_ref, ls_ref))],
        sems,
    )
    msg_ref[:shard, :] = b_scr[...]
    line = jnp.concatenate([v_scr[k] for k in range(4)] + [jnp.zeros((1, cols - 4 * shard), BF16)], axis=1)
    msg_ref[shard:, :] = jnp.broadcast_to(line, (16, cols))
    scr[...] = jnp.zeros_like(scr)
    for k in range(3):
        scr[k : k + 1, :own] = l_scr[k]
    table_ref[...] = pltpu.roll(scr[...], lax.axis_index("seq") * own, 1)


def k0b_body(c_ref, g_ref, msg_ref, c_scr, g_scr, sems):
    c_shard = c_ref.shape[0]
    fetch([(c_ref, c_scr), (g_ref, g_scr)], sems)
    msg_ref[:c_shard, :] = c_scr[...]
    msg_ref[c_shard:, :] = g_scr[...]


def lay_marks(seg_ref, mask_ref, link_ref, valid_ref, ids_ref):
    seqs, block_len = seg_ref.shape
    seg = seg_ref[...].astype(F32)
    link_ref[:PAD, :] = jnp.ones((PAD, LANES), F32)
    lane = lax.broadcasted_iota(jnp.int32, (1, block_len), 1)
    for s in range(seqs):
        row = seg[s : s + 1, :]
        link = jnp.where((row == pltpu.roll(row, 1, 1)) | (lane == 0), 1.0, 0.0)
        mask = mask_ref[s : s + 1, :].astype(F32)
        start = PAD + s * (block_len + PAD)
        link_ref[start : start + PAD, :] = jnp.ones((PAD, LANES), F32)
        for src, dst, start in ((link, link_ref, start + PAD), (mask, valid_ref, s * block_len)):
            for k in range(block_len // LANES):
                piece = jnp.broadcast_to(src[:, k * LANES : (k + 1) * LANES], (LANES, LANES))
                at = start + k * LANES
                dst[at : at + LANES, :] = jnp.transpose(piece)
        ids_ref[s : s + 1, :] = jnp.broadcast_to(row[:, :1], (1, LANES))
        ids_ref[seqs + s : seqs + s + 1, :] = jnp.broadcast_to(row[:, block_len - 1 :], (1, LANES))


def k1_body(x_ref, b0, b1, b2, b3, table_ref, seg_ref, mask_ref,
            low_ref, n_ref, proj_ref, vec_ref, full_ref, s1_ref, msg_ref, rates_ref, link_ref, valid_ref, ids_ref, *, seqs):
    rows, width = x_ref.shape
    shard = b0.shape[0] - 16
    block_len = rows // seqs
    pitch = block_len + PAD
    w = own_w()
    for k, piece in enumerate((b0, b1, b2, b3)):
        at = pl.multiple_of((w ^ k) * shard, shard)
        full_ref[pl.ds(at, shard), :] = piece[:shard, :]
        extra = piece[shard:, :].astype(F32)
        for v in range(4):
            vec_ref[v : v + 1, pl.ds(at, shard)] = extra[0:1, v * shard : (v + 1) * shard]
    vec_ref[4:8, :] = jnp.zeros((4, width), F32)
    gain = vec_ref[0:1, :]
    bias = vec_ref[1:2, :]
    for i in range(rows // TILE):
        at = slice(i * TILE, (i + 1) * TILE)
        n = centre(x_ref[at, :])[0]
        n_ref[at, :] = n.astype(BF16)
        low = (n * gain + bias).astype(BF16)
        low_ref[at, :] = low
        p = jnp.dot(low, full_ref[...], preferred_element_type=F32)
        put(proj_ref, padded(i, block_len), 0, p.astype(BF16).astype(F32))
    clear_pads(proj_ref, seqs, pitch)
    lay_marks(seg_ref, mask_ref, link_ref, valid_ref, ids_ref)
    states = table_ref.shape[1]
    groups = states // LANES
    steps = block_len // CHUNKS + 1
    lam = [table_ref[v : v + 1, :] for v in range(3)]
    parts, back = jax.vjp(rates_map, *lam)
    one, zero = jnp.ones_like(lam[0]), jnp.zeros_like(lam[0])
    for v in range(4):
        rates_ref[v : v + 1, :] = parts[v]
        for k, jac in enumerate(back(tuple(one if i == v else zero for i in range(4)))):
            rates_ref[8 + 3 * v + k : 9 + 3 * v + k, :] = jac
    rates_ref[4:8, :] = jnp.zeros((4, states), F32)
    rates_ref[20:24, :] = jnp.zeros((4, states), F32)
    ar = jnp.broadcast_to(parts[0], (CHUNKS, states))
    ai = jnp.broadcast_to(parts[1], (CHUNKS, states))

    def step(j, carry):
        out = []
        for s in range(seqs):
            ur, ui, q = carry[s]
            at = pl.ds(PAD + s * pitch + j, CHUNKS, stride=steps)
            lk = link_ref[at, :]
            lw = wide(lk, groups)
            nr, ni = cmul(ar, ai, ur, ui)
            out.append((lw * nr + take(proj_ref, at, 0, groups), lw * ni + take(proj_ref, at, groups, groups), q * lk))
        return tuple(out)

    zero = jnp.zeros((CHUNKS, states), F32)
    init = tuple((zero, zero, jnp.ones((CHUNKS, LANES), F32)) for _ in range(seqs))
    ends = run(steps, step, init, 13)
    pr, pi = chunk_powers(ar, ai, steps)
    for s in range(seqs):
        ur, ui, q = ends[s]
        qw = wide(q, groups)
        sc = chunk_scan(pr * qw, pi * qw, ur, ui, False)
        for v in range(4):
            s1_ref[s * CHUNKS : (s + 1) * CHUNKS, v * states : (v + 1) * states] = sc[v]
        msg_ref[s : s + 1, :states] = sc[2][CHUNKS - 1 :, :]
        msg_ref[s : s + 1, states : 2 * states] = sc[3][CHUNKS - 1 :, :]
        msg_ref[s : s + 1, 2 * states :] = ids_ref[seqs + s : seqs + s + 1, :]


def k2_body(*refs, seqs, hops):
    (x_ref, t_ref, link_ref, valid_ref, ids_ref, low_ref, proj_ref, s1_ref, rates_ref, vec_ref,
     c0, c1, c2, c3) = refs[:14]
    recvs = refs[14 : 14 + hops]
    (out_hbm, state_ref, gs_ref, gres_ref, gssm_ref, s2_ref, msg_ref, send_ref, keep_ref, sums_ref,
     wc_scr, wg_scr, gc_scr, gg_scr, out_ref, sems) = refs[14 + hops :]
    rows, width = x_ref.shape
    states = rates_ref.shape[1]
    groups = states // LANES
    block_len = rows // seqs
    steps = block_len // CHUNKS + 1
    pitch = block_len + PAD
    g_shard = width // 4
    c_shard = 2 * states // 4
    w = own_w()
    for k, piece in enumerate((c0, c1, c2, c3)):
        wc_scr[pl.ds(pl.multiple_of((w ^ k) * c_shard, c_shard), c_shard), :] = piece[:c_shard, :]
        wg_scr[pl.ds(pl.multiple_of((w ^ k) * g_shard, g_shard), g_shard), :] = piece[c_shard:, :]
    a1r, a1i = rates_ref[0:1, :], rates_ref[1:2, :]
    ar = jnp.broadcast_to(a1r, (CHUNKS, states))
    ai = jnp.broadcast_to(a1i, (CHUNKS, states))
    zr = jnp.broadcast_to(rates_ref[2:3, :], (CHUNKS, states))
    zi = jnp.broadcast_to(rates_ref[3:4, :], (CHUNKS, states))
    top = lax.broadcasted_iota(jnp.int32, (CHUNKS, states), 0)
    ids = ids_ref[...]
    init, carries = [], []
    for s in range(seqs):
        cr, ci = carry_in(recvs, ids, s, s, a1r, a1i, block_len, False, lax.axis_index("seq"))
        sc = [s1_ref[s * CHUNKS : (s + 1) * CHUNKS, v * states : (v + 1) * states] for v in range(4)]
        mr, mi = cmul(sc[0], sc[1], cr, ci)
        init.append((pltpu.roll(sc[2] + mr, 1, 0), pltpu.roll(sc[3] + mi, 1, 0)))
        carries.append((cr, ci))

    def step(j, carry):
        out = []
        for s in range(seqs):
            ur, ui = carry[s]
            at = pl.ds(PAD + s * pitch + j, CHUNKS, stride=steps)
            lw = wide(link_ref[at, :], groups)
            nr, ni = cmul(ar, ai, ur, ui)
            ur, ui = lw * nr + take(proj_ref, at, 0, groups), lw * ni + take(proj_ref, at, groups, groups)
            sr, si = cmul(zr, zi, ur, ui)
            put(state_ref, at, 0, sr)
            put(state_ref, at, groups, si)
            out.append((ur, ui))
        return tuple(out)

    for g in range(2 * groups):
        state_ref[g, :PAD, :] = jnp.zeros((PAD, LANES), F32)
    entry = list(run(PAD, step, tuple(init), PAD))
    for s in range(seqs):
        ur, ui = (jnp.where(top == 0, c, u) for c, u in zip(carries[s], entry[s]))
        sr, si = cmul(zr, zi, ur, ui)
        at = pl.ds(PAD + s * pitch + PAD - 1, CHUNKS, stride=steps)
        put(state_ref, at, 0, sr)
        put(state_ref, at, groups, si)
        entry[s] = (ur, ui)
    run(steps - PAD, lambda i, c: step(i + PAD, c), tuple(entry), 19)

    skip = vec_ref[2:3, :]
    gbias = 0.5 * vec_ref[3:4, :]
    leaving = []
    loss_acc = jnp.zeros((8, width), F32)
    gbias_acc = jnp.zeros((8, width), F32)
    skip_acc = jnp.zeros((8, width), F32)
    for i in range(rows // TILE):
        at = slice(i * TILE, (i + 1) * TILE)
        pad_at = padded(i, block_len)
        sl = take(state_ref, pad_at, 0, 2 * groups).astype(BF16)
        so = jnp.dot(sl, wc_scr[...], preferred_element_type=F32) + skip * low_ref[at, :].astype(F32)
        e = jnp.exp2(so * so * -0.7213475204444817)
        t = 1.0 / (1.0 + 0.23164189 * jnp.abs(so))
        tail = e * t * (0.127414796 + t * (-0.142248368 + t * (0.7107068705 + t * (-0.7265760135 + t * 0.5307027145))))
        phi = jnp.where(so >= 0.0, 1.0 - tail, tail)
        act = (so * phi).astype(BF16)
        dgelu = phi + so * e * 0.3989422804014327
        g = 0.5 * jnp.tanh(0.5 * jnp.dot(act, wg_scr[...], preferred_element_type=F32) + gbias) + 0.5
        gated = act.astype(F32) * g
        res = x_ref[at, :].astype(F32) + gated
        out_ref[at, :] = res.astype(BF16)
        leaving.append(pltpu.make_async_copy(out_ref.at[at, :], out_hbm.at[at, :], sems.at[i]))
        leaving[-1].start()
        err = res - t_ref[at, :].astype(F32)
        gr = err * wide(valid_ref[at, :], width // LANES)
        loss_acc = loss_acc + fold_rows(gr * err)
        gres_ref[at, :] = gr.astype(BF16)
        gg = gr * gated * (1.0 - g)
        gbias_acc = gbias_acc + fold_rows(gg)
        gl = gg.astype(BF16)
        add_to(gg_scr, i, tn_dot(act, gl))
        gssm = dgelu * (gr * g + nt_dot(gl, wg_scr[...]))
        gssm_ref[at, :] = gssm
        skip_acc = skip_acc + fold_rows(gssm * low_ref[at, :].astype(F32))
        ssl = gssm.astype(BF16)
        put(gs_ref, pad_at, 0, nt_dot(ssl, wc_scr[...]).astype(BF16).astype(F32))
        add_to(gc_scr, i, tn_dot(sl, ssl))
    clear_pads(gs_ref, seqs, pitch)
    sums_ref[0:1, :] = one_row(skip_acc)
    sums_ref[1:2, :] = one_row(gbias_acc)
    sums_ref[2:3, :] = jnp.broadcast_to(jnp.sum(one_row(loss_acc), axis=1, keepdims=True), (1, width))
    sums_ref[3:4, :] = wide(one_row(fold_rows(valid_ref[...])), width // LANES)
    sums_ref[4:8, :] = jnp.zeros((4, width), F32)

    def back(i, carry):
        j = steps - 1 - i
        out = []
        for s in range(seqs):
            yr, yi, q = carry[s]
            at = pl.ds(PAD + s * pitch + j, CHUNKS, stride=steps)
            lk = link_ref[at, :]
            lw = wide(lk, groups)
            nr, ni = cmul(ar, -ai, yr, yi)
            out.append((lw * (nr + take(gs_ref, at, 0, groups)), lw * (ni + take(gs_ref, at, groups, groups)), q * lk))
        return tuple(out)

    zero = jnp.zeros((CHUNKS, states), F32)
    init = tuple((zero, zero, jnp.ones((CHUNKS, LANES), F32)) for _ in range(seqs))
    firsts = run(steps - PAD, back, init, 19)
    ends = run(PAD, lambda i, c: back(i + steps - PAD, c), firsts, PAD)
    pr, pi = chunk_powers(ar, -ai, steps)
    for s in range(seqs):
        yr, yi, q = (jnp.where(top[:, : v.shape[1]] == 0, u, v) for u, v in zip(firsts[s], ends[s]))
        qw = wide(q, groups)
        sc = chunk_scan(pr * qw, pi * qw, yr, yi, True)
        for v in range(4):
            s2_ref[s * CHUNKS : (s + 1) * CHUNKS, v * states : (v + 1) * states] = sc[v]
        msg_ref[s : s + 1, :states] = sc[2][:1, :]
        msg_ref[s : s + 1, states : 2 * states] = sc[3][:1, :]
        msg_ref[s : s + 1, 2 * states :] = ids_ref[s : s + 1, :]

    for k, dst in enumerate((keep_ref, send_ref, keep_ref, send_ref)):
        q = w ^ k
        slot = q // 2
        dst[slot, :c_shard, :] = gc_scr[pl.ds(pl.multiple_of(q * c_shard, c_shard), c_shard), :].astype(BF16)
        lanes = pl.multiple_of(q * g_shard, g_shard)
        dst[slot, c_shard : c_shard + g_shard, :] = gg_scr[pl.ds(lanes, g_shard), :].astype(BF16)
    for copy in leaving:
        copy.wait()


def split16(v):
    high = v.astype(BF16)
    return high, (v - high.astype(F32)).astype(BF16)


def split_rows(lines):
    width = lines[0].shape[1]
    rows = sum(v.shape[0] for v in lines)
    v = jnp.concatenate(lines + [jnp.zeros((8 - rows, width), F32)] * (rows < 8), axis=0)
    high, rest = split16(v)
    return jnp.concatenate([high.astype(F32), rest.astype(F32)], axis=0).astype(BF16)


def k3_body(*refs, seqs, hops, blocks):
    (n_ref, sums_ref, link_ref, ids_ref, low_ref, proj_ref, state_ref, gs_ref, gssm_ref,
     s2_ref, rates_ref, vec_ref, w_full) = refs[:13]
    recvs = refs[13 : 13 + hops]
    (gn_ref, send_ref, keep_ref, gp_scr, gpl_scr, gb_scr, vec_scr) = refs[13 + hops :]
    rows, width = n_ref.shape
    states = rates_ref.shape[1]
    groups = states // LANES
    block_len = rows // seqs
    steps = block_len // CHUNKS + 1
    pitch = block_len + PAD
    shard = width // 4
    w = own_w()
    a1r, a1i = rates_ref[0:1, :], rates_ref[1:2, :]
    ar = jnp.broadcast_to(a1r, (CHUNKS, states))
    ai = jnp.broadcast_to(a1i, (CHUNKS, states))
    zr = jnp.broadcast_to(rates_ref[2:3, :], (CHUNKS, states))
    zi = jnp.broadcast_to(rates_ref[3:4, :], (CHUNKS, states))
    rowid = lax.broadcasted_iota(jnp.int32, (CHUNKS, states), 0)
    ids = ids_ref[...]
    rate_sums = [jnp.zeros((CHUNKS, states), F32) for _ in range(4)]
    for s in range(seqs):
        cr, ci = carry_in(recvs, ids, s, seqs + s, a1r, a1i, block_len, True, blocks - 1 - lax.axis_index("seq"))
        sc = [s2_ref[s * CHUNKS : (s + 1) * CHUNKS, v * states : (v + 1) * states] for v in range(4)]
        mr, mi = cmul(sc[0], sc[1], cr, ci)
        yr = jnp.where(rowid == CHUNKS - 1, cr, pltpu.roll(sc[2] + mr, CHUNKS - 1, 0))
        yi = jnp.where(rowid == CHUNKS - 1, ci, pltpu.roll(sc[3] + mi, CHUNKS - 1, 0))

        def step(i, carry):
            yr, yi, gar, gai, gsr, gsi = carry
            j = steps - 1 - i
            at = pl.ds(PAD + s * pitch + j, CHUNKS, stride=steps)
            before = pl.ds(PAD + s * pitch + j - 1, CHUNKS, stride=steps)
            lw = wide(link_ref[at, :], groups)
            nr, ni = cmul(ar, -ai, yr, yi)
            dr, di = nr + take(gs_ref, at, 0, groups), ni + take(gs_ref, at, groups, groups)
            yr, yi = lw * dr, lw * di
            pr, pi = take(proj_ref, at, 0, groups), take(proj_ref, at, groups, groups)
            ur, ui = take(state_ref, before, 0, groups), take(state_ref, before, groups, groups)
            put(gp_scr, at, 0, zr * dr + zi * di)
            put(gp_scr, at, groups, zr * di - zi * dr)
            return (
                yr, yi,
                gar + (ur * yr + ui * yi), gai + (ur * yi - ui * yr),
                gsr + (pr * dr + pi * di), gsi + (pr * di - pi * dr),
            )

        carry = run(steps - PAD, step, (yr, yi, *rate_sums), 8)
        yr, yi = (jnp.where(rowid == 0, 0.0, v) for v in carry[:2])
        carry = run(PAD, lambda i, c: step(i + steps - PAD, c), (yr, yi, *carry[2:]), PAD)
        rate_sums = list(carry[2:])

    skip = vec_ref[2:3, :]
    gain_acc = jnp.zeros((8, width), F32)
    bias_acc = jnp.zeros((8, width), F32)
    for i in range(rows // TILE):
        at = slice(i * TILE, (i + 1) * TILE)
        gpl = take(gp_scr, padded(i, block_len), 0, 2 * groups).astype(BF16)
        gpl_scr[at, :] = gpl
        gn = nt_dot(gpl, w_full[...]) + skip * gssm_ref[at, :]
        gn_ref[at, :] = gn.astype(BF16)
        gain_acc = gain_acc + fold_rows(gn * n_ref[at, :].astype(F32))
        bias_acc = bias_acc + fold_rows(gn)
    gb_scr[...] = tn_dot(low_ref[...], gpl_scr[...])
    sums4 = [one_row(v) for v in rate_sums]
    rate_grads = []
    for k in range(3):
        rate_grads.append(sum(rates_ref[8 + 3 * c + k : 9 + 3 * c + k, :] * sums4[c] for c in range(4)))
    vec_scr[0:1, :] = one_row(gain_acc)
    vec_scr[1:2, :] = one_row(bias_acc)
    extra = 3 * shard // 2
    half = shard // 2
    for k, dst in enumerate((keep_ref, send_ref, keep_ref, send_ref)):
        slot = (w ^ k) // 2
        q = pl.multiple_of((w ^ k) * shard, shard)
        dst[slot, :shard, :] = gb_scr[pl.ds(q, shard), :width].astype(BF16)
        dst[slot, shard:extra, : width // 2] = gb_scr[pl.ds(q, half), width:].astype(BF16)
        dst[slot, shard:extra, width // 2 :] = gb_scr[pl.ds(q + half, half), width:].astype(BF16)
        mine = [vec_scr[v : v + 1, pl.ds(q, shard)] for v in range(2)] + [jnp.zeros((1, shard), F32)]
        others = [sums_ref[v : v + 1, pl.ds(q, shard)] for v in range(2)] + [sums_ref[v : v + 1, :shard] for v in (2, 3)]
        lines = [jnp.concatenate(p, axis=1) for p in [*zip(rate_grads, mine), others]]
        dst[slot, extra:, :] = split_rows(lines)


def centre(values):
    x = values.astype(F32)
    c = x - jnp.mean(x, -1, keepdims=True)
    r = lax.rsqrt(jnp.mean(c * c, -1, keepdims=True) + 1e-05)
    return c * r, r


def sum_body(c0, c1, c2, c3, sum_ref):
    sum_ref[...] = total((c0, c1, c2, c3), slice(0, sum_ref.shape[0]))


def quarter_body(keep_ref, got_ref, *outs, extra):
    half = outs[0].shape[0] - extra
    x, y = lax.axis_index("seq") % 2, lax.axis_index("wy")
    for out, slot, side in zip(outs, (y, 1 - y, y, 1 - y), (x, x, 1 - x, 1 - x)):
        def both(rows):
            return keep_ref[slot, rows, :].astype(F32) + got_ref[slot, rows, :].astype(F32)

        out[:half, :] = both(pl.ds(pl.multiple_of(side * half, half), half)).astype(BF16)
        if extra:
            v = both(slice(2 * half, 2 * half + 16))
            out[half:, :] = split_rows([v[:8] + v[8:]])


def total(refs, rows):
    return sum([r[rows, :].astype(F32) for r in refs[1:]], refs[0][rows, :].astype(F32))


def deal_body(*refs):
    n = len(refs) - 6
    bs, c_sum, outs, b_scr = refs[:4], refs[4], refs[5 : 5 + n], refs[5 + n]
    b_half, c_half = b_scr.shape[0], c_sum.shape[0]
    b_part, c_part = b_half // n, c_half // n
    b_scr[...] = total(bs, slice(0, b_half))
    tail = total(bs, slice(b_half, b_half + 16))
    ends = split_rows([tail[:8] + tail[8:]]).astype(F32)
    for k, out in enumerate(outs):
        at = (lax.axis_index("seq") // 2) ^ k
        rows = [
            b_scr[pl.ds(pl.multiple_of(at * b_part, 8), b_part), :],
            c_sum[pl.ds(pl.multiple_of(at * c_part, 8), c_part), :],
            ends[:4], ends[8:12],
        ]
        out[...] = jnp.concatenate(rows, axis=0).astype(BF16)


def close_body(*refs):
    parts, (piece_ref, tail_ref) = refs[:-2], refs[-2:]
    bulk = piece_ref.shape[0]
    v = total(parts, slice(0, bulk + 8))
    piece_ref[...] = v[:bulk].astype(BF16)
    tail_ref[...] = jnp.concatenate([v[bulk : bulk + 4] + v[bulk + 4 :], jnp.zeros((4, v.shape[1]), F32)], axis=0)


def scale_of(tail, tokens):
    return tokens / tail[3:4, 3 * LANES : 3 * LANES + 1]


def norm_body(x_ref, gn_ref, gres_ref, vec_ref, ig_ref):
    gain = vec_ref[0:1, :]
    for i in range(x_ref.shape[0] // TILE):
        at = slice(i * TILE, (i + 1) * TILE)
        n, r = centre(x_ref[at, :])
        q = gn_ref[at, :].astype(F32) * gain
        back = (q - jnp.mean(q, -1, keepdims=True) - n * jnp.mean(q * n, -1, keepdims=True)) * r
        ig_ref[at, :] = (gres_ref[at, :].astype(F32) + back).astype(BF16)


def finish_body(tail_ref, ig_ref,
                out_ref, loss_ref, gain_ref, bias_ref, skip_ref, gate_ref, real_ref, imag_ref, step_ref, *, tokens):
    width = ig_ref.shape[1]
    states = width - gain_ref.shape[1]
    own = real_ref.shape[1]
    tail = tail_ref[...]
    scale = scale_of(tail, tokens)
    out_ref[...] = scale * ig_ref[...].astype(F32)
    scaled = tail * scale
    gain_ref[...] = scaled[0:1, states:]
    bias_ref[...] = scaled[1:2, states:]
    skip_ref[...] = scaled[3:4, :LANES]
    gate_ref[...] = scaled[3:4, LANES : 2 * LANES]
    loss_ref[...] = tail[3:4, 2 * LANES : 2 * LANES + 1] * scale * (1.0 / (tokens * width))
    rates = pltpu.roll(scaled[:, :states], states - lax.axis_index("seq") * own, 1)
    for k, ref in enumerate((real_ref, imag_ref, step_ref)):
        ref[...] = rates[k : k + 1, :own]


def unpack_body(tail_ref, *refs, tokens):
    pieces, (gb_hbm, gc_hbm, gg_hbm, b_scr, c_scr, sems) = refs[:-6], refs[-6:]
    scale = scale_of(tail_ref[...], tokens)
    S = len(pieces)
    b_rows, c_rows = b_scr.shape[0] // S, c_scr.shape[0] // S
    for k, piece in enumerate(pieces):
        s = lax.axis_index("seq") ^ k
        v = piece[...].astype(F32) * scale
        b_at = s % 2 * (b_scr.shape[0] // 2) + s // 2 * b_rows
        c_at = s % 2 * (c_scr.shape[0] // 2) + s // 2 * c_rows
        b_scr[pl.ds(pl.multiple_of(b_at, 8), b_rows), :] = v[:b_rows, :]
        c_scr[pl.ds(pl.multiple_of(c_at, 8), c_rows), :] = v[b_rows:, :]
    shard, cols = gb_hbm.shape
    width = b_scr.shape[1]
    half, c_shard = shard // 2, gc_hbm.shape[0]
    fetch([
        (c_scr.at[:c_shard, :], gc_hbm),
        (c_scr.at[c_shard:, :], gg_hbm),
        (b_scr.at[:shard, :], gb_hbm.at[:, :width]),
        (b_scr.at[shard:, : cols - width], gb_hbm.at[:half, width:]),
        (b_scr.at[shard:, cols - width :], gb_hbm.at[half:, width:]),
    ], sems)


def whole(n, far=()):
    return [pl.BlockSpec(memory_space=pltpu.HBM if i in far else pltpu.VMEM) for i in range(n)]


def call(body, outs, scratch, *args, us=1, limit=30, far=(), far_outs=(), copies=0):
    return pl.pallas_call(
        body,
        out_shape=[jax.ShapeDtypeStruct(*o) for o in outs],
        in_specs=whole(len(args), far),
        out_specs=whole(len(outs), far_outs),
        scratch_shapes=[pltpu.VMEM(*s) for s in scratch] + [pltpu.SemaphoreType.DMA((copies,))] * (copies > 0),
        compiler_params=pltpu.CompilerParams(vmem_limit_bytes=limit * MIB),
        cost_estimate=pl.CostEstimate(flops=us * 1_000_000_000, bytes_accessed=MIB, transcendentals=0),
    )(*args)


def per_device(inputs, teacher, segment_ids, valid_mask, ln_gain, ln_bias, b_weight, c_weight, skip_weight,
               glu_weight, glu_bias, lambda_real, lambda_imag, log_step):
    S = lax.axis_size("seq")
    s_at = lax.axis_index("seq")
    seqs, block_len, width = inputs.shape
    rows = seqs * block_len
    padded_rows = PAD + seqs * (block_len + PAD)
    length = S * block_len
    own = lambda_real.shape[0]
    states = own * S
    doc_most = {4096: 1024, 32768: 8192}.get(length, length)
    hops = min((doc_most - 2) // block_len + 1, S - 1)
    shard, c_shard, g_shard = b_weight.shape[0], c_weight.shape[0], glu_weight.shape[0]

    def swap(v, axis, bit=1, n=2):
        return lax.ppermute(v, axis, [(i, i ^ bit) for i in range(n)])

    def after(v, *others):
        return lax.optimization_barrier((v, *others))[0]

    b_msg, table = call(
        k0_body,
        [((shard + 16, b_weight.shape[1]), BF16), ((8, states), F32)],
        [(b_weight.shape, BF16), ((4, 1, shard), BF16), ((3, 1, own), F32), ((8, states), F32)],
        b_weight, *(v[None] for v in (ln_gain, ln_bias, skip_weight, glu_bias, lambda_real, lambda_imag, log_step)),
        far=range(8), copies=8, limit=60,
    )
    b_far = swap(b_msg, "wy")
    b_near = swap(b_msg, "wc")
    (c_msg,) = call(
        k0b_body,
        [((c_shard + g_shard, width), BF16)],
        [(c_weight.shape, BF16), (glu_weight.shape, BF16)],
        c_weight, glu_weight, far=range(2), copies=2, limit=4,
    )
    c_far = swap(after(c_msg, b_far), "wy")
    bit = 1
    while bit < S:
        radix = 4 if 4 * bit <= S else 2
        table = sum([swap(table, "seq", k * bit, S) for k in range(1, radix)], table)
        bit *= radix
    bs = (b_msg, b_near, b_far, swap(b_far, "wc"))

    x = inputs.reshape(rows, width)
    teach = teacher.reshape(rows, width)
    R = seqs * CHUNKS
    slab = (2 * states // LANES, padded_rows, LANES)
    msg_shape = ((seqs, 2 * states + LANES), F32)
    low, norm, proj, vec, w_full, s1, fwd, rates, link, valid, ids = call(
        functools.partial(k1_body, seqs=seqs),
        [((rows, width), BF16), ((rows, width), BF16), (slab, F32), ((8, width), F32), ((width, 2 * states), BF16),
         ((R, 4 * states), F32), msg_shape, ((24, states), F32),
         ((padded_rows, LANES), F32), ((rows, LANES), F32), ((2 * seqs, LANES), F32)],
        [],
        x, *bs, table, segment_ids, valid_mask, us=2, limit=8,
    )
    cs = (c_msg, swap(c_msg, "wc"), c_far, swap(after(c_far, fwd), "wc"))
    fwds = [lax.ppermute(fwd, "seq", [(i, (i + k) % S) for i in range(S)]) for k in range(1, hops + 1)]
    c_bulk = c_shard + g_shard
    out, state, gs, gres, gssm, s2, bwd, send_c, keep_c, sums = call(
        functools.partial(k2_body, seqs=seqs, hops=hops),
        [((rows, width), BF16), (slab, F32), (slab, F32),
         ((rows, width), BF16), ((rows, width), F32), ((R, 4 * states), F32), msg_shape,
         ((2, c_bulk, width), BF16), ((2, c_bulk, width), BF16), ((8, width), F32)],
        [((2 * states, width), BF16), ((width, width), BF16), ((2 * states, width), F32), ((width, width), F32),
         ((rows, width), BF16)],
        x, teach, link, valid, ids, low, proj, s1, rates, vec, *cs, *fwds, us=10, limit=20, far_outs=(0,), copies=rows // TILE,
    )
    bwds = [lax.ppermute(bwd, "seq", [((i + k) % S, i) for i in range(S)]) for k in range(1, hops + 1)]
    def cross(v, flip_x, flip_y):
        return lax.ppermute(
            v, ("seq", "wy"), [(2 * a + b, 2 * (a ^ flip_x) + (b ^ flip_y)) for a in range(S) for b in range(2)])

    def quarters(keep, got, extra):
        shape = ((keep.shape[1] - extra) // 2 + extra, width)
        return call(functools.partial(quarter_body, extra=extra), [(shape, BF16)] * 4, [], keep, got, limit=4)

    def exchange(q):
        return (q[0], cross(q[1], 0, 1), cross(q[2], 1, 0), cross(q[3], 1, 1))

    q_c = quarters(keep_c, swap(send_c, "wc"), 0)
    bwds = lax.optimization_barrier((bwds, q_c))[0]
    part_c = exchange(q_c)
    b_bulk = 3 * shard // 2
    b_part, c_part = b_bulk // S, c_bulk // S
    gn, send_b, keep_b = call(
        functools.partial(k3_body, seqs=seqs, hops=hops, blocks=S),
        [((rows, width), BF16), ((2, b_bulk + 16, width), BF16), ((2, b_bulk + 16, width), BF16)],
        [(slab, F32), ((rows, 2 * states), BF16), ((width, 2 * states), F32), ((8, width), F32)],
        norm, sums, link, ids, low, proj, state, gs, gssm, s2, rates, vec, w_full, *bwds, us=8, limit=14,
    )
    (c_sum,) = call(sum_body, [((c_bulk // 2, width), F32)], [], *part_c, limit=4)
    got_b = swap(after(send_b, part_c[3]), "wc")
    part_b = exchange(quarters(keep_b, got_b, 16))
    (ig,) = call(norm_body, [((rows, width), BF16)], [], x, gn, gres, vec, us=3, limit=8)
    part_b, ig = lax.optimization_barrier((part_b, ig))
    tokens = float(length * seqs * lax.axis_size(("wy", "wc")))
    deal = S // 2
    if b_part % 8 == 0 and c_part % 8 == 0:
        dealt = call(
            deal_body, [((b_part + c_part + 8, width), BF16)] * deal,
            [((b_bulk // 2, width), F32)], *part_b, c_sum, limit=4,
        )
        parts = [dealt[0]] + [swap(dealt[k], "seq", 2 * k, S) for k in range(1, deal)]
        piece, tail = call(
            close_body, [((b_part + c_part, width), BF16), ((8, width), F32)], [], *parts, limit=4,
        )
        pieces = {0: piece}
        for k in range(1, deal):
            pieces[2 * k] = swap(piece, "seq", 2 * k, S)
        for k in range(deal):
            pieces[2 * k + 1] = swap(pieces[2 * k] if k else after(piece, pieces[2]), "seq", 1, S)
        pieces = [pieces[k] for k in range(S)]
    else:
        piece, tail, pieces = sum_by_all_to_all(part_b, c_sum, S, s_at)
    ingrad, loss, *lines = call(
        functools.partial(finish_body, tokens=tokens),
        [((rows, width), F32), ((1, 1), F32)] + [((1, shard), F32)] * 4 + [((1, own), F32)] * 3,
        [], tail, ig, limit=8,
    )
    gb, gc, gg = call(
        functools.partial(unpack_body, tokens=tokens),
        [((shard, 2 * states), F32), ((c_shard, width), F32), ((g_shard, width), F32)],
        [((b_bulk, width), F32), ((c_bulk, width), F32)],
        tail, *pieces, limit=8, far_outs=range(3), copies=5,
    )
    gain, bias, skip, gate, real, imag, step = (v[0] for v in lines)
    return (
        out.reshape(inputs.shape), loss[0, 0], ingrad.reshape(inputs.shape), gain, bias, gb, gc, skip, gg, gate,
        real, imag, step,
    )


def sum_by_all_to_all(part_b, v_c, S, s_at):
    v_b = sum([p.astype(F32) for p in part_b[1:]], part_b[0].astype(F32))
    width = v_b.shape[1]
    tail = v_b[-16:-8] + v_b[-8:]
    high = lax.reduce_precision(tail, 8, 7)
    ends = jnp.concatenate([high, tail - high], 0).astype(BF16)
    both = jnp.concatenate([v.astype(BF16).reshape(S // 2, -1, width) for v in (v_b[:-16], v_c)], 1)
    bulk = both.shape[1]
    both = jnp.concatenate([both, jnp.broadcast_to(ends[None], (S // 2, 16, width))], 1)
    empty = jnp.zeros_like(both)
    mine = (lax.iota(jnp.int32, S) % 2 == s_at % 2)[:, None, None]
    sent = jnp.where(mine, jnp.stack([both, both], 1).reshape(S, bulk + 16, width), jnp.stack([empty, empty], 1).reshape(S, bulk + 16, width))
    v = jnp.sum(lax.all_to_all(sent, "seq", 0, 0, tiled=True).astype(F32), 0)
    piece, tail = v[:bulk].astype(BF16), v[bulk : bulk + 8] + v[bulk + 8 :]
    back = lax.all_to_all(jnp.broadcast_to(piece[None], (S, bulk, width)), "seq", 0, 0, tiled=True)
    order = lax.iota(jnp.int32, S) ^ s_at
    return piece, tail, [lax.dynamic_index_in_dim(back, order[k], 0, keepdims=False) for k in range(S)]


def solution(mesh):
    sizes = mesh.devices.shape
    fine = Mesh(mesh.devices.reshape(sizes[0], 2, sizes[1] // 2), ("seq", "wy", "wc"))
    w = ("wy", "wc")
    tokens = P(w, "seq", None)
    return jax.shard_map(
        per_device,
        mesh=fine,
        in_specs=(
            tokens, tokens, P(w, "seq"), P(w, "seq"), P(w), P(w), P(w, None), P(w, None), P(w), P(w, None), P(w),
            P("seq"), P("seq"), P("seq"),
        ),
        out_specs=(
            tokens, P(), tokens, P(w), P(w), P(w, None), P(w, None), P(w), P(w, None), P(w),
            P("seq"), P("seq"), P("seq"),
        ),
        check_vma=False,
    )
```

```python
import functools

import jax
import jax.numpy as jnp
from jax import lax
from jax.experimental import pallas as pl
from jax.experimental.pallas import tpu as pltpu
from jax.sharding import Mesh
from jax.sharding import PartitionSpec as P

CHUNKS = 8
LANES = 128
TILE = 512
PAD = 8
MIB = 1024 * 1024
F32 = jnp.float32
BF16 = jnp.bfloat16


def small_expm1(x):
    return x * (1.0 + x / 2 * (1.0 + x / 3 * (1.0 + x / 4 * (1.0 + x / 5 * (1.0 + x / 6)))))


def rates_map(real_rate, imag_rate, log_rate):
    time_step = jnp.exp(log_rate)
    grow_re = real_rate * time_step
    turn_im = imag_rate * time_step
    growth = jnp.exp(grow_re)
    abar_re = growth * jnp.cos(turn_im)
    abar_im = growth * jnp.sin(turn_im)
    half_sine = jnp.sin(0.5 * turn_im)
    numer_re = small_expm1(grow_re) * jnp.cos(turn_im) - 2.0 * half_sine * half_sine
    divisor = real_rate * real_rate + imag_rate * imag_rate
    scale_re = (numer_re * real_rate + abar_im * imag_rate) / divisor
    scale_im = (abar_im * real_rate - numer_re * imag_rate) / divisor
    return (abar_re, abar_im, scale_re, scale_im)


def cmul(xr, xi, yr, yi):
    return xr * yr - xi * yi, xr * yi + xi * yr


def power2(xr, xi, times):
    for _ in range(times):
        xr, xi = xr * xr - xi * xi, 2.0 * xr * xi
    return xr, xi


def log2(n):
    return n.bit_length() - 1


def power(xr, xi, n):
    out = None
    while n:
        if n & 1:
            out = (xr, xi) if out is None else cmul(*out, xr, xi)
        n >>= 1
        if n:
            xr, xi = power2(xr, xi, 1)
    return out


def chunk_powers(ar, ai, steps):
    first = lax.broadcasted_iota(jnp.int32, ar.shape, 0) == 0
    sr, si = power(ar, ai, steps - PAD)
    pr, pi = power(ar, ai, steps)
    return jnp.where(first, sr, pr), jnp.where(first, si, pi)


def padded(i, block_len):
    start = i * TILE + PAD * (2 + i * TILE // block_len)
    return slice(start, start + TILE)


def add_to(ref, i, v):
    ref[...] = v if i == 0 else ref[...] + v


def run(count, body, carry, unroll):
    def block(k, c):
        for u in range(unroll):
            c = body(k * unroll + u, c)
        return c

    whole_blocks = count // unroll
    carry = lax.fori_loop(0, whole_blocks, block, carry)
    for i in range(whole_blocks * unroll, count):
        carry = body(i, carry)
    return carry


def wide(v, groups):
    return jnp.concatenate([v] * groups, axis=1)


def fold_rows(v):
    return jnp.sum(v.reshape(-1, 8, v.shape[-1]), axis=0)


def take(ref, at, first, count):
    return jnp.concatenate([ref[first + g, at, :] for g in range(count)], axis=1)


def put(ref, at, first, v):
    for g in range(v.shape[1] // LANES):
        ref[first + g, at, :] = v[:, g * LANES : (g + 1) * LANES]


def clear_pads(ref, seqs, pitch):
    for g in range(ref.shape[0]):
        ref[g, :PAD, :] = jnp.zeros((PAD, LANES), F32)
        for s in range(seqs):
            ref[g, PAD + s * pitch : 2 * PAD + s * pitch, :] = jnp.zeros((PAD, LANES), F32)


def own_w():
    return 2 * lax.axis_index("wy") + lax.axis_index("wc")


def one_row(v):
    return jnp.sum(v, axis=0, keepdims=True)


def nt_dot(a, b):
    return lax.dot_general(a, b, (((1,), (1,)), ((), ())), preferred_element_type=F32)


def tn_dot(a, b):
    return lax.dot_general(a, b, (((0,), (0,)), ((), ())), preferred_element_type=F32)


def chunk_scan(ar, ai, br, bi, reverse):
    rows = lax.broadcasted_iota(jnp.int32, ar.shape, 0)
    d = 1
    while d < CHUNKS:
        shift = (CHUNKS - d) if reverse else d
        keep = (rows < CHUNKS - d) if reverse else (rows >= d)
        pr, pi = pltpu.roll(ar, shift, 0), pltpu.roll(ai, shift, 0)
        qr, qi = pltpu.roll(br, shift, 0), pltpu.roll(bi, shift, 0)
        mr, mi = cmul(ar, ai, qr, qi)
        br, bi = jnp.where(keep, br + mr, br), jnp.where(keep, bi + mi, bi)
        mr, mi = cmul(ar, ai, pr, pi)
        ar, ai = jnp.where(keep, mr, ar), jnp.where(keep, mi, ai)
        d *= 2
    return ar, ai, br, bi


def carry_in(recvs, ids, s, own_row, ar, ai, block_len, conj, blocks):
    states = ar.shape[1]
    pr, pi = power2(ar, -ai if conj else ai, log2(block_len))
    cr = jnp.zeros((1, states), F32)
    ci = jnp.zeros((1, states), F32)
    own = wide(ids[own_row : own_row + 1, :], states // LANES)
    for k in range(len(recvs), 0, -1):
        msg = recvs[k - 1][s : s + 1, :]
        same = (wide(msg[:, 2 * states :], states // LANES) == own) & (blocks >= k)
        cr, ci = cmul(pr, pi, cr, ci)
        cr = cr + jnp.where(same, msg[:, :states], 0.0)
        ci = ci + jnp.where(same, msg[:, states : 2 * states], 0.0)
    return cr, ci


def fetch(pairs, sems):
    copies = [pltpu.make_async_copy(src, dst, sems.at[k]) for k, (src, dst) in enumerate(pairs)]
    for c in copies:
        c.start()
    for c in copies:
        c.wait()


def k0_body(b_ref, g_ref, n_ref, s_ref, q_ref, lr_ref, li_ref, ls_ref, msg_ref, table_ref,
            b_scr, v_scr, l_scr, scr, sems):
    shard, cols = b_scr.shape
    own = lr_ref.shape[1]
    fetch(
        [(b_ref, b_scr)]
        + [(r, v_scr.at[k]) for k, r in enumerate((g_ref, n_ref, s_ref, q_ref))]
        + [(r, l_scr.at[k]) for k, r in enumerate((lr_ref, li_ref, ls_ref))],
        sems,
    )
    msg_ref[:shard, :] = b_scr[...]
    line = jnp.concatenate([v_scr[k] for k in range(4)] + [jnp.zeros((1, cols - 4 * shard), BF16)], axis=1)
    msg_ref[shard:, :] = jnp.broadcast_to(line, (16, cols))
    scr[...] = jnp.zeros_like(scr)
    for k in range(3):
        scr[k : k + 1, :own] = l_scr[k]
    table_ref[...] = pltpu.roll(scr[...], lax.axis_index("seq") * own, 1)


def k0b_body(c_ref, g_ref, msg_ref, c_scr, g_scr, sems):
    c_shard = c_ref.shape[0]
    fetch([(c_ref, c_scr), (g_ref, g_scr)], sems)
    msg_ref[:c_shard, :] = c_scr[...]
    msg_ref[c_shard:, :] = g_scr[...]


def lay_marks(seg_ref, mask_ref, link_ref, valid_ref, ids_ref):
    seqs, block_len = seg_ref.shape
    seg = seg_ref[...].astype(F32)
    link_ref[:PAD, :] = jnp.ones((PAD, LANES), F32)
    lane = lax.broadcasted_iota(jnp.int32, (1, block_len), 1)
    for s in range(seqs):
        row = seg[s : s + 1, :]
        link = jnp.where((row == pltpu.roll(row, 1, 1)) | (lane == 0), 1.0, 0.0)
        mask = mask_ref[s : s + 1, :].astype(F32)
        start = PAD + s * (block_len + PAD)
        link_ref[start : start + PAD, :] = jnp.ones((PAD, LANES), F32)
        for src, dst, start in ((link, link_ref, start + PAD), (mask, valid_ref, s * block_len)):
            for k in range(block_len // LANES):
                piece = jnp.broadcast_to(src[:, k * LANES : (k + 1) * LANES], (LANES, LANES))
                at = start + k * LANES
                dst[at : at + LANES, :] = jnp.transpose(piece)
        ids_ref[s : s + 1, :] = jnp.broadcast_to(row[:, :1], (1, LANES))
        ids_ref[seqs + s : seqs + s + 1, :] = jnp.broadcast_to(row[:, block_len - 1 :], (1, LANES))


def k1_body(x_ref, b0, b1, b2, b3, table_ref, seg_ref, mask_ref,
            low_ref, n_ref, proj_ref, vec_ref, full_ref, s1_ref, msg_ref, rates_ref, link_ref, valid_ref, ids_ref, *, seqs):
    rows, width = x_ref.shape
    shard = b0.shape[0] - 16
    block_len = rows // seqs
    pitch = block_len + PAD
    w = own_w()
    for k, piece in enumerate((b0, b1, b2, b3)):
        at = pl.multiple_of((w ^ k) * shard, shard)
        full_ref[pl.ds(at, shard), :] = piece[:shard, :]
        extra = piece[shard:, :].astype(F32)
        for v in range(4):
            vec_ref[v : v + 1, pl.ds(at, shard)] = extra[0:1, v * shard : (v + 1) * shard]
    vec_ref[4:8, :] = jnp.zeros((4, width), F32)
    gain = vec_ref[0:1, :]
    bias = vec_ref[1:2, :]
    for i in range(rows // TILE):
        at = slice(i * TILE, (i + 1) * TILE)
        n = centre(x_ref[at, :])[0]
        n_ref[at, :] = n.astype(BF16)
        low = (n * gain + bias).astype(BF16)
        low_ref[at, :] = low
        p = jnp.dot(low, full_ref[...], preferred_element_type=F32)
        put(proj_ref, padded(i, block_len), 0, p.astype(BF16).astype(F32))
    clear_pads(proj_ref, seqs, pitch)
    lay_marks(seg_ref, mask_ref, link_ref, valid_ref, ids_ref)
    states = table_ref.shape[1]
    groups = states // LANES
    steps = block_len // CHUNKS + 1
    lam = [table_ref[v : v + 1, :] for v in range(3)]
    parts, back = jax.vjp(rates_map, *lam)
    one, zero = jnp.ones_like(lam[0]), jnp.zeros_like(lam[0])
    for v in range(4):
        rates_ref[v : v + 1, :] = parts[v]
        for k, jac in enumerate(back(tuple(one if i == v else zero for i in range(4)))):
            rates_ref[8 + 3 * v + k : 9 + 3 * v + k, :] = jac
    rates_ref[4:8, :] = jnp.zeros((4, states), F32)
    rates_ref[20:24, :] = jnp.zeros((4, states), F32)
    ar = jnp.broadcast_to(parts[0], (CHUNKS, states))
    ai = jnp.broadcast_to(parts[1], (CHUNKS, states))

    def step(j, carry):
        out = []
        for s in range(seqs):
            ur, ui, q = carry[s]
            at = pl.ds(PAD + s * pitch + j, CHUNKS, stride=steps)
            lk = link_ref[at, :]
            lw = wide(lk, groups)
            nr, ni = cmul(ar, ai, ur, ui)
            out.append((lw * nr + take(proj_ref, at, 0, groups), lw * ni + take(proj_ref, at, groups, groups), q * lk))
        return tuple(out)

    zero = jnp.zeros((CHUNKS, states), F32)
    init = tuple((zero, zero, jnp.ones((CHUNKS, LANES), F32)) for _ in range(seqs))
    ends = run(steps, step, init, 13)
    pr, pi = chunk_powers(ar, ai, steps)
    for s in range(seqs):
        ur, ui, q = ends[s]
        qw = wide(q, groups)
        sc = chunk_scan(pr * qw, pi * qw, ur, ui, False)
        for v in range(4):
            s1_ref[s * CHUNKS : (s + 1) * CHUNKS, v * states : (v + 1) * states] = sc[v]
        msg_ref[s : s + 1, :states] = sc[2][CHUNKS - 1 :, :]
        msg_ref[s : s + 1, states : 2 * states] = sc[3][CHUNKS - 1 :, :]
        msg_ref[s : s + 1, 2 * states :] = ids_ref[seqs + s : seqs + s + 1, :]


def k2_body(*refs, seqs, hops):
    (x_ref, t_ref, link_ref, valid_ref, ids_ref, low_ref, proj_ref, s1_ref, rates_ref, vec_ref,
     c0, c1, c2, c3) = refs[:14]
    recvs = refs[14 : 14 + hops]
    (out_hbm, state_ref, gs_ref, gres_ref, gssm_ref, s2_ref, msg_ref, send_ref, keep_ref, sums_ref,
     wc_scr, wg_scr, gc_scr, gg_scr, out_ref, sems) = refs[14 + hops :]
    rows, width = x_ref.shape
    states = rates_ref.shape[1]
    groups = states // LANES
    block_len = rows // seqs
    steps = block_len // CHUNKS + 1
    pitch = block_len + PAD
    g_shard = width // 4
    c_shard = 2 * states // 4
    w = own_w()
    for k, piece in enumerate((c0, c1, c2, c3)):
        wc_scr[pl.ds(pl.multiple_of((w ^ k) * c_shard, c_shard), c_shard), :] = piece[:c_shard, :]
        wg_scr[pl.ds(pl.multiple_of((w ^ k) * g_shard, g_shard), g_shard), :] = piece[c_shard:, :]
    a1r, a1i = rates_ref[0:1, :], rates_ref[1:2, :]
    ar = jnp.broadcast_to(a1r, (CHUNKS, states))
    ai = jnp.broadcast_to(a1i, (CHUNKS, states))
    zr = jnp.broadcast_to(rates_ref[2:3, :], (CHUNKS, states))
    zi = jnp.broadcast_to(rates_ref[3:4, :], (CHUNKS, states))
    top = lax.broadcasted_iota(jnp.int32, (CHUNKS, states), 0)
    ids = ids_ref[...]
    init, carries = [], []
    for s in range(seqs):
        cr, ci = carry_in(recvs, ids, s, s, a1r, a1i, block_len, False, lax.axis_index("seq"))
        sc = [s1_ref[s * CHUNKS : (s + 1) * CHUNKS, v * states : (v + 1) * states] for v in range(4)]
        mr, mi = cmul(sc[0], sc[1], cr, ci)
        init.append((pltpu.roll(sc[2] + mr, 1, 0), pltpu.roll(sc[3] + mi, 1, 0)))
        carries.append((cr, ci))

    def step(j, carry):
        out = []
        for s in range(seqs):
            ur, ui = carry[s]
            at = pl.ds(PAD + s * pitch + j, CHUNKS, stride=steps)
            lw = wide(link_ref[at, :], groups)
            nr, ni = cmul(ar, ai, ur, ui)
            ur, ui = lw * nr + take(proj_ref, at, 0, groups), lw * ni + take(proj_ref, at, groups, groups)
            sr, si = cmul(zr, zi, ur, ui)
            put(state_ref, at, 0, sr)
            put(state_ref, at, groups, si)
            out.append((ur, ui))
        return tuple(out)

    for g in range(2 * groups):
        state_ref[g, :PAD, :] = jnp.zeros((PAD, LANES), F32)
    entry = list(run(PAD, step, tuple(init), PAD))
    for s in range(seqs):
        ur, ui = (jnp.where(top == 0, c, u) for c, u in zip(carries[s], entry[s]))
        sr, si = cmul(zr, zi, ur, ui)
        at = pl.ds(PAD + s * pitch + PAD - 1, CHUNKS, stride=steps)
        put(state_ref, at, 0, sr)
        put(state_ref, at, groups, si)
        entry[s] = (ur, ui)
    run(steps - PAD, lambda i, c: step(i + PAD, c), tuple(entry), 8)

    skip = vec_ref[2:3, :]
    gbias = 0.5 * vec_ref[3:4, :]
    leaving = []
    loss_acc = jnp.zeros((8, width), F32)
    gbias_acc = jnp.zeros((8, width), F32)
    skip_acc = jnp.zeros((8, width), F32)
    for i in range(rows // TILE):
        at = slice(i * TILE, (i + 1) * TILE)
        pad_at = padded(i, block_len)
        sl = take(state_ref, pad_at, 0, 2 * groups).astype(BF16)
        so = jnp.dot(sl, wc_scr[...], preferred_element_type=F32) + skip * low_ref[at, :].astype(F32)
        e = jnp.exp2(so * so * -0.7213475204444817)
        t = 1.0 / (1.0 + 0.23164189 * jnp.abs(so))
        tail = e * t * (0.127414796 + t * (-0.142248368 + t * (0.7107068705 + t * (-0.7265760135 + t * 0.5307027145))))
        phi = jnp.where(so >= 0.0, 1.0 - tail, tail)
        act = (so * phi).astype(BF16)
        dgelu = phi + so * e * 0.3989422804014327
        g = 0.5 * jnp.tanh(0.5 * jnp.dot(act, wg_scr[...], preferred_element_type=F32) + gbias) + 0.5
        gated = act.astype(F32) * g
        res = x_ref[at, :].astype(F32) + gated
        out_ref[at, :] = res.astype(BF16)
        leaving.append(pltpu.make_async_copy(out_ref.at[at, :], out_hbm.at[at, :], sems.at[i]))
        leaving[-1].start()
        err = res - t_ref[at, :].astype(F32)
        gr = err * wide(valid_ref[at, :], width // LANES)
        loss_acc = loss_acc + fold_rows(gr * err)
        gres_ref[at, :] = gr.astype(BF16)
        gg = gr * gated * (1.0 - g)
        gbias_acc = gbias_acc + fold_rows(gg)
        gl = gg.astype(BF16)
        add_to(gg_scr, i, tn_dot(act, gl))
        gssm = dgelu * (gr * g + nt_dot(gl, wg_scr[...]))
        gssm_ref[at, :] = gssm
        skip_acc = skip_acc + fold_rows(gssm * low_ref[at, :].astype(F32))
        ssl = gssm.astype(BF16)
        put(gs_ref, pad_at, 0, nt_dot(ssl, wc_scr[...]).astype(BF16).astype(F32))
        add_to(gc_scr, i, tn_dot(sl, ssl))
    clear_pads(gs_ref, seqs, pitch)
    sums_ref[0:1, :] = one_row(skip_acc)
    sums_ref[1:2, :] = one_row(gbias_acc)
    sums_ref[2:3, :] = jnp.broadcast_to(jnp.sum(one_row(loss_acc), axis=1, keepdims=True), (1, width))
    sums_ref[3:4, :] = wide(one_row(fold_rows(valid_ref[...])), width // LANES)
    sums_ref[4:8, :] = jnp.zeros((4, width), F32)

    def back(i, carry):
        j = steps - 1 - i
        out = []
        for s in range(seqs):
            yr, yi, q = carry[s]
            at = pl.ds(PAD + s * pitch + j, CHUNKS, stride=steps)
            lk = link_ref[at, :]
            lw = wide(lk, groups)
            nr, ni = cmul(ar, -ai, yr, yi)
            out.append((lw * (nr + take(gs_ref, at, 0, groups)), lw * (ni + take(gs_ref, at, groups, groups)), q * lk))
        return tuple(out)

    zero = jnp.zeros((CHUNKS, states), F32)
    init = tuple((zero, zero, jnp.ones((CHUNKS, LANES), F32)) for _ in range(seqs))
    firsts = run(steps - PAD, back, init, 8)
    ends = run(PAD, lambda i, c: back(i + steps - PAD, c), firsts, PAD)
    pr, pi = chunk_powers(ar, -ai, steps)
    for s in range(seqs):
        yr, yi, q = (jnp.where(top[:, : v.shape[1]] == 0, u, v) for u, v in zip(firsts[s], ends[s]))
        qw = wide(q, groups)
        sc = chunk_scan(pr * qw, pi * qw, yr, yi, True)
        for v in range(4):
            s2_ref[s * CHUNKS : (s + 1) * CHUNKS, v * states : (v + 1) * states] = sc[v]
        msg_ref[s : s + 1, :states] = sc[2][:1, :]
        msg_ref[s : s + 1, states : 2 * states] = sc[3][:1, :]
        msg_ref[s : s + 1, 2 * states :] = ids_ref[s : s + 1, :]

    for k, dst in enumerate((keep_ref, send_ref, keep_ref, send_ref)):
        q = w ^ k
        slot = q // 2
        dst[slot, :c_shard, :] = gc_scr[pl.ds(pl.multiple_of(q * c_shard, c_shard), c_shard), :].astype(BF16)
        lanes = pl.multiple_of(q * g_shard, g_shard)
        dst[slot, c_shard : c_shard + g_shard, :] = gg_scr[pl.ds(lanes, g_shard), :].astype(BF16)
    for copy in leaving:
        copy.wait()


def split16(v):
    high = v.astype(BF16)
    return high, (v - high.astype(F32)).astype(BF16)


def split_rows(lines):
    width = lines[0].shape[1]
    rows = sum(v.shape[0] for v in lines)
    v = jnp.concatenate(lines + [jnp.zeros((8 - rows, width), F32)] * (rows < 8), axis=0)
    high, rest = split16(v)
    return jnp.concatenate([high.astype(F32), rest.astype(F32)], axis=0).astype(BF16)


def k3_body(*refs, seqs, hops, blocks):
    (n_ref, sums_ref, link_ref, ids_ref, low_ref, proj_ref, state_ref, gs_ref, gssm_ref,
     s2_ref, rates_ref, vec_ref, w_full) = refs[:13]
    recvs = refs[13 : 13 + hops]
    (gn_ref, send_ref, keep_ref, gp_scr, gb_scr, vec_scr) = refs[13 + hops :]
    rows, width = n_ref.shape
    states = rates_ref.shape[1]
    groups = states // LANES
    block_len = rows // seqs
    steps = block_len // CHUNKS + 1
    pitch = block_len + PAD
    shard = width // 4
    w = own_w()
    a1r, a1i = rates_ref[0:1, :], rates_ref[1:2, :]
    ar = jnp.broadcast_to(a1r, (CHUNKS, states))
    ai = jnp.broadcast_to(a1i, (CHUNKS, states))
    zr = jnp.broadcast_to(rates_ref[2:3, :], (CHUNKS, states))
    zi = jnp.broadcast_to(rates_ref[3:4, :], (CHUNKS, states))
    rowid = lax.broadcasted_iota(jnp.int32, (CHUNKS, states), 0)
    ids = ids_ref[...]
    rate_sums = [jnp.zeros((CHUNKS, states), F32) for _ in range(4)]
    for s in range(seqs):
        cr, ci = carry_in(recvs, ids, s, seqs + s, a1r, a1i, block_len, True, blocks - 1 - lax.axis_index("seq"))
        sc = [s2_ref[s * CHUNKS : (s + 1) * CHUNKS, v * states : (v + 1) * states] for v in range(4)]
        mr, mi = cmul(sc[0], sc[1], cr, ci)
        yr = jnp.where(rowid == CHUNKS - 1, cr, pltpu.roll(sc[2] + mr, CHUNKS - 1, 0))
        yi = jnp.where(rowid == CHUNKS - 1, ci, pltpu.roll(sc[3] + mi, CHUNKS - 1, 0))

        def step(i, carry):
            yr, yi, gar, gai, gsr, gsi = carry
            j = steps - 1 - i
            at = pl.ds(PAD + s * pitch + j, CHUNKS, stride=steps)
            before = pl.ds(PAD + s * pitch + j - 1, CHUNKS, stride=steps)
            lw = wide(link_ref[at, :], groups)
            nr, ni = cmul(ar, -ai, yr, yi)
            dr, di = nr + take(gs_ref, at, 0, groups), ni + take(gs_ref, at, groups, groups)
            yr, yi = lw * dr, lw * di
            pr, pi = take(proj_ref, at, 0, groups), take(proj_ref, at, groups, groups)
            ur, ui = take(state_ref, before, 0, groups), take(state_ref, before, groups, groups)
            put(gp_scr, at, 0, zr * dr + zi * di)
            put(gp_scr, at, groups, zr * di - zi * dr)
            return (
                yr, yi,
                gar + (ur * yr + ui * yi), gai + (ur * yi - ui * yr),
                gsr + (pr * dr + pi * di), gsi + (pr * di - pi * dr),
            )

        carry = run(steps - PAD, step, (yr, yi, *rate_sums), 8)
        yr, yi = (jnp.where(rowid == 0, 0.0, v) for v in carry[:2])
        carry = run(PAD, lambda i, c: step(i + steps - PAD, c), (yr, yi, *carry[2:]), PAD)
        rate_sums = list(carry[2:])

    skip = vec_ref[2:3, :]
    gain_acc = jnp.zeros((8, width), F32)
    bias_acc = jnp.zeros((8, width), F32)
    for i in range(rows // TILE):
        at = slice(i * TILE, (i + 1) * TILE)
        gpl = take(gp_scr, padded(i, block_len), 0, 2 * groups).astype(BF16)
        add_to(gb_scr, i, tn_dot(low_ref[at, :], gpl))
        gn = nt_dot(gpl, w_full[...]) + skip * gssm_ref[at, :]
        gn_ref[at, :] = gn.astype(BF16)
        gain_acc = gain_acc + fold_rows(gn * n_ref[at, :].astype(F32))
        bias_acc = bias_acc + fold_rows(gn)
    sums4 = [one_row(v) for v in rate_sums]
    rate_grads = []
    for k in range(3):
        rate_grads.append(sum(rates_ref[8 + 3 * c + k : 9 + 3 * c + k, :] * sums4[c] for c in range(4)))
    vec_scr[0:1, :] = one_row(gain_acc)
    vec_scr[1:2, :] = one_row(bias_acc)
    extra = 3 * shard // 2
    half = shard // 2
    for k, dst in enumerate((keep_ref, send_ref, keep_ref, send_ref)):
        slot = (w ^ k) // 2
        q = pl.multiple_of((w ^ k) * shard, shard)
        dst[slot, :shard, :] = gb_scr[pl.ds(q, shard), :width].astype(BF16)
        dst[slot, shard:extra, : width // 2] = gb_scr[pl.ds(q, half), width:].astype(BF16)
        dst[slot, shard:extra, width // 2 :] = gb_scr[pl.ds(q + half, half), width:].astype(BF16)
        mine = [vec_scr[v : v + 1, pl.ds(q, shard)] for v in range(2)] + [jnp.zeros((1, shard), F32)]
        others = [sums_ref[v : v + 1, pl.ds(q, shard)] for v in range(2)] + [sums_ref[v : v + 1, :shard] for v in (2, 3)]
        lines = [jnp.concatenate(p, axis=1) for p in [*zip(rate_grads, mine), others]]
        dst[slot, extra:, :] = split_rows(lines)


def centre(values):
    x = values.astype(F32)
    c = x - jnp.mean(x, -1, keepdims=True)
    r = lax.rsqrt(jnp.mean(c * c, -1, keepdims=True) + 1e-05)
    return c * r, r


def sum_body(c0, c1, c2, c3, sum_ref):
    sum_ref[...] = total((c0, c1, c2, c3), slice(0, sum_ref.shape[0]))


def quarter_body(keep_ref, got_ref, *outs, extra):
    half = outs[0].shape[0] - extra
    x, y = lax.axis_index("seq") % 2, lax.axis_index("wy")
    for out, slot, side in zip(outs, (y, 1 - y, y, 1 - y), (x, x, 1 - x, 1 - x)):
        def both(rows):
            return keep_ref[slot, rows, :].astype(F32) + got_ref[slot, rows, :].astype(F32)

        out[:half, :] = both(pl.ds(pl.multiple_of(side * half, half), half)).astype(BF16)
        if extra:
            v = both(slice(2 * half, 2 * half + 16))
            out[half:, :] = split_rows([v[:8] + v[8:]])


def total(refs, rows):
    return sum([r[rows, :].astype(F32) for r in refs[1:]], refs[0][rows, :].astype(F32))


def deal_body(*refs):
    n = len(refs) - 6
    bs, c_sum, outs, b_scr = refs[:4], refs[4], refs[5 : 5 + n], refs[5 + n]
    b_half, c_half = b_scr.shape[0], c_sum.shape[0]
    b_part, c_part = b_half // n, c_half // n
    b_scr[...] = total(bs, slice(0, b_half))
    tail = total(bs, slice(b_half, b_half + 16))
    ends = split_rows([tail[:8] + tail[8:]]).astype(F32)
    for k, out in enumerate(outs):
        at = (lax.axis_index("seq") // 2) ^ k
        rows = [
            b_scr[pl.ds(pl.multiple_of(at * b_part, 8), b_part), :],
            c_sum[pl.ds(pl.multiple_of(at * c_part, 8), c_part), :],
            ends[:4], ends[8:12],
        ]
        out[...] = jnp.concatenate(rows, axis=0).astype(BF16)


def close_body(*refs):
    parts, (piece_ref, tail_ref) = refs[:-2], refs[-2:]
    bulk = piece_ref.shape[0]
    v = total(parts, slice(0, bulk + 8))
    piece_ref[...] = v[:bulk].astype(BF16)
    tail_ref[...] = jnp.concatenate([v[bulk : bulk + 4] + v[bulk + 4 :], jnp.zeros((4, v.shape[1]), F32)], axis=0)


def scale_of(tail, tokens):
    return tokens / tail[3:4, 3 * LANES : 3 * LANES + 1]


def norm_body(x_ref, gn_ref, gres_ref, vec_ref, ig_ref):
    gain = vec_ref[0:1, :]
    for i in range(x_ref.shape[0] // TILE):
        at = slice(i * TILE, (i + 1) * TILE)
        n, r = centre(x_ref[at, :])
        q = gn_ref[at, :].astype(F32) * gain
        back = (q - jnp.mean(q, -1, keepdims=True) - n * jnp.mean(q * n, -1, keepdims=True)) * r
        ig_ref[at, :] = (gres_ref[at, :].astype(F32) + back).astype(BF16)


def finish_body(tail_ref, ig_ref,
                out_ref, loss_ref, gain_ref, bias_ref, skip_ref, gate_ref, real_ref, imag_ref, step_ref, *, tokens):
    width = ig_ref.shape[1]
    states = width - gain_ref.shape[1]
    own = real_ref.shape[1]
    tail = tail_ref[...]
    scale = scale_of(tail, tokens)
    out_ref[...] = scale * ig_ref[...].astype(F32)
    scaled = tail * scale
    gain_ref[...] = scaled[0:1, states:]
    bias_ref[...] = scaled[1:2, states:]
    skip_ref[...] = scaled[3:4, :LANES]
    gate_ref[...] = scaled[3:4, LANES : 2 * LANES]
    loss_ref[...] = tail[3:4, 2 * LANES : 2 * LANES + 1] * scale * (1.0 / (tokens * width))
    rates = pltpu.roll(scaled[:, :states], states - lax.axis_index("seq") * own, 1)
    for k, ref in enumerate((real_ref, imag_ref, step_ref)):
        ref[...] = rates[k : k + 1, :own]


def unpack_body(tail_ref, *refs, tokens):
    pieces, (gb_hbm, gc_hbm, gg_hbm, b_scr, c_scr, sems) = refs[:-6], refs[-6:]
    scale = scale_of(tail_ref[...], tokens)
    S = len(pieces)
    b_rows, c_rows = b_scr.shape[0] // S, c_scr.shape[0] // S
    for k, piece in enumerate(pieces):
        s = lax.axis_index("seq") ^ k
        v = piece[...].astype(F32) * scale
        b_at = s % 2 * (b_scr.shape[0] // 2) + s // 2 * b_rows
        c_at = s % 2 * (c_scr.shape[0] // 2) + s // 2 * c_rows
        b_scr[pl.ds(pl.multiple_of(b_at, 8), b_rows), :] = v[:b_rows, :]
        c_scr[pl.ds(pl.multiple_of(c_at, 8), c_rows), :] = v[b_rows:, :]
    shard, cols = gb_hbm.shape
    width = b_scr.shape[1]
    half, c_shard = shard // 2, gc_hbm.shape[0]
    fetch([
        (c_scr.at[:c_shard, :], gc_hbm),
        (c_scr.at[c_shard:, :], gg_hbm),
        (b_scr.at[:shard, :], gb_hbm.at[:, :width]),
        (b_scr.at[shard:, : cols - width], gb_hbm.at[:half, width:]),
        (b_scr.at[shard:, cols - width :], gb_hbm.at[half:, width:]),
    ], sems)


def whole(n, far=()):
    return [pl.BlockSpec(memory_space=pltpu.HBM if i in far else pltpu.VMEM) for i in range(n)]


def call(body, outs, scratch, *args, us=1, limit=30, far=(), far_outs=(), copies=0):
    return pl.pallas_call(
        body,
        out_shape=[jax.ShapeDtypeStruct(*o) for o in outs],
        in_specs=whole(len(args), far),
        out_specs=whole(len(outs), far_outs),
        scratch_shapes=[pltpu.VMEM(*s) for s in scratch] + [pltpu.SemaphoreType.DMA((copies,))] * (copies > 0),
        compiler_params=pltpu.CompilerParams(vmem_limit_bytes=limit * MIB),
        cost_estimate=pl.CostEstimate(flops=us * 1_000_000_000, bytes_accessed=MIB, transcendentals=0),
    )(*args)


def per_device(inputs, teacher, segment_ids, valid_mask, ln_gain, ln_bias, b_weight, c_weight, skip_weight,
               glu_weight, glu_bias, lambda_real, lambda_imag, log_step):
    S = lax.axis_size("seq")
    s_at = lax.axis_index("seq")
    seqs, block_len, width = inputs.shape
    rows = seqs * block_len
    padded_rows = PAD + seqs * (block_len + PAD)
    length = S * block_len
    own = lambda_real.shape[0]
    states = own * S
    doc_most = {4096: 1024, 32768: 8192}.get(length, length)
    hops = min((doc_most - 2) // block_len + 1, S - 1)
    shard, c_shard, g_shard = b_weight.shape[0], c_weight.shape[0], glu_weight.shape[0]

    def swap(v, axis, bit=1, n=2):
        return lax.ppermute(v, axis, [(i, i ^ bit) for i in range(n)])

    def after(v, *others):
        return lax.optimization_barrier((v, *others))[0]

    b_msg, table = call(
        k0_body,
        [((shard + 16, b_weight.shape[1]), BF16), ((8, states), F32)],
        [(b_weight.shape, BF16), ((4, 1, shard), BF16), ((3, 1, own), F32), ((8, states), F32)],
        b_weight, *(v[None] for v in (ln_gain, ln_bias, skip_weight, glu_bias, lambda_real, lambda_imag, log_step)),
        far=range(8), copies=8, limit=60,
    )
    b_far = swap(b_msg, "wy")
    b_near = swap(b_msg, "wc")
    (c_msg,) = call(
        k0b_body,
        [((c_shard + g_shard, width), BF16)],
        [(c_weight.shape, BF16), (glu_weight.shape, BF16)],
        c_weight, glu_weight, far=range(2), copies=2, limit=4,
    )
    c_far = swap(after(c_msg, b_far), "wy")
    bit = 1
    while bit < S:
        radix = 4 if 4 * bit <= S else 2
        table = sum([swap(table, "seq", k * bit, S) for k in range(1, radix)], table)
        bit *= radix
    bs = (b_msg, b_near, b_far, swap(b_far, "wc"))

    x = inputs.reshape(rows, width)
    teach = teacher.reshape(rows, width)
    R = seqs * CHUNKS
    slab = (2 * states // LANES, padded_rows, LANES)
    msg_shape = ((seqs, 2 * states + LANES), F32)
    low, norm, proj, vec, w_full, s1, fwd, rates, link, valid, ids = call(
        functools.partial(k1_body, seqs=seqs),
        [((rows, width), BF16), ((rows, width), BF16), (slab, F32), ((8, width), F32), ((width, 2 * states), BF16),
         ((R, 4 * states), F32), msg_shape, ((24, states), F32),
         ((padded_rows, LANES), F32), ((rows, LANES), F32), ((2 * seqs, LANES), F32)],
        [],
        x, *bs, table, segment_ids, valid_mask, us=2, limit=8,
    )
    cs = (c_msg, swap(c_msg, "wc"), c_far, swap(after(c_far, fwd), "wc"))
    fwds = [lax.ppermute(fwd, "seq", [(i, (i + k) % S) for i in range(S)]) for k in range(1, hops + 1)]
    c_bulk = c_shard + g_shard
    out, state, gs, gres, gssm, s2, bwd, send_c, keep_c, sums = call(
        functools.partial(k2_body, seqs=seqs, hops=hops),
        [((rows, width), BF16), (slab, F32), (slab, F32),
         ((rows, width), BF16), ((rows, width), F32), ((R, 4 * states), F32), msg_shape,
         ((2, c_bulk, width), BF16), ((2, c_bulk, width), BF16), ((8, width), F32)],
        [((2 * states, width), BF16), ((width, width), BF16), ((2 * states, width), F32), ((width, width), F32),
         ((rows, width), BF16)],
        x, teach, link, valid, ids, low, proj, s1, rates, vec, *cs, *fwds, us=10, limit=20, far_outs=(0,), copies=rows // TILE,
    )
    bwds = [lax.ppermute(bwd, "seq", [((i + k) % S, i) for i in range(S)]) for k in range(1, hops + 1)]
    def cross(v, flip_x, flip_y):
        return lax.ppermute(
            v, ("seq", "wy"), [(2 * a + b, 2 * (a ^ flip_x) + (b ^ flip_y)) for a in range(S) for b in range(2)])

    def quarters(keep, got, extra):
        shape = ((keep.shape[1] - extra) // 2 + extra, width)
        return call(functools.partial(quarter_body, extra=extra), [(shape, BF16)] * 4, [], keep, got, limit=4)

    def exchange(q):
        return (q[0], cross(q[1], 0, 1), cross(q[2], 1, 0), cross(q[3], 1, 1))

    q_c = quarters(keep_c, swap(send_c, "wc"), 0)
    bwds = lax.optimization_barrier((bwds, q_c))[0]
    part_c = exchange(q_c)
    b_bulk = 3 * shard // 2
    b_part, c_part = b_bulk // S, c_bulk // S
    gn, send_b, keep_b = call(
        functools.partial(k3_body, seqs=seqs, hops=hops, blocks=S),
        [((rows, width), BF16), ((2, b_bulk + 16, width), BF16), ((2, b_bulk + 16, width), BF16)],
        [(slab, F32), ((width, 2 * states), F32), ((8, width), F32)],
        norm, sums, link, ids, low, proj, state, gs, gssm, s2, rates, vec, w_full, *bwds, us=8, limit=14,
    )
    (c_sum,) = call(sum_body, [((c_bulk // 2, width), F32)], [], *part_c, limit=4)
    got_b = swap(after(send_b, part_c[3]), "wc")
    part_b = exchange(quarters(keep_b, got_b, 16))
    (ig,) = call(norm_body, [((rows, width), BF16)], [], x, gn, gres, vec, us=3, limit=8)
    part_b, ig = lax.optimization_barrier((part_b, ig))
    tokens = float(length * seqs * lax.axis_size(("wy", "wc")))
    deal = S // 2
    if b_part % 8 == 0 and c_part % 8 == 0:
        dealt = call(
            deal_body, [((b_part + c_part + 8, width), BF16)] * deal,
            [((b_bulk // 2, width), F32)], *part_b, c_sum, limit=4,
        )
        parts = [dealt[0]] + [swap(dealt[k], "seq", 2 * k, S) for k in range(1, deal)]
        piece, tail = call(
            close_body, [((b_part + c_part, width), BF16), ((8, width), F32)], [], *parts, limit=4,
        )
        pieces = {0: piece}
        for k in range(1, deal):
            pieces[2 * k] = swap(piece, "seq", 2 * k, S)
        for k in range(deal):
            pieces[2 * k + 1] = swap(pieces[2 * k] if k else after(piece, pieces[2]), "seq", 1, S)
        pieces = [pieces[k] for k in range(S)]
    else:
        piece, tail, pieces = sum_by_all_to_all(part_b, c_sum, S, s_at)
    ingrad, loss, *lines = call(
        functools.partial(finish_body, tokens=tokens),
        [((rows, width), F32), ((1, 1), F32)] + [((1, shard), F32)] * 4 + [((1, own), F32)] * 3,
        [], tail, ig, limit=8,
    )
    gb, gc, gg = call(
        functools.partial(unpack_body, tokens=tokens),
        [((shard, 2 * states), F32), ((c_shard, width), F32), ((g_shard, width), F32)],
        [((b_bulk, width), F32), ((c_bulk, width), F32)],
        tail, *pieces, limit=8, far_outs=range(3), copies=5,
    )
    gain, bias, skip, gate, real, imag, step = (v[0] for v in lines)
    return (
        out.reshape(inputs.shape), loss[0, 0], ingrad.reshape(inputs.shape), gain, bias, gb, gc, skip, gg, gate,
        real, imag, step,
    )


def sum_by_all_to_all(part_b, v_c, S, s_at):
    v_b = sum([p.astype(F32) for p in part_b[1:]], part_b[0].astype(F32))
    width = v_b.shape[1]
    tail = v_b[-16:-8] + v_b[-8:]
    high = lax.reduce_precision(tail, 8, 7)
    ends = jnp.concatenate([high, tail - high], 0).astype(BF16)
    both = jnp.concatenate([v.astype(BF16).reshape(S // 2, -1, width) for v in (v_b[:-16], v_c)], 1)
    bulk = both.shape[1]
    both = jnp.concatenate([both, jnp.broadcast_to(ends[None], (S // 2, 16, width))], 1)
    empty = jnp.zeros_like(both)
    mine = (lax.iota(jnp.int32, S) % 2 == s_at % 2)[:, None, None]
    sent = jnp.where(mine, jnp.stack([both, both], 1).reshape(S, bulk + 16, width), jnp.stack([empty, empty], 1).reshape(S, bulk + 16, width))
    v = jnp.sum(lax.all_to_all(sent, "seq", 0, 0, tiled=True).astype(F32), 0)
    piece, tail = v[:bulk].astype(BF16), v[bulk : bulk + 8] + v[bulk + 8 :]
    back = lax.all_to_all(jnp.broadcast_to(piece[None], (S, bulk, width)), "seq", 0, 0, tiled=True)
    order = lax.iota(jnp.int32, S) ^ s_at
    return piece, tail, [lax.dynamic_index_in_dim(back, order[k], 0, keepdims=False) for k in range(S)]


def solution(mesh):
    sizes = mesh.devices.shape
    fine = Mesh(mesh.devices.reshape(sizes[0], 2, sizes[1] // 2), ("seq", "wy", "wc"))
    w = ("wy", "wc")
    tokens = P(w, "seq", None)
    return jax.shard_map(
        per_device,
        mesh=fine,
        in_specs=(
            tokens, tokens, P(w, "seq"), P(w, "seq"), P(w), P(w), P(w, None), P(w, None), P(w), P(w, None), P(w),
            P("seq"), P("seq"), P("seq"),
        ),
        out_specs=(
            tokens, P(), tokens, P(w), P(w), P(w, None), P(w, None), P(w), P(w, None), P(w),
            P("seq"), P("seq"), P("seq"),
        ),
        check_vma=False,
    )
```
